256 devices in a mesh: real: 4 (over z_lo), sx: 8 (over x, z_hi), sy: 8 (over y, core).
Axes of the slice: x: 4, y: 4, z: 8 (z_hi: 2, z_lo: 4; z = z_hi * 4 + z_lo), core: 2. Of those that a mesh axis runs over, the one named last changes fastest.
Arguments:
- noise: float32 [64, 256, 512], P('sx', 'sy', 'real'), parts along dimension 2, may hold values from -6 to 6
- classes: int32 [64, 256, 64], P('sx', 'sy'), may hold values from 0 to 7
- table: float32 [8, 27], replicated, may hold values from 0 to 0.07
- obs_matrix: bfloat16 [512, 256, 512], P(('sx', 'sy')), may hold values from -0.25 to 0.25
- node_block: int32 [512], P(('sx', 'sy')), may hold values from 0 to 31
- sample_block: int32 [512], P(('sx', 'sy')), may hold values from 0 to 127
- sample_count: int32 [512], P(('sx', 'sy')), may hold values from 1 to 256, as said below
- drill_data: float32 [128, 256], P(('sx', 'sy')), may hold values from -6 to 6
- obs_gain: float32 [128, 256], P(('sx', 'sy')), may hold values from 0.1 to 1
Outputs:
- conditioned: float32 [64, 256, 512], P('sx', 'sy', 'real'), parts along dimension 2
- misfit: float32 [128, 8, 256], P(('sx', 'sy'), 'real'), parts along dimension 1
The draws below stay inside these ranges and needn't reach their ends.
There are 4 independent parts, one for each index of `real`. The reference program is written for one: setup_inputs(seed, part) draws one part's arguments, and reference() takes and returns one part's arrays. A program takes and returns all parts, laid end to end along the dimension named above; an argument that names none is the same for every part. Nothing has to cross between parts.
Inputs may be any that keep to these rules, and one draw needn't show every extreme that they name: `sample_count`: the largest value is reached in every draw. `sample_block`: sample block k is held by tile k // 2.
All inputs are finite; a program needn't handle non-finite values.
Results may differ from the reference program's by a relative error of at most 0.0003.
Values sent between devices are 32-bit elements; how exact they have to be, the bound alone decides.
No kernel may reach another device: no remote copies, remote signals or barrier semaphores. Data moves between devices by JAX's collectives and lax.ppermute only.
A program may use at most 128 MiB of HBM per device.

```python
import math
import jax
import jax.numpy as jnp
from jax import lax

CX = 8
CY = 32
NZ = 64
R = 2
NCLS = 8
SB = 256
OBS_TILE = 8
NX = 64
NY = 256
TILE_BLOCKS = 32
OBS_BLOCKS = 512
SAMPLE_BLOCKS = 128
N_SX = 8
N_SY = 8


def draw_sample_count(key, part):
    key = jax.random.fold_in(key, 7)
    first_key, second_key = jax.random.split(key)
    counts = jax.random.randint(first_key, (OBS_BLOCKS,), 1, SB + 1, dtype=jnp.int32)
    target = jax.random.randint(second_key, (), 0, OBS_BLOCKS, dtype=jnp.int32)
    return jnp.where(jnp.arange(OBS_BLOCKS, dtype=jnp.int32) == target, SB, counts).astype(jnp.int32)


def touch_ends(entries, key, smallest, high):
    index_at = [jax.random.randint(jax.random.fold_in(key, axis), (), 0, length) for axis, length in enumerate(entries.shape)]
    main_axis = entries.shape.index(max(entries.shape))
    next_to = index_at[:main_axis] + [(index_at[main_axis] + 1) % entries.shape[main_axis]] + index_at[main_axis + 1:]
    return entries.at[tuple(index_at)].set(smallest).at[tuple(next_to)].set(high)


def block_levels(key, dims, shards, least, high):
    level, own = 1.0, jax.random.fold_in(key, 6)
    for dim, blocks in shards:
        heights = jnp.exp(jax.random.uniform(jax.random.fold_in(own, dim), (blocks,), jnp.float32, least / len(shards), high / len(shards)))
        level = level * jnp.repeat(heights, dims[dim] // blocks).reshape([-1 if axis == dim else 1 for axis in range(len(dims))])
    return level


def gaussian(key, shape, deviation, reach, shards=(), kind=jnp.bfloat16):
    values = jax.random.normal(key, shape, jnp.float32) * deviation
    if len(shards) > 0:
        values = block_levels(key, shape, shards, -0.22, 0.18) * values
    return jnp.clip(values, min=-reach, max=reach).astype(kind)


def setup_inputs(seed: int = 0, part: int = 0) -> dict:
    key_list = jax.random.split(jax.random.key(seed), 10)
    own_keys = jax.random.split(jax.random.fold_in(key_list[9], part), 10)
    noise = gaussian(own_keys[0], (NX, NY, R * NZ), 1.0, 6.0, ((0, 8), (1, 8)), jnp.float32)
    classes = touch_ends(jax.random.randint(key_list[1], (NX, NY, NZ), 0, NCLS), jax.random.fold_in(key_list[1], 1), 0, NCLS - 1).astype(jnp.int32)
    table = jnp.clip(jax.random.uniform(key_list[2], (NCLS, 27), jnp.float32, 0.0, 0.07), 0.0, 0.07)
    obs_matrix = gaussian(key_list[3], (OBS_BLOCKS, SB, 8 * NZ), (8 * NZ) ** -0.5, 0.25, ((0, 64),))
    node_block = touch_ends(jax.random.randint(key_list[4], (OBS_BLOCKS,), 0, TILE_BLOCKS), jax.random.fold_in(key_list[4], 1), 0, TILE_BLOCKS - 1).astype(jnp.int32)
    sample_block = touch_ends(jax.random.randint(key_list[5], (OBS_BLOCKS,), 0, SAMPLE_BLOCKS), jax.random.fold_in(key_list[5], 1), 0, SAMPLE_BLOCKS - 1).astype(jnp.int32)
    sample_count = draw_sample_count(jax.random.fold_in(key_list[9], 71), part)
    drill_data = gaussian(key_list[7], (SAMPLE_BLOCKS, SB), 1.0, 6.0, ((0, 64),), jnp.float32)
    obs_gain = jnp.clip(jnp.exp(math.log(1.0) - 2.3025851 * jax.random.uniform(key_list[8], (SAMPLE_BLOCKS, SB), jnp.float32) ** block_levels(key_list[8], (SAMPLE_BLOCKS, SB), ((0, 64),), -0.2, 0.2)), 0.1, 1.0)
    return dict(noise=noise, classes=classes, table=table, obs_matrix=obs_matrix, node_block=node_block, sample_block=sample_block, sample_count=sample_count, drill_data=drill_data, obs_gain=obs_gain)


CHEB = (0.6, 0.5, 0.3, 0.2)


def stencil(padded, classes, table):
    size_x = padded.shape[0] - 2
    size_y = padded.shape[1] - 2
    layers = classes.shape[2]
    copies = padded.shape[2] // layers
    grid_cells = padded.reshape(size_x + 2, size_y + 2, copies, layers)
    grid_cells = jnp.pad(grid_cells, ((0, 0), (0, 0), (0, 0), (1, 1)))
    onehot = (classes[..., None] == jnp.arange(table.shape[0], dtype=jnp.int32)).astype(jnp.float32)
    coeffs = jnp.einsum('xyzc,co->oxyz', onehot, table, precision=lax.Precision.HIGHEST)
    summed = jnp.zeros((size_x, size_y, copies, layers), jnp.float32)
    offset = 0
    for shift_x in range(3):
        for shift_y in range(3):
            for shift_z in range(3):
                summed = summed + coeffs[offset][:, :, None, :] * grid_cells[shift_x:shift_x + size_x, shift_y:shift_y + size_y, :, shift_z:shift_z + layers]
                offset += 1
    return summed.reshape(size_x, size_y, copies * layers)


def reference(noise, classes, table, obs_matrix, node_block, sample_block, sample_count, drill_data, obs_gain):
    def operate(field):
        return stencil(jnp.pad(field, ((1, 1), (1, 1), (0, 0))), classes, table)

    first = noise
    second = operate(first)
    third = 2.0 * operate(second) - first
    fourth = 2.0 * operate(third) - second
    smooth = CHEB[0] * first + CHEB[1] * second + CHEB[2] * third + CHEB[3] * fourth
    tiles = N_SX * N_SY
    grid = smooth.reshape(N_SX, CX, N_SY, CY, R, NZ).transpose(0, 2, 1, 3, 4, 5).reshape(tiles * TILE_BLOCKS, 8, R, NZ)
    holder = jnp.arange(OBS_BLOCKS, dtype=jnp.int32) // OBS_TILE
    flat_id = (holder * TILE_BLOCKS + node_block).astype(jnp.int32)
    chosen = grid[flat_id]
    matrix = obs_matrix.astype(jnp.float32).reshape(OBS_BLOCKS, SB, 8, NZ)
    live = (jnp.arange(SB, dtype=jnp.int32)[None, :] < sample_count[:, None]).astype(jnp.float32)
    partial_value = jnp.einsum('bsak,bark->brs', matrix, chosen, precision=lax.Precision.HIGHEST) * live[:, None, :]
    totals = jax.ops.segment_sum(partial_value, sample_block, num_segments=SAMPLE_BLOCKS)
    misfit = drill_data[:, None, :] - totals
    scaled = obs_gain[:, None, :] * misfit
    picked = scaled[sample_block] * live[:, None, :]
    update = jnp.einsum('bsak,brs->bark', matrix, picked, precision=lax.Precision.HIGHEST)
    added = jax.ops.segment_sum(update, flat_id, num_segments=tiles * TILE_BLOCKS)
    merged = grid + added
    conditioned = merged.reshape(N_SX, N_SY, CX, CY, R, NZ).transpose(0, 2, 1, 3, 4, 5).reshape(NX, NY, R * NZ)
    return conditioned, misfit
```

```python
import itertools

import jax
import jax.numpy as jnp
from jax import lax
from jax.experimental import pallas as pl
from jax.experimental.pallas import tpu as pltpu
from jax.sharding import Mesh, PartitionSpec as P

CHEB = (0.6, 0.5, 0.3, 0.2)
X, Y, Z = 8, 32, 64
W = 2 * Z
YP = 40
OFF = 4
BLOCKS = 8
SAMPLES = 256
NODES = 512
ROWS = 24
F32 = jnp.float32
VMEM = pl.BlockSpec(memory_space=pltpu.VMEM)
SMEM = pl.BlockSpec(memory_space=pltpu.SMEM)
ANY = pl.BlockSpec(memory_space=pl.ANY)
SIZES = {"x": 4, "zh": 2, "y": 4, "core": 2}


def permute(value, axes, target):
    dims = [SIZES[a] for a in axes]

    def flat(place):
        number = 0
        for coordinate, size in zip(place, dims):
            number = number * size + coordinate
        return number

    pairs = []
    for place in itertools.product(*[range(d) for d in dims]):
        other = target(*place)
        if other is not None:
            pairs.append((flat(place), flat(other)))
    return lax.ppermute(value, axes if len(axes) > 1 else axes[0], pairs)


def even_pair(a, b):
    return (a, b ^ 1)


def odd_pair(a, b):
    if b == 1:
        return (a + 1, 0) if a < 3 else None
    return (a - 1, 1) if a > 0 else None


def half_lanes(shape):
    return lax.broadcasted_iota(jnp.int32, shape, len(shape) - 1) < Z


def swap_halves(value):
    return pltpu.roll(value, Z, axis=value.ndim - 1)


def pack(first, second):
    return jnp.where(half_lanes(first.shape), first, second)


def unpack(row):
    low = half_lanes(row.shape)
    other = swap_halves(row)
    return jnp.where(low, row, other), jnp.where(low, other, row)


def edge_y_kernel(place, noise, classes, even, odd, doubled):
    kinds = (classes[...] + 1).astype(F32)
    doubled[...] = jnp.concatenate([kinds, kinds], axis=-1)
    core = place[1]

    def low(out):
        out[:, 0:3, :] = noise[:, 0:3, :]
        out[:, 3:4, :] = pack(doubled[:, 0:1, :], doubled[:, 1:2, :])

    def high(out):
        out[:, 0:3, :] = noise[:, Y - 3 : Y, :]
        out[:, 3:4, :] = pack(doubled[:, Y - 2 : Y - 1, :], doubled[:, Y - 1 : Y, :])

    @pl.when(core == 0)
    def _():
        high(even)
        low(odd)

    @pl.when(core == 1)
    def _():
        low(even)
        high(odd)


def edge_x_kernel(place, noise, doubled, even_in, odd_in, field, kinds, even, odd):
    core, half = place[1], place[0]
    field[:, 0:8, :] = jnp.zeros((X, 8, W), F32)
    field[:, 32:40, :] = jnp.zeros((X, 8, W), F32)
    kinds[:, 0:8, :] = jnp.zeros((X, 8, W), F32)
    kinds[:, 32:40, :] = jnp.zeros((X, 8, W), F32)
    field[:, OFF : OFF + Y, :] = noise[...]
    kinds[:, OFF : OFF + Y, :] = doubled[...]

    def sides(low, high):
        field[:, 1:4, :] = low[:, 0:3, :]
        first, second = unpack(low[:, 3:4, :])
        kinds[:, 2:3, :] = first
        kinds[:, 3:4, :] = second
        field[:, 36:39, :] = high[:, 0:3, :]
        first, second = unpack(high[:, 3:4, :])
        kinds[:, 36:37, :] = first
        kinds[:, 37:38, :] = second

    @pl.when(core == 0)
    def _():
        sides(odd_in, even_in)

    @pl.when(core == 1)
    def _():
        sides(even_in, odd_in)

    def low(out):
        out[0:3] = field[0:3]
        out[3] = pack(kinds[0], kinds[1])

    def high(out):
        out[0:3] = field[X - 3 : X]
        out[3] = pack(kinds[X - 2], kinds[X - 1])

    @pl.when(half == 0)
    def _():
        high(even)
        low(odd)

    @pl.when(half == 1)
    def _():
        low(even)
        high(odd)


def rows_by_column(block_rows):
    return [block_rows[pl.ds(c, 8, stride=8), :] for c in range(8)]


def split(value):
    high = value.astype(jnp.bfloat16)
    low = (value - high.astype(F32)).astype(jnp.bfloat16)
    return high, low


def smooth_kernel(
    place, node_block, field, kinds, even_in, odd_in, weights_of, matrix, count, owner, drill, gain,
    smooth, payload,
    grown, mask, weights, shifted, level, chosen, matrix_vmem, sem,
):
    copy = pltpu.make_async_copy(matrix, matrix_vmem, sem)
    copy.start()
    half = place[0]

    def sides(low, high):
        grown[0:3] = low[0:3]
        grown[11:14] = high[0:3]
        first, second = unpack(low[3])
        mask[0] = first
        mask[1] = second
        first, second = unpack(high[3])
        mask[10] = first
        mask[11] = second

    @pl.when(half == 0)
    def _():
        sides(odd_in, even_in)

    @pl.when(half == 1)
    def _():
        sides(even_in, odd_in)

    grown[3:11] = field[...]
    mask[2:10] = kinds[...]

    def weigh(x, carry):
        for g in range(YP // 8):
            rows = pl.ds(g * 8, 8)
            kind = mask[x, rows, :]
            index = jnp.maximum(kind.astype(jnp.int32) - 1, 0)
            for o in range(27):
                weights[o, x, rows, :] = jnp.take_along_axis(
                    weights_of[o], index, axis=0, mode="promise_in_bounds"
                )
            mask[x, rows, :] = jnp.minimum(kind, 1.0)
        return carry

    lax.fori_loop(0, 12, weigh, 0)

    lanes = lax.broadcasted_iota(jnp.int32, (YP, W), 1) % Z
    not_first = lanes > 0
    not_last = lanes < Z - 1

    def shift_row(x, value):
        below = jnp.where(not_first, pltpu.roll(value, 1, axis=1), 0.0)
        above = jnp.where(not_last, pltpu.roll(value, W - 1, axis=1), 0.0)
        for c, moved in enumerate((below, value, above)):
            shifted[c, x] = pltpu.roll(moved, 1, axis=0)
            shifted[3 + c, x] = moved
            shifted[6 + c, x] = pltpu.roll(moved, YP - 1, axis=0)

    def apply(first_row, rows, put):
        def one(i, carry):
            x = first_row + i
            for g in range(YP // 8):
                part = pl.ds(g * 8, 8)
                total = None
                for a in range(3):
                    for bc in range(9):
                        term = weights[9 * a + bc, x - 1, part, :] * shifted[bc, x + a - 1, part, :]
                        total = term if total is None else total + term
                put(x, part, total * mask[x - 1, part, :])
            return carry

        lax.fori_loop(0, rows, one, 0)

    def shift_all(source, first_row, rows):
        def one(i, carry):
            shift_row(first_row + i, source[first_row + i])
            return carry

        lax.fori_loop(0, rows, one, 0)

    def put_second(x, part, value):
        level[0, x, part, :] = value

    def put_third(x, part, value):
        level[1, x, part, :] = 2.0 * value - grown[x, part, :]

    def put_fourth(x, part, value):
        second = level[0, x, part, :]
        fourth = 2.0 * value - second
        level[2, x, part, :] = (
            CHEB[0] * grown[x, part, :]
            + CHEB[1] * second
            + CHEB[2] * level[1, x, part, :]
            + CHEB[3] * fourth
        )

    shift_all(grown, 0, 14)
    apply(1, 12, put_second)
    shift_all(level.at[0], 1, 12)
    apply(2, 10, put_third)
    shift_all(level.at[1], 2, 10)
    apply(3, 8, put_fourth)
    for x in range(X):
        for g in range(4):
            smooth[x * 4 + g] = level[2, x + 3, OFF + 8 * g : OFF + 8 * g + 8, :]

    for b in range(BLOCKS):
        chosen[pl.ds(8 * b, 8), :] = smooth[node_block[b]]
    columns = rows_by_column(chosen)
    low = half_lanes((8, W))
    parts = ([], [])
    for j in range(4):
        one, two = columns[2 * j], columns[2 * j + 1]
        parts[0].append(jnp.where(low, one, swap_halves(two)))
        parts[1].append(jnp.where(low, swap_halves(one), two))
    values = [jnp.concatenate(p, axis=1) for p in parts]
    pieces = [split(v) for v in values]
    left = jnp.concatenate([pieces[0][0], pieces[1][0], pieces[0][1], pieces[1][1]], axis=0)
    copy.wait()
    block = lax.broadcasted_iota(jnp.int32, (BLOCKS, SAMPLES), 0)
    sums = [jnp.zeros((BLOCKS, SAMPLES), F32) for _ in range(2)]
    for b in range(BLOCKS):
        product = lax.dot_general(
            left, matrix_vmem[b], (((1,), (1,)), ((), ())), preferred_element_type=F32
        )
        for r in range(2):
            both = product[8 * r : 8 * r + 8] + product[16 + 8 * r : 24 + 8 * r]
            sums[r] = jnp.where(block == b, both, sums[r])
    live = lax.broadcasted_iota(jnp.int32, (BLOCKS, SAMPLES), 1) < count[...]
    for r in range(2):
        payload[8 * r : 8 * r + 8, :] = jnp.where(live, sums[r], 0.0)
    for k in range(2):
        for h in range(2):
            payload[16 + 2 * k + h : 17 + 2 * k + h, 0:W] = drill[k : k + 1, h * W : h * W + W]
            payload[20 + 2 * k + h : 21 + 2 * k + h, 0:W] = gain[k : k + 1, h * W : h * W + W]
    payload[16:24, W : 2 * W] = jnp.broadcast_to(owner[...].astype(F32), (8, W))


def update_kernel(
    place, node_block, wanted, here, there, smooth, matrix, count, drill, gain,
    out, misfit,
    totals, update, matrix_vmem, sem,
):
    copy = pltpu.make_async_copy(matrix, matrix_vmem, sem)
    copy.start()
    targets = BLOCKS + 2

    def add(source):
        def one(n, sums):
            x, z = n // 2, n % 2
            kind = source[x, z, 16:24, W : 2 * W]
            fields = [
                [source[x, z, 8 * r : 8 * r + 8, h * W : h * W + W] for h in range(2)]
                for r in range(2)
            ]
            result = []
            for t in range(targets):
                hit = kind == wanted[t].astype(F32)
                for r in range(2):
                    for h in range(2):
                        result.append(sums[4 * t + 2 * r + h] + jnp.where(hit, fields[r][h], 0.0))
            return tuple(result)

        return one

    sums = tuple(jnp.zeros((8, W), F32) for _ in range(4 * targets))
    sums = lax.fori_loop(0, 32, add(here), sums)
    sums = lax.fori_loop(0, 32, add(there), sums)
    for t in range(targets):
        for r in range(2):
            for h in range(2):
                totals[r, t : t + 1, h * W : h * W + W] = jnp.sum(
                    sums[4 * t + 2 * r + h], axis=0, keepdims=True
                )
    half, core = place[0], place[1]
    for k in range(2):
        for r in range(2):
            misfit[k, r : r + 1, :] = drill[k : k + 1, :] - totals[r, BLOCKS + k : BLOCKS + k + 1, :]

    live = lax.broadcasted_iota(jnp.int32, (BLOCKS, SAMPLES), 1) < count[...]
    for b in range(BLOCKS):
        k = wanted[b]
        tile = k // 2
        sx, sy = tile // 8, tile % 8
        where_x = (sx // 2) * 4 + sy // 2
        where_z = (sx % 2) ^ half
        row = k % 2

        def fetch(source):
            held = source[where_x, where_z, 16:24, 0:W]
            for h in range(2):
                for which in range(2):
                    base = 4 * which + h
                    totals[2 + which, b : b + 1, h * W : h * W + W] = jnp.where(
                        row == 0, held[base : base + 1], held[base + 2 : base + 3]
                    )

        @pl.when(sy % 2 == core)
        def _():
            fetch(here)

        @pl.when(sy % 2 != core)
        def _():
            fetch(there)

    picked = [
        jnp.where(live, totals[3, 0:BLOCKS, :] * (totals[2, 0:BLOCKS, :] - totals[r, 0:BLOCKS, :]), 0.0)
        for r in range(2)
    ]
    pieces = [split(v) for v in picked]
    left = jnp.concatenate([pieces[0][0], pieces[1][0], pieces[0][1], pieces[1][1]], axis=0)
    copy.wait()
    block = lax.broadcasted_iota(jnp.int32, (BLOCKS, NODES), 0)
    sums = [jnp.zeros((BLOCKS, NODES), F32) for _ in range(2)]
    for b in range(BLOCKS):
        product = jnp.dot(left, matrix_vmem[b], preferred_element_type=F32)
        for r in range(2):
            both = product[8 * r : 8 * r + 8] + product[16 + 8 * r : 24 + 8 * r]
            sums[r] = jnp.where(block == b, both, sums[r])
    low = half_lanes((8, W))
    for j in range(4):
        one, two = sums[0][:, j * W : j * W + W], sums[1][:, j * W : j * W + W]
        update[pl.ds(2 * j, 8, stride=8), :] = jnp.where(low, one, swap_halves(two))
        update[pl.ds(2 * j + 1, 8, stride=8), :] = jnp.where(low, swap_halves(one), two)
    out[...] = smooth[...]
    for b in range(BLOCKS):
        n = node_block[b]
        out[n] = out[n] + update[8 * b : 8 * b + 8, :]


def shape(*dims, dtype=F32):
    return jax.ShapeDtypeStruct(dims, dtype)


def shards(
    noise, classes, table, obs_matrix, node_block, sample_block, sample_count, drill_data, obs_gain
):
    place = jnp.stack([lax.axis_index("zh"), lax.axis_index("core")]).astype(jnp.int32)
    tile = lax.axis_index(("x", "zh", "y", "core"))
    wanted = jnp.concatenate([sample_block, 2 * tile + jnp.arange(2, dtype=jnp.int32)])
    wanted = wanted.astype(jnp.int32)
    weights_of = jnp.broadcast_to(table.T[:, :, None], (27, 8, W))
    count = sample_count[:, None]
    owner = sample_block[:, None]

    even, odd, doubled = pl.pallas_call(
        edge_y_kernel,
        out_shape=(shape(X, 4, W), shape(X, 4, W), shape(X, Y, W)),
        in_specs=[SMEM, VMEM, VMEM],
        out_specs=(VMEM, VMEM, VMEM),
        name="edge_y",
    )(place, noise, classes)
    odd = permute(odd, ("y", "core"), odd_pair)
    even = permute(even, ("y", "core"), even_pair)
    field, kinds, even, odd = pl.pallas_call(
        edge_x_kernel,
        out_shape=(shape(X, YP, W), shape(X, YP, W), shape(4, YP, W), shape(4, YP, W)),
        in_specs=[SMEM] + [VMEM] * 4,
        out_specs=(VMEM,) * 4,
        name="edge_x",
    )(place, noise, doubled, even, odd)
    odd = permute(odd, ("x", "zh"), odd_pair)
    even = permute(even, ("x", "zh"), even_pair)
    smooth, payload = pl.pallas_call(
        smooth_kernel,
        out_shape=(shape(32, 8, W), shape(ROWS, SAMPLES)),
        in_specs=[SMEM, SMEM] + [VMEM] * 5 + [ANY] + [VMEM] * 4,
        out_specs=(VMEM, VMEM),
        scratch_shapes=[
            pltpu.VMEM((14, YP, W), F32),
            pltpu.VMEM((12, YP, W), F32),
            pltpu.VMEM((27, 12, YP, W), F32),
            pltpu.VMEM((9, 14, YP, W), F32),
            pltpu.VMEM((3, 14, YP, W), F32),
            pltpu.VMEM((64, W), F32),
            pltpu.VMEM((BLOCKS, SAMPLES, NODES), jnp.bfloat16),
            pltpu.SemaphoreType.DMA,
        ],
        compiler_params=pltpu.CompilerParams(vmem_limit_bytes=32 * 1024 * 1024),
        name="smooth",
    )(
        place, node_block, field, kinds, even, odd, weights_of, obs_matrix, count, owner,
        drill_data, obs_gain,
    )
    other = permute(payload, ("zh",), lambda z: (z ^ 1,))
    pair = jnp.stack([payload, other])
    here = lax.all_to_all(
        jnp.broadcast_to(pair[None], (16, 2, ROWS, SAMPLES)), ("x", "y"), 0, 0, tiled=True
    )
    there = permute(here, ("core",), lambda c: (c ^ 1,))
    out, misfit = pl.pallas_call(
        update_kernel,
        out_shape=(shape(32, 8, W), shape(2, 2, SAMPLES)),
        in_specs=[SMEM, SMEM, SMEM, VMEM, VMEM, VMEM, ANY, VMEM, VMEM, VMEM],
        out_specs=(VMEM, VMEM),
        scratch_shapes=[
            pltpu.VMEM((4, 16, SAMPLES), F32),
            pltpu.VMEM((64, W), F32),
            pltpu.VMEM((BLOCKS, SAMPLES, NODES), jnp.bfloat16),
            pltpu.SemaphoreType.DMA,
        ],
        compiler_params=pltpu.CompilerParams(vmem_limit_bytes=32 * 1024 * 1024),
        name="update",
    )(
        place, node_block, wanted, here, there, smooth, obs_matrix, count, drill_data, obs_gain
    )
    return out.reshape(X, Y, W), misfit


def solution(mesh):
    fine = Mesh(
        mesh.devices.reshape(4, 4, 2, 4, 2), ("real", "x", "zh", "y", "core")
    )
    sx, sy = ("x", "zh"), ("y", "core")
    both = sx + sy
    in_specs = (
        P(sx, sy, "real"),
        P(sx, sy, None),
        P(),
        P(both, None, None),
        P(both),
        P(both),
        P(both),
        P(both, None),
        P(both, None),
    )
    out_specs = (P(sx, sy, "real"), P(both, "real", None))
    return jax.shard_map(shards, mesh=fine, in_specs=in_specs, out_specs=out_specs, check_vma=False)
```

```python
import itertools

import jax
import jax.numpy as jnp
from jax import lax
from jax.experimental import pallas as pl
from jax.experimental.pallas import tpu as pltpu
from jax.sharding import Mesh, PartitionSpec as P

CHEB = (0.6, 0.5, 0.3, 0.2)
X, Y, Z = 8, 32, 64
W = 2 * Z
YP = 40
OFF = 4
BLOCKS = 8
SAMPLES = 256
NODES = 512
ROWS = 24
F32 = jnp.float32
VMEM = pl.BlockSpec(memory_space=pltpu.VMEM)
SMEM = pl.BlockSpec(memory_space=pltpu.SMEM)
HBM = pl.BlockSpec(memory_space=pltpu.HBM)
SIZES = {"x": 4, "zh": 2, "y": 4, "core": 2}


def permute(value, axes, target):
    dims = [SIZES[a] for a in axes]

    def flat(place):
        number = 0
        for coordinate, size in zip(place, dims):
            number = number * size + coordinate
        return number

    pairs = []
    for place in itertools.product(*[range(d) for d in dims]):
        other = target(*place)
        if other is not None:
            pairs.append((flat(place), flat(other)))
    return lax.ppermute(value, axes if len(axes) > 1 else axes[0], pairs)


def even_pair(a, b):
    return (a, b ^ 1)


def odd_pair(a, b):
    if b == 1:
        return (a + 1, 0) if a < 3 else None
    return (a - 1, 1) if a > 0 else None


def half_lanes(shape):
    return lax.broadcasted_iota(jnp.int32, shape, len(shape) - 1) < Z


def swap_halves(value):
    return pltpu.roll(value, Z, axis=value.ndim - 1)


def pack(first, second):
    return jnp.where(half_lanes(first.shape), first, second)


def unpack(row):
    low = half_lanes(row.shape)
    other = swap_halves(row)
    return jnp.where(low, row, other), jnp.where(low, other, row)


def edge_y_kernel(place, noise, classes, even, odd, doubled):
    kinds = (classes[...] + 1).astype(F32)
    doubled[...] = jnp.concatenate([kinds, kinds], axis=-1)
    core = place[1]

    def low(out):
        out[:, 0:3, :] = noise[:, 0:3, :]
        out[:, 3:4, :] = pack(doubled[:, 0:1, :], doubled[:, 1:2, :])

    def high(out):
        out[:, 0:3, :] = noise[:, Y - 3 : Y, :]
        out[:, 3:4, :] = pack(doubled[:, Y - 2 : Y - 1, :], doubled[:, Y - 1 : Y, :])

    @pl.when(core == 0)
    def _():
        high(even)
        low(odd)

    @pl.when(core == 1)
    def _():
        low(even)
        high(odd)


def edge_x_kernel(place, noise, doubled, even_in, odd_in, field, kinds, even, odd):
    core, half = place[1], place[0]
    field[:, 0:8, :] = jnp.zeros((X, 8, W), F32)
    field[:, 32:40, :] = jnp.zeros((X, 8, W), F32)
    kinds[:, 0:8, :] = jnp.zeros((X, 8, W), F32)
    kinds[:, 32:40, :] = jnp.zeros((X, 8, W), F32)
    field[:, OFF : OFF + Y, :] = noise[...]
    kinds[:, OFF : OFF + Y, :] = doubled[...]

    def sides(low, high):
        field[:, 1:4, :] = low[:, 0:3, :]
        first, second = unpack(low[:, 3:4, :])
        kinds[:, 2:3, :] = first
        kinds[:, 3:4, :] = second
        field[:, 36:39, :] = high[:, 0:3, :]
        first, second = unpack(high[:, 3:4, :])
        kinds[:, 36:37, :] = first
        kinds[:, 37:38, :] = second

    @pl.when(core == 0)
    def _():
        sides(odd_in, even_in)

    @pl.when(core == 1)
    def _():
        sides(even_in, odd_in)

    def low(out):
        out[0:3] = field[0:3]
        out[3] = pack(kinds[0], kinds[1])

    def high(out):
        out[0:3] = field[X - 3 : X]
        out[3] = pack(kinds[X - 2], kinds[X - 1])

    @pl.when(half == 0)
    def _():
        high(even)
        low(odd)

    @pl.when(half == 1)
    def _():
        low(even)
        high(odd)


def rows_by_column(block_rows):
    return [block_rows[pl.ds(c, 8, stride=8), :] for c in range(8)]


def split(value):
    high = value.astype(jnp.bfloat16)
    low = (value - high.astype(F32)).astype(jnp.bfloat16)
    return high, low


def weigh(kinds, table, put):
    for b in range(3):
        moved = kinds if b == 1 else pltpu.roll(kinds, (b - 1) % YP, axis=0)
        index = jnp.maximum(moved.astype(jnp.int32) - 1, 0)
        for g in range(YP // 8):
            part = index[8 * g : 8 * g + 8]
            for a in range(3):
                for c in range(3):
                    o = 9 * a + 3 * b + c
                    put(
                        o,
                        pl.ds(8 * g, 8),
                        jnp.take_along_axis(table[o], part, axis=0, mode="promise_in_bounds"),
                    )


def spread_table(table, out):
    held = table[...]
    for o in range(27):
        out[o] = jnp.broadcast_to(held[:, o : o + 1], (8, W))


def lean(row):
    lanes = lax.broadcasted_iota(jnp.int32, (YP, W), 1) % Z
    below = jnp.where(lanes > 0, pltpu.roll(row, 1, axis=1), 0.0)
    above = jnp.where(lanes < Z - 1, pltpu.roll(row, W - 1, axis=1), 0.0)
    return below, row, above


def operate(weight, moved, inside):
    sums = []
    for b in range(3):
        total = None
        for a in range(3):
            for c in range(3):
                term = weight(9 * a + 3 * b + c) * moved(a, c)
                total = term if total is None else total + term
        sums.append(total)
    result = pltpu.roll(sums[0], 1, axis=0) + sums[1] + pltpu.roll(sums[2], YP - 1, axis=0)
    return result * inside


def interior_kernel(
    field, kinds, table, matrix, drill, gain,
    weights, first, second, third, smooth, tables, held_matrix, held_rows,
    sems,
):
    copies = [
        pltpu.make_async_copy(matrix, held_matrix, sems.at[0]),
        pltpu.make_async_copy(drill, held_rows.at[0], sems.at[1]),
        pltpu.make_async_copy(gain, held_rows.at[1], sems.at[2]),
    ]
    for copy in copies:
        copy.start()
    spread_table(table, tables)
    for x in range(X):
        def put(o, rows, value, x=x):
            weights[o, x, rows, :] = value

        weigh(kinds[x], tables, put)
        for c, value in enumerate(lean(field[x])):
            first[c, x] = value

    def step(source, start, x):
        return operate(
            lambda o: weights[o, x],
            lambda a, c: source[c, x + a - 1 - start],
            jnp.minimum(kinds[x], 1.0),
        )

    for x in range(1, 7):
        for c, value in enumerate(lean(step(first, 0, x))):
            second[c, x - 1] = value
    for x in range(2, 6):
        value = 2.0 * step(second, 1, x) - first[1, x]
        for c, value in enumerate(lean(value)):
            third[c, x - 2] = value
    for x in range(3, 5):
        fourth = 2.0 * step(third, 2, x) - second[1, x - 1]
        result = (
            CHEB[0] * first[1, x] + CHEB[1] * second[1, x - 1] + CHEB[2] * third[1, x - 2] + CHEB[3] * fourth
        )
        for g in range(4):
            smooth[4 * (x - 3) + g] = result[OFF + 8 * g : OFF + 8 * g + 8]
    for copy in copies:
        copy.wait()


def finish_kernel(
    place, node_block, count, owner, kinds, even_in, odd_in,
    weights, first, second, third, middle, tables, matrix, rows,
    smooth, payload,
    halo, halo_kinds, halo_weights, edge_first, edge_second, edge_third, chosen,
):
    half = place[0]

    def sides(low, high):
        halo[0:3] = low[0:3]
        halo[3:6] = high[0:3]
        one, two = unpack(low[3])
        halo_kinds[0], halo_kinds[1] = one, two
        one, two = unpack(high[3])
        halo_kinds[2], halo_kinds[3] = one, two

    @pl.when(half == 0)
    def _():
        sides(odd_in, even_in)

    @pl.when(half == 1)
    def _():
        sides(even_in, odd_in)

    smooth[12:20] = middle[...]
    for i in range(4):
        def put(o, part, value, i=i):
            halo_weights[o, i, part, :] = value

        weigh(halo_kinds[i], tables, put)
    for i in range(6):
        for c, value in enumerate(lean(halo[i])):
            edge_first[c, i] = value

    def weight(x):
        if 0 <= x < X:
            return (lambda o: weights[o, x]), jnp.minimum(kinds[x], 1.0)
        i = x + 2 if x < 0 else x - 6
        return (lambda o: halo_weights[o, i]), jnp.minimum(halo_kinds[i], 1.0)

    def at_first(x, c):
        if 0 <= x < X:
            return first[c, x]
        return edge_first[c, x + 3 if x < 0 else x - 5]

    def at_second(x, c):
        if 1 <= x < 7:
            return second[c, x - 1]
        return edge_second[c, x + 2 if x < 1 else x - 4]

    def at_third(x, c):
        if 2 <= x < 6:
            return third[c, x - 2]
        return edge_third[c, x + 1 if x < 2 else x - 3]

    def step(at, x):
        of, inside = weight(x)
        return operate(of, lambda a, c: at(x + a - 1, c), inside)

    for x in (-2, -1, 0, 7, 8, 9):
        for c, value in enumerate(lean(step(at_first, x))):
            edge_second[c, x + 2 if x < 1 else x - 4] = value
    for x in (-1, 0, 1, 6, 7, 8):
        value = 2.0 * step(at_second, x) - at_first(x, 1)
        for c, value in enumerate(lean(value)):
            edge_third[c, x + 1 if x < 2 else x - 3] = value
    for x in (0, 1, 2, 5, 6, 7):
        fourth = 2.0 * step(at_third, x) - at_second(x, 1)
        result = (
            CHEB[0] * at_first(x, 1) + CHEB[1] * at_second(x, 1) + CHEB[2] * at_third(x, 1) + CHEB[3] * fourth
        )
        for g in range(4):
            smooth[4 * x + g] = result[OFF + 8 * g : OFF + 8 * g + 8]

    for b in range(BLOCKS):
        chosen[pl.ds(8 * b, 8), :] = smooth[node_block[b]]
    columns = rows_by_column(chosen)
    low = half_lanes((8, W))
    parts = ([], [])
    for j in range(4):
        one, two = columns[2 * j], columns[2 * j + 1]
        parts[0].append(jnp.where(low, one, swap_halves(two)))
        parts[1].append(jnp.where(low, swap_halves(one), two))
    values = [jnp.concatenate(p, axis=1) for p in parts]
    pieces = [split(v) for v in values]
    left = jnp.concatenate([pieces[0][0], pieces[1][0], pieces[0][1], pieces[1][1]], axis=0)
    block = lax.broadcasted_iota(jnp.int32, (BLOCKS, SAMPLES), 0)
    sums = [jnp.zeros((BLOCKS, SAMPLES), F32) for _ in range(2)]
    for b in range(BLOCKS):
        product = lax.dot_general(
            left, matrix[b], (((1,), (1,)), ((), ())), preferred_element_type=F32
        )
        for r in range(2):
            both = product[8 * r : 8 * r + 8] + product[16 + 8 * r : 24 + 8 * r]
            sums[r] = jnp.where(block == b, both, sums[r])
    live = is_live(count)
    for r in range(2):
        payload[8 * r : 8 * r + 8, :] = jnp.where(live, sums[r], 0.0)
    payload[16:24, :] = jnp.zeros((8, SAMPLES), F32)
    for k in range(2):
        for h in range(2):
            for kind in range(2):
                row = 16 + 4 * kind + 2 * k + h
                payload[row : row + 1, 0:W] = rows[kind, k : k + 1, h * W : h * W + W]
    lane = lax.broadcasted_iota(jnp.int32, (8, W), 1)
    names = jnp.zeros((8, W), F32)
    for b in range(BLOCKS):
        names = jnp.where(lane == 8 * place[2] + b, (owner[b] + 1).astype(F32), names)
    payload[16:17, W : 2 * W] = names[0:1]


def is_live(count):
    block = lax.broadcasted_iota(jnp.int32, (BLOCKS, SAMPLES), 0)
    limit = jnp.zeros((BLOCKS, SAMPLES), jnp.int32)
    for b in range(BLOCKS):
        limit = jnp.where(block == b, count[b], limit)
    return lax.broadcasted_iota(jnp.int32, (BLOCKS, SAMPLES), 1) < limit


def collect(source, owner, place, core, out):
    half = place[0]
    names = []
    for z in range(2):
        total = source[0, z, 16:24, W : 2 * W]
        for n in range(1, 16):
            total = total + source[n, z, 16:24, W : 2 * W]
        names.append(total[0:1])
    names = jnp.concatenate(names, axis=1)
    target = lax.broadcasted_iota(jnp.int32, (16, 2 * W), 0)
    lane = lax.broadcasted_iota(jnp.int32, (16, 2 * W), 1)
    name = jnp.full((16, 2 * W), -1.0, F32)
    spot = jnp.full((16, 2 * W), -1, jnp.int32)
    for t in range(BLOCKS):
        k = owner[t]
        tiles = k // 2
        sx, sy = tiles // 8, tiles % 8
        where = ((sx % 2) ^ half) * W + ((sx // 2) * 4 + sy // 2) * 8 + 2 * (k % 2)
        where = jnp.where(sy % 2 == core, where, -1024)
        name = jnp.where(target == t, (k + 1).astype(F32), name)
        spot = jnp.where(target == t, where, spot)
    for t in range(2):
        name = jnp.where(target == BLOCKS + t, (2 * place[4] + t + 1).astype(F32), name)
    hit = (name == names).astype(jnp.bfloat16)
    for r in range(2):
        data = jnp.concatenate(
            [source[n, z, 8 * r : 8 * r + 8, :] for z in range(2) for n in range(16)], axis=0
        )
        high, low = split(data)
        out[r] = jnp.dot(hit, high, preferred_element_type=F32) + jnp.dot(
            hit, low, preferred_element_type=F32
        )
    data = jnp.concatenate([source[n, z, 16:24, 0:W] for z in range(2) for n in range(16)], axis=0)
    high, low = split(data)
    choose = jnp.concatenate(
        [(lane == spot + 4 * kind + h).astype(jnp.bfloat16) for kind in range(2) for h in range(2)], axis=0
    )
    found = jnp.dot(choose, high, preferred_element_type=F32) + jnp.dot(
        choose, low, preferred_element_type=F32
    )
    for kind in range(2):
        for h in range(2):
            row = 32 * kind + 16 * h
            out[2 + kind, :, h * W : h * W + W] = found[row : row + 16]


def collect_kernel(place, owner, here, out):
    collect(here, owner, place, place[1], out)


def update_kernel(
    place, node_block, owner, count, mine, there, smooth, matrix, rows,
    out, misfit,
    other, update,
):
    collect(there, owner, place, 1 - place[1], other)
    for k in range(2):
        for r in range(2):
            t = BLOCKS + k
            misfit[k, r : r + 1, :] = rows[0, k : k + 1, :] - (mine[r, t : t + 1, :] + other[r, t : t + 1, :])
    live = is_live(count)
    drill, gain = [mine[i, 0:BLOCKS, :] + other[i, 0:BLOCKS, :] for i in (2, 3)]
    picked = [
        jnp.where(live, gain * (drill - (mine[r, 0:BLOCKS, :] + other[r, 0:BLOCKS, :])), 0.0)
        for r in range(2)
    ]
    pieces = [split(v) for v in picked]
    left = jnp.concatenate([pieces[0][0], pieces[1][0], pieces[0][1], pieces[1][1]], axis=0)
    block = lax.broadcasted_iota(jnp.int32, (BLOCKS, NODES), 0)
    sums = [jnp.zeros((BLOCKS, NODES), F32) for _ in range(2)]
    for b in range(BLOCKS):
        product = jnp.dot(left, matrix[b], preferred_element_type=F32)
        for r in range(2):
            both = product[8 * r : 8 * r + 8] + product[16 + 8 * r : 24 + 8 * r]
            sums[r] = jnp.where(block == b, both, sums[r])
    low = half_lanes((8, W))
    for j in range(4):
        one, two = sums[0][:, j * W : j * W + W], sums[1][:, j * W : j * W + W]
        update[pl.ds(2 * j, 8, stride=8), :] = jnp.where(low, one, swap_halves(two))
        update[pl.ds(2 * j + 1, 8, stride=8), :] = jnp.where(low, swap_halves(one), two)
    out[...] = smooth[...]
    for b in range(BLOCKS):
        n = node_block[b]
        out[n] = out[n] + update[8 * b : 8 * b + 8, :]


def shape(*dims, dtype=F32):
    return jax.ShapeDtypeStruct(dims, dtype)


def call(kernel, outs, ins, name, scratch=()):
    return pl.pallas_call(
        kernel,
        out_shape=outs,
        in_specs=ins,
        out_specs=(VMEM,) * len(outs),
        scratch_shapes=scratch,
        compiler_params=pltpu.CompilerParams(vmem_limit_bytes=24 * 1024 * 1024),
        name=name,
    )


def shards(
    noise, classes, table, obs_matrix, node_block, sample_block, sample_count, drill_data, obs_gain
):
    place = jnp.stack(
        [
            lax.axis_index("zh"),
            lax.axis_index("core"),
            lax.axis_index(("x", "y")),
            lax.axis_index(("x", "y")),
            lax.axis_index(("x", "zh", "y", "core")),
        ]
    ).astype(jnp.int32)

    even, odd, doubled = call(
        edge_y_kernel,
        (shape(X, 4, W), shape(X, 4, W), shape(X, Y, W)),
        [SMEM, VMEM, VMEM],
        "edge_y",
    )(place, noise, classes)
    odd = permute(odd, ("y", "core"), odd_pair)
    even = permute(even, ("y", "core"), even_pair)
    field, kinds, even, odd = call(
        edge_x_kernel,
        (shape(X, YP, W), shape(X, YP, W), shape(4, YP, W), shape(4, YP, W)),
        [SMEM] + [VMEM] * 4,
        "edge_x",
    )(place, noise, doubled, even, odd)
    odd = permute(odd, ("x", "zh"), odd_pair)
    even = permute(even, ("x", "zh"), even_pair)
    weights, first, second, third, middle, tables, matrix, rows = call(
        interior_kernel,
        (
            shape(27, X, YP, W),
            shape(3, X, YP, W),
            shape(3, 6, YP, W),
            shape(3, 4, YP, W),
            shape(8, 8, W),
            shape(27, 8, W),
            shape(BLOCKS, SAMPLES, NODES, dtype=jnp.bfloat16),
            shape(2, 2, SAMPLES),
        ),
        [VMEM] * 3 + [HBM] * 3,
        "interior",
        [pltpu.SemaphoreType.DMA((3,))],
    )(field, kinds, table, obs_matrix, drill_data, obs_gain)
    smooth, payload = call(
        finish_kernel,
        (shape(32, 8, W), shape(ROWS, SAMPLES)),
        [SMEM] * 4 + [VMEM] * 11,
        "finish",
        [
            pltpu.VMEM((6, YP, W), F32),
            pltpu.VMEM((4, YP, W), F32),
            pltpu.VMEM((27, 4, YP, W), F32),
            pltpu.VMEM((3, 6, YP, W), F32),
            pltpu.VMEM((3, 6, YP, W), F32),
            pltpu.VMEM((3, 6, YP, W), F32),
            pltpu.VMEM((64, W), F32),
        ],
    )(
        place, node_block, sample_count, sample_block, kinds, even, odd,
        weights, first, second, third, middle, tables, matrix, rows,
    )
    other = permute(payload, ("zh",), lambda z: (z ^ 1,))
    pair = jnp.stack([payload, other])
    here = lax.all_to_all(
        jnp.broadcast_to(pair[None], (16, 2, ROWS, SAMPLES)), ("x", "y"), 0, 0, tiled=True
    )
    there = permute(here, ("core",), lambda c: (c ^ 1,))
    (mine,) = call(collect_kernel, (shape(4, 16, SAMPLES),), [SMEM, SMEM, VMEM], "collect")(
        place, sample_block, here
    )
    out, misfit = call(
        update_kernel,
        (shape(32, 8, W), shape(2, 2, SAMPLES)),
        [SMEM] * 4 + [VMEM] * 5,
        "update",
        [pltpu.VMEM((4, 16, SAMPLES), F32), pltpu.VMEM((64, W), F32)],
    )(place, node_block, sample_block, sample_count, mine, there, smooth, matrix, rows)
    return out.reshape(X, Y, W), misfit


def solution(mesh):
    fine = Mesh(
        mesh.devices.reshape(4, 4, 2, 4, 2), ("real", "x", "zh", "y", "core")
    )
    sx, sy = ("x", "zh"), ("y", "core")
    both = sx + sy
    in_specs = (
        P(sx, sy, "real"),
        P(sx, sy, None),
        P(),
        P(both, None, None),
        P(both),
        P(both),
        P(both),
        P(both, None),
        P(both, None),
    )
    out_specs = (P(sx, sy, "real"), P(both, "real", None))
    return jax.shard_map(shards, mesh=fine, in_specs=in_specs, out_specs=out_specs, check_vma=False)
```

```python
import itertools

import jax
import jax.numpy as jnp
from jax import lax
from jax.experimental import pallas as pl
from jax.experimental.pallas import tpu as pltpu
from jax.sharding import Mesh, PartitionSpec as P

CHEB = (0.6, 0.5, 0.3, 0.2)
X, Y, Z = 8, 32, 64
W = 2 * Z
YP = 40
OFF = 4
BLOCKS = 8
SAMPLES = 256
NODES = 512
ROWS = 24
F32 = jnp.float32
VMEM = pl.BlockSpec(memory_space=pltpu.VMEM)
SMEM = pl.BlockSpec(memory_space=pltpu.SMEM)
HBM = pl.BlockSpec(memory_space=pltpu.HBM)
SIZES = {"x": 4, "zh": 2, "y": 4, "core": 2}


def permute(value, axes, target):
    dims = [SIZES[a] for a in axes]

    def flat(place):
        number = 0
        for coordinate, size in zip(place, dims):
            number = number * size + coordinate
        return number

    pairs = []
    for place in itertools.product(*[range(d) for d in dims]):
        other = target(*place)
        if other is not None:
            pairs.append((flat(place), flat(other)))
    return lax.ppermute(value, axes if len(axes) > 1 else axes[0], pairs)


def even_pair(a, b):
    return (a, b ^ 1)


def odd_pair(a, b):
    if b == 1:
        return (a + 1, 0) if a < 3 else None
    return (a - 1, 1) if a > 0 else None


def half_lanes(shape):
    return lax.broadcasted_iota(jnp.int32, shape, len(shape) - 1) < Z


def swap_halves(value):
    return pltpu.roll(value, Z, axis=value.ndim - 1)


def pack(first, second):
    return jnp.where(half_lanes(first.shape), first, second)


def unpack(row):
    low = half_lanes(row.shape)
    other = swap_halves(row)
    return jnp.where(low, row, other), jnp.where(low, other, row)


def edge_y_kernel(
    place, noise_far, classes_far, owner_far,
    even, odd, noise, doubled, names,
    classes, owner, sems,
):
    copies = [
        pltpu.make_async_copy(noise_far, noise, sems.at[0]),
        pltpu.make_async_copy(classes_far, classes, sems.at[1]),
        pltpu.make_async_copy(owner_far, owner, sems.at[2]),
    ]
    for copy in copies:
        copy.start()
    for copy in copies:
        copy.wait()
    kinds = (classes[...] + 1).astype(F32)
    doubled[...] = jnp.concatenate([kinds, kinds], axis=-1)
    core = place[1]
    lane = lax.broadcasted_iota(jnp.int32, (8, W), 1)
    own = jnp.zeros((8, W), F32)
    for b in range(BLOCKS):
        own = jnp.where(lane == b, (owner[b] + 1).astype(F32), own)
    names[...] = own
    even[X] = own[0:4]

    def low(out):
        out[0:X, 0:3, :] = noise[:, 0:3, :]
        out[0:X, 3:4, :] = pack(doubled[:, 0:1, :], doubled[:, 1:2, :])

    def high(out):
        out[0:X, 0:3, :] = noise[:, Y - 3 : Y, :]
        out[0:X, 3:4, :] = pack(doubled[:, Y - 2 : Y - 1, :], doubled[:, Y - 1 : Y, :])

    @pl.when(core == 0)
    def _():
        high(even)
        low(odd)

    @pl.when(core == 1)
    def _():
        low(even)
        high(odd)


def edge_x_kernel(
    place, noise, doubled, names, even_in, odd_in, field, kinds, even, odd, lists
):
    core, half = place[1], place[0]
    field[:, 0:8, :] = jnp.zeros((X, 8, W), F32)
    field[:, 32:40, :] = jnp.zeros((X, 8, W), F32)
    kinds[:, 0:8, :] = jnp.zeros((X, 8, W), F32)
    kinds[:, 32:40, :] = jnp.zeros((X, 8, W), F32)
    field[:, OFF : OFF + Y, :] = noise[...]
    kinds[:, OFF : OFF + Y, :] = doubled[...]

    lists[0:4] = names[0:4]
    lists[1:2] = even_in[X, 0:1, :]

    def sides(low, high):
        field[:, 1:4, :] = low[0:X, 0:3, :]
        first, second = unpack(low[0:X, 3:4, :])
        kinds[:, 2:3, :] = first
        kinds[:, 3:4, :] = second
        field[:, 36:39, :] = high[0:X, 0:3, :]
        first, second = unpack(high[0:X, 3:4, :])
        kinds[:, 36:37, :] = first
        kinds[:, 37:38, :] = second

    @pl.when(core == 0)
    def _():
        sides(odd_in, even_in)

    @pl.when(core == 1)
    def _():
        sides(even_in, odd_in)

    def low(out):
        out[0:3] = field[0:3]
        out[3] = pack(kinds[0], kinds[1])

    def high(out):
        out[0:3] = field[X - 3 : X]
        out[3] = pack(kinds[X - 2], kinds[X - 1])

    @pl.when(half == 0)
    def _():
        high(even)
        low(odd)

    @pl.when(half == 1)
    def _():
        low(even)
        high(odd)

    even[3, 0:1, :] = lists[0:1]
    even[3, YP - 1 : YP, :] = lists[1:2]


def rows_by_column(block_rows):
    return [block_rows[pl.ds(c, 8, stride=8), :] for c in range(8)]


def split(value):
    high = value.astype(jnp.bfloat16)
    low = (value - high.astype(F32)).astype(jnp.bfloat16)
    return high, low


def weigh(kinds, table, put):
    for b in range(3):
        moved = kinds if b == 1 else pltpu.roll(kinds, (b - 1) % YP, axis=0)
        index = jnp.maximum(moved.astype(jnp.int32) - 1, 0)
        for g in range(YP // 8):
            part = index[8 * g : 8 * g + 8]
            for a in range(3):
                for c in range(3):
                    o = 9 * a + 3 * b + c
                    put(
                        o,
                        pl.ds(8 * g, 8),
                        jnp.take_along_axis(table[o], part, axis=0, mode="promise_in_bounds"),
                    )


def spread_table(table, out):
    held = table[...]
    for o in range(27):
        out[o] = jnp.broadcast_to(held[:, o : o + 1], (8, W))


def lean(row):
    lanes = lax.broadcasted_iota(jnp.int32, (YP, W), 1) % Z
    below = jnp.where(lanes > 0, pltpu.roll(row, 1, axis=1), 0.0)
    above = jnp.where(lanes < Z - 1, pltpu.roll(row, W - 1, axis=1), 0.0)
    return below, row, above


def operate(weight, moved, inside):
    sums = []
    for b in range(3):
        total = None
        for a in range(3):
            for c in range(3):
                term = weight(9 * a + 3 * b + c) * moved(a, c)
                total = term if total is None else total + term
        sums.append(total)
    result = pltpu.roll(sums[0], 1, axis=0) + sums[1] + pltpu.roll(sums[2], YP - 1, axis=0)
    return result * inside


def interior_kernel(
    field, kinds, table, matrix, drill, gain,
    weights, first, second, third, smooth, tables, held_matrix, held_rows,
    held_table, sems,
):
    copies = [
        pltpu.make_async_copy(matrix, held_matrix, sems.at[0]),
        pltpu.make_async_copy(drill, held_rows.at[0], sems.at[1]),
        pltpu.make_async_copy(gain, held_rows.at[1], sems.at[2]),
        pltpu.make_async_copy(table, held_table, sems.at[3]),
    ]
    for copy in reversed(copies):
        copy.start()
    copies[3].wait()
    spread_table(held_table, tables)
    for x in range(X):
        def put(o, rows, value, x=x):
            weights[o, x, rows, :] = value

        weigh(kinds[x], tables, put)
        for c, value in enumerate(lean(field[x])):
            first[c, x] = value

    def step(source, start, x):
        return operate(
            lambda o: weights[o, x],
            lambda a, c: source[c, x + a - 1 - start],
            jnp.minimum(kinds[x], 1.0),
        )

    for x in range(1, 7):
        for c, value in enumerate(lean(step(first, 0, x))):
            second[c, x - 1] = value
    for x in range(2, 6):
        value = 2.0 * step(second, 1, x) - first[1, x]
        for c, value in enumerate(lean(value)):
            third[c, x - 2] = value
    for x in range(3, 5):
        fourth = 2.0 * step(third, 2, x) - second[1, x - 1]
        result = (
            CHEB[0] * first[1, x] + CHEB[1] * second[1, x - 1] + CHEB[2] * third[1, x - 2] + CHEB[3] * fourth
        )
        for g in range(4):
            smooth[4 * (x - 3) + g] = result[OFF + 8 * g : OFF + 8 * g + 8]
    for copy in copies[:3]:
        copy.wait()


def finish_kernel(
    place, node_block, count, owner, kinds, even_in, odd_in, near,
    weights, first, second, third, middle, tables, matrix, rows,
    smooth, payload, lists,
    halo, halo_kinds, halo_weights, edge_first, edge_second, edge_third, chosen,
):
    half = place[0]

    def sides(low, high):
        halo[0:3] = low[0:3]
        halo[3:6] = high[0:3]
        one, two = unpack(low[3])
        halo_kinds[0], halo_kinds[1] = one, two
        one, two = unpack(high[3])
        halo_kinds[2], halo_kinds[3] = one, two
        halo_kinds[:, 0:1, :] = jnp.zeros((4, 1, W), F32)
        halo_kinds[:, YP - 1 : YP, :] = jnp.zeros((4, 1, W), F32)

    lists[0:4] = near[0:4]
    lists[4:8] = jnp.zeros((4, W), F32)
    lists[2:3] = even_in[3, 0:1, :]
    lists[3:4] = even_in[3, YP - 1 : YP, :]

    @pl.when(half == 0)
    def _():
        sides(odd_in, even_in)

    @pl.when(half == 1)
    def _():
        sides(even_in, odd_in)

    smooth[12:20] = middle[...]
    for i in range(4):
        def put(o, part, value, i=i):
            halo_weights[o, i, part, :] = value

        weigh(halo_kinds[i], tables, put)
    for i in range(6):
        for c, value in enumerate(lean(halo[i])):
            edge_first[c, i] = value

    def weight(x):
        if 0 <= x < X:
            return (lambda o: weights[o, x]), jnp.minimum(kinds[x], 1.0)
        i = x + 2 if x < 0 else x - 6
        return (lambda o: halo_weights[o, i]), jnp.minimum(halo_kinds[i], 1.0)

    def at_first(x, c):
        if 0 <= x < X:
            return first[c, x]
        return edge_first[c, x + 3 if x < 0 else x - 5]

    def at_second(x, c):
        if 1 <= x < 7:
            return second[c, x - 1]
        return edge_second[c, x + 2 if x < 1 else x - 4]

    def at_third(x, c):
        if 2 <= x < 6:
            return third[c, x - 2]
        return edge_third[c, x + 1 if x < 2 else x - 3]

    def step(at, x):
        of, inside = weight(x)
        return operate(of, lambda a, c: at(x + a - 1, c), inside)

    for x in (-2, -1, 0, 7, 8, 9):
        for c, value in enumerate(lean(step(at_first, x))):
            edge_second[c, x + 2 if x < 1 else x - 4] = value
    for x in (-1, 0, 1, 6, 7, 8):
        value = 2.0 * step(at_second, x) - at_first(x, 1)
        for c, value in enumerate(lean(value)):
            edge_third[c, x + 1 if x < 2 else x - 3] = value
    for x in (0, 1, 2, 5, 6, 7):
        fourth = 2.0 * step(at_third, x) - at_second(x, 1)
        result = (
            CHEB[0] * at_first(x, 1) + CHEB[1] * at_second(x, 1) + CHEB[2] * at_third(x, 1) + CHEB[3] * fourth
        )
        for g in range(4):
            smooth[4 * x + g] = result[OFF + 8 * g : OFF + 8 * g + 8]

    for b in range(BLOCKS):
        chosen[pl.ds(8 * b, 8), :] = smooth[node_block[b]]
    columns = rows_by_column(chosen)
    low = half_lanes((8, W))
    parts = ([], [])
    for j in range(4):
        one, two = columns[2 * j], columns[2 * j + 1]
        parts[0].append(jnp.where(low, one, swap_halves(two)))
        parts[1].append(jnp.where(low, swap_halves(one), two))
    values = [jnp.concatenate(p, axis=1) for p in parts]
    pieces = [split(v) for v in values]
    left = jnp.concatenate([pieces[0][0], pieces[1][0], pieces[0][1], pieces[1][1]], axis=0)
    block = lax.broadcasted_iota(jnp.int32, (BLOCKS, SAMPLES), 0)
    sums = [jnp.zeros((BLOCKS, SAMPLES), F32) for _ in range(2)]
    for b in range(BLOCKS):
        product = lax.dot_general(
            left, matrix[b], (((1,), (1,)), ((), ())), preferred_element_type=F32
        )
        for r in range(2):
            both = product[8 * r : 8 * r + 8] + product[16 + 8 * r : 24 + 8 * r]
            sums[r] = jnp.where(block == b, both, sums[r])
    live = is_live(count)
    for r in range(2):
        payload[8 * r : 8 * r + 8, :] = jnp.where(live, sums[r], 0.0)
    payload[16:24, :] = jnp.zeros((8, SAMPLES), F32)
    for k in range(2):
        for h in range(2):
            for kind in range(2):
                row = 16 + 4 * kind + 2 * k + h
                payload[row : row + 1, 0:W] = rows[kind, k : k + 1, h * W : h * W + W]
    lane = lax.broadcasted_iota(jnp.int32, (8, W), 1)
    names = jnp.zeros((8, W), F32)
    for b in range(BLOCKS):
        names = jnp.where(lane == 8 * place[2] + b, (owner[b] + 1).astype(F32), names)
    payload[16:17, W : 2 * W] = names[0:1]


def is_live(count):
    block = lax.broadcasted_iota(jnp.int32, (BLOCKS, SAMPLES), 0)
    limit = jnp.zeros((BLOCKS, SAMPLES), jnp.int32)
    for b in range(BLOCKS):
        limit = jnp.where(block == b, count[b], limit)
    return lax.broadcasted_iota(jnp.int32, (BLOCKS, SAMPLES), 1) < limit


def collect_kernel(place, lists, here, keep, send):
    names = here[0, 16:24, W : 2 * W]
    for n in range(1, 16):
        names = names + here[n, 16:24, W : 2 * W]
    names = jnp.broadcast_to(names[0:1], (8, W))
    lane = lax.broadcasted_iota(jnp.int32, (8, W), 1)
    row = lax.broadcasted_iota(jnp.int32, (8, W), 0)
    hits, spots = [], []
    for member in range(4):
        tile = place[4] ^ (1 if member & 1 else 0) ^ (8 if member & 2 else 0)
        held = jnp.broadcast_to(lists[member : member + 1], (8, W))
        name = jnp.sum(jnp.where(lane == row, held, 0.0), axis=1, keepdims=True)
        name = jnp.broadcast_to(name, (8, W))
        hits.append(name == names)
        hits.append((2 * tile + 1 + (row & 1)).astype(F32) == names)
        block = name.astype(jnp.int32) - 1
        holder = block >> 1
        spot = ((holder >> 4) * 4 + ((holder >> 1) & 3)) * 8 + 2 * (block & 1)
        mine = ((holder & 1) == place[1]) & (((holder >> 3) & 1) == place[0])
        spots.append(jnp.where(mine, spot, -1024))
    hit = jnp.concatenate([h.astype(F32) for h in hits], axis=0).astype(jnp.bfloat16)
    spots = jnp.concatenate(spots, axis=0)
    lane = lax.broadcasted_iota(jnp.int32, (32, W), 1)
    choose = jnp.concatenate(
        [(lane == spots + 4 * kind + h).astype(F32) for kind in range(2) for h in range(2)], axis=0
    ).astype(jnp.bfloat16)

    def gather(left, rows, lanes):
        data = jnp.concatenate([here[n, rows, lanes] for n in range(16)], axis=0)
        high, low = split(data)
        return jnp.dot(left, high, preferred_element_type=F32) + jnp.dot(
            left, low, preferred_element_type=F32
        )

    totals = [gather(hit, slice(8 * r, 8 * r + 8), slice(0, 2 * W)) for r in range(2)]
    found = gather(choose, slice(16, 24), slice(0, W))
    row = lax.broadcasted_iota(jnp.int32, (8, SAMPLES), 0)
    for member in range(4):
        out = (send if member & 1 else keep).at[member // 2]
        drill, gain = [
            jnp.concatenate(
                [found[64 * kind + 32 * h + 8 * member : 64 * kind + 32 * h + 8 * member + 8] for h in range(2)],
                axis=1,
            )
            for kind in range(2)
        ]
        for r in range(2):
            out[8 * r : 8 * r + 8, :] = drill - totals[r][16 * member : 16 * member + 8]
        out[16:24, :] = gain
        own = [totals[r][16 * member + 8 : 16 * member + 16] for r in range(2)]
        out[24:32, :] = jnp.where(row < 2, own[0], own[1])


def update_kernel(
    node_block, count, keep, near, far, smooth, matrix, rows,
    out, misfit,
    update,
):
    sums = keep[0] + near[0] + far[...]
    for k in range(2):
        for r in range(2):
            t = 24 + 2 * r + k
            misfit[k, r : r + 1, :] = rows[0, k : k + 1, :] - sums[t : t + 1, :]
    live = is_live(count)
    picked = [jnp.where(live, sums[16:24] * sums[8 * r : 8 * r + 8], 0.0) for r in range(2)]
    pieces = [split(v) for v in picked]
    left = jnp.concatenate([pieces[0][0], pieces[1][0], pieces[0][1], pieces[1][1]], axis=0)
    block = lax.broadcasted_iota(jnp.int32, (BLOCKS, NODES), 0)
    sums = [jnp.zeros((BLOCKS, NODES), F32) for _ in range(2)]
    for b in range(BLOCKS):
        product = jnp.dot(left, matrix[b], preferred_element_type=F32)
        for r in range(2):
            both = product[8 * r : 8 * r + 8] + product[16 + 8 * r : 24 + 8 * r]
            sums[r] = jnp.where(block == b, both, sums[r])
    low = half_lanes((8, W))
    for j in range(4):
        one, two = sums[0][:, j * W : j * W + W], sums[1][:, j * W : j * W + W]
        update[pl.ds(2 * j, 8, stride=8), :] = jnp.where(low, one, swap_halves(two))
        update[pl.ds(2 * j + 1, 8, stride=8), :] = jnp.where(low, swap_halves(one), two)
    out[...] = smooth[...]
    for b in range(BLOCKS):
        n = node_block[b]
        out[n] = out[n] + update[8 * b : 8 * b + 8, :]


def shape(*dims, dtype=F32):
    return jax.ShapeDtypeStruct(dims, dtype)


def call(kernel, outs, ins, name, scratch=()):
    return pl.pallas_call(
        kernel,
        out_shape=outs,
        in_specs=ins,
        out_specs=(VMEM,) * len(outs),
        scratch_shapes=scratch,
        compiler_params=pltpu.CompilerParams(vmem_limit_bytes=24 * 1024 * 1024),
        name=name,
    )


def shards(
    noise, classes, table, obs_matrix, node_block, sample_block, sample_count, drill_data, obs_gain
):
    place = jnp.stack(
        [
            lax.axis_index("zh"),
            lax.axis_index("core"),
            lax.axis_index(("x", "y")),
            lax.axis_index(("x", "y")),
            lax.axis_index(("x", "zh", "y", "core")),
        ]
    ).astype(jnp.int32)
    noise, classes, table, obs_matrix, owner, drill_data, obs_gain = [
        pltpu.with_memory_space_constraint(a, pltpu.HBM)
        for a in (noise, classes, table, obs_matrix, sample_block, drill_data, obs_gain)
    ]

    even, odd, near_noise, doubled, names = call(
        edge_y_kernel,
        (shape(X + 1, 4, W), shape(X, 4, W), shape(X, Y, W), shape(X, Y, W), shape(8, W)),
        [SMEM, HBM, HBM, HBM],
        "edge_y",
        [
            pltpu.VMEM((X, Y, Z), jnp.int32),
            pltpu.SMEM((BLOCKS,), jnp.int32),
            pltpu.SemaphoreType.DMA((3,)),
        ],
    )(place, noise, classes, owner)
    even = permute(even, ("y", "core"), even_pair)
    odd = permute(odd, ("y", "core"), odd_pair)
    field, kinds, even, odd, lists = call(
        edge_x_kernel,
        (shape(X, YP, W), shape(X, YP, W), shape(4, YP, W), shape(4, YP, W), shape(4, W)),
        [SMEM] + [VMEM] * 5,
        "edge_x",
    )(place, near_noise, doubled, names, even, odd)
    even = permute(even, ("x", "zh"), even_pair)
    odd = permute(odd, ("x", "zh"), odd_pair)
    weights, first, second, third, middle, tables, matrix, rows = call(
        interior_kernel,
        (
            shape(27, X, YP, W),
            shape(3, X, YP, W),
            shape(3, 6, YP, W),
            shape(3, 4, YP, W),
            shape(8, 8, W),
            shape(27, 8, W),
            shape(BLOCKS, SAMPLES, NODES, dtype=jnp.bfloat16),
            shape(2, 2, SAMPLES),
        ),
        [VMEM] * 2 + [HBM] * 4,
        "interior",
        [pltpu.VMEM((8, 27), F32), pltpu.SemaphoreType.DMA((4,))],
    )(field, kinds, table, obs_matrix, drill_data, obs_gain)
    smooth, payload, lists = call(
        finish_kernel,
        (shape(32, 8, W), shape(ROWS, SAMPLES), shape(8, W)),
        [SMEM] * 4 + [VMEM] * 12,
        "finish",
        [
            pltpu.VMEM((6, YP, W), F32),
            pltpu.VMEM((4, YP, W), F32),
            pltpu.VMEM((27, 4, YP, W), F32),
            pltpu.VMEM((3, 6, YP, W), F32),
            pltpu.VMEM((3, 6, YP, W), F32),
            pltpu.VMEM((3, 6, YP, W), F32),
            pltpu.VMEM((64, W), F32),
        ],
    )(
        place, node_block, sample_count, sample_block, kinds, even, odd, lists,
        weights, first, second, third, middle, tables, matrix, rows,
    )
    here = lax.all_to_all(
        jnp.broadcast_to(payload[None], (16, ROWS, SAMPLES)), ("x", "y"), 0, 0, tiled=True
    )
    keep, send = call(
        collect_kernel, (shape(2, 32, SAMPLES), shape(2, 32, SAMPLES)), [SMEM, VMEM, VMEM], "collect"
    )(place, lists, here)
    near = permute(send, ("core",), lambda c: (c ^ 1,))
    far = permute(keep[1] + near[1], ("zh",), lambda z: (z ^ 1,))
    out, misfit = call(
        update_kernel,
        (shape(32, 8, W), shape(2, 2, SAMPLES)),
        [SMEM] * 2 + [VMEM] * 6,
        "update",
        [pltpu.VMEM((64, W), F32)],
    )(node_block, sample_count, keep, near, far, smooth, matrix, rows)
    return out.reshape(X, Y, W), misfit


def solution(mesh):
    fine = Mesh(
        mesh.devices.reshape(4, 4, 2, 4, 2), ("real", "x", "zh", "y", "core")
    )
    sx, sy = ("x", "zh"), ("y", "core")
    both = sx + sy
    in_specs = (
        P(sx, sy, "real"),
        P(sx, sy, None),
        P(),
        P(both, None, None),
        P(both),
        P(both),
        P(both),
        P(both, None),
        P(both, None),
    )
    out_specs = (P(sx, sy, "real"), P(both, "real", None))
    return jax.shard_map(shards, mesh=fine, in_specs=in_specs, out_specs=out_specs, check_vma=False)
```

```python
import itertools

import jax
import jax.numpy as jnp
from jax import lax
from jax.experimental import pallas as pl
from jax.experimental.pallas import tpu as pltpu
from jax.sharding import Mesh, PartitionSpec as P

CHEB = (0.6, 0.5, 0.3, 0.2)
X, Y, Z = 8, 32, 64
W = 2 * Z
YP = 40
OFF = 4
BLOCKS = 8
SAMPLES = 256
NODES = 512
ROWS = 24
F32 = jnp.float32
VMEM = pl.BlockSpec(memory_space=pltpu.VMEM)
SMEM = pl.BlockSpec(memory_space=pltpu.SMEM)
HBM = pl.BlockSpec(memory_space=pltpu.HBM)
SIZES = {"x": 4, "zh": 2, "y": 4, "core": 2}


def permute(value, axes, target):
    dims = [SIZES[a] for a in axes]

    def flat(place):
        number = 0
        for coordinate, size in zip(place, dims):
            number = number * size + coordinate
        return number

    pairs = []
    for place in itertools.product(*[range(d) for d in dims]):
        other = target(*place)
        if other is not None:
            pairs.append((flat(place), flat(other)))
    return lax.ppermute(value, axes if len(axes) > 1 else axes[0], pairs)


def even_pair(a, b):
    return (a, b ^ 1)


def odd_pair(a, b):
    if b == 1:
        return (a + 1, 0) if a < 3 else None
    return (a - 1, 1) if a > 0 else None


def half_lanes(shape):
    return lax.broadcasted_iota(jnp.int32, shape, len(shape) - 1) < Z


def swap_halves(value):
    return pltpu.roll(value, Z, axis=value.ndim - 1)


def pack(first, second):
    return jnp.where(half_lanes(first.shape), first, second)


def unpack(row):
    low = half_lanes(row.shape)
    other = swap_halves(row)
    return jnp.where(low, row, other), jnp.where(low, other, row)


def edge_y_kernel(
    place, noise_far, classes_far, owner_far,
    even, odd, noise, doubled, names,
    classes, owner, sems,
):
    copies = [
        pltpu.make_async_copy(noise_far, noise, sems.at[0]),
        pltpu.make_async_copy(classes_far, classes, sems.at[1]),
        pltpu.make_async_copy(owner_far, owner, sems.at[2]),
    ]
    for copy in copies:
        copy.start()
    for copy in copies:
        copy.wait()
    kinds = (classes[...] + 1).astype(F32)
    doubled[...] = jnp.concatenate([kinds, kinds], axis=-1)
    core = place[1]
    lane = lax.broadcasted_iota(jnp.int32, (8, W), 1)
    own = jnp.zeros((8, W), F32)
    for b in range(BLOCKS):
        own = jnp.where(lane == b, (owner[b] + 1).astype(F32), own)
    names[...] = own
    even[X] = own[0:4]

    def low(out):
        out[0:X, 0:3, :] = noise[:, 0:3, :]
        out[0:X, 3:4, :] = pack(doubled[:, 0:1, :], doubled[:, 1:2, :])

    def high(out):
        out[0:X, 0:3, :] = noise[:, Y - 3 : Y, :]
        out[0:X, 3:4, :] = pack(doubled[:, Y - 2 : Y - 1, :], doubled[:, Y - 1 : Y, :])

    @pl.when(core == 0)
    def _():
        high(even)
        low(odd)

    @pl.when(core == 1)
    def _():
        low(even)
        high(odd)


def edge_x_kernel(
    place, noise, doubled, names, even_in, odd_in,
    field, kinds, odd, even, lists,
    true_field, true_kinds,
):
    core, half = place[1], place[0]
    for out in (true_field, true_kinds):
        out[:, 0:8, :] = jnp.zeros((X, 8, W), F32)
        out[:, 32:40, :] = jnp.zeros((X, 8, W), F32)
    true_field[:, OFF : OFF + Y, :] = noise[...]
    true_kinds[:, OFF : OFF + Y, :] = doubled[...]
    lists[0:4] = names[0:4]
    lists[1:2] = even_in[X, 0:1, :]

    def sides(low, high):
        true_field[:, 1:4, :] = low[0:X, 0:3, :]
        first, second = unpack(low[0:X, 3:4, :])
        true_kinds[:, 2:3, :] = first
        true_kinds[:, 3:4, :] = second
        true_field[:, 36:39, :] = high[0:X, 0:3, :]
        first, second = unpack(high[0:X, 3:4, :])
        true_kinds[:, 36:37, :] = first
        true_kinds[:, 37:38, :] = second

    @pl.when(core == 0)
    def _():
        sides(odd_in, even_in)

    @pl.when(core == 1)
    def _():
        sides(even_in, odd_in)

    for x in range(X):
        true = mirrored(x, half)
        field[x] = true_field[true]
        kinds[x] = true_kinds[true]
    for n in range(3):
        even[n] = field[X - 1 - n]
        odd[n] = field[n]
    even[3] = pack(kinds[X - 1], kinds[X - 2])
    odd[3] = pack(kinds[0], kinds[1])
    even[3, 0:1, :] = lists[0:1]
    even[3, YP - 1 : YP, :] = lists[1:2]


def mirrored(x, half):
    return x + half * (X - 1 - 2 * x)


def rows_by_column(block_rows):
    return [block_rows[pl.ds(c, 8, stride=8), :] for c in range(8)]


def split(value):
    high = value.astype(jnp.bfloat16)
    low = (value - high.astype(F32)).astype(jnp.bfloat16)
    return high, low


def weigh(kinds, table, put):
    for b in range(3):
        moved = kinds if b == 1 else pltpu.roll(kinds, (b - 1) % YP, axis=0)
        index = jnp.maximum(moved.astype(jnp.int32) - 1, 0)
        for g in range(YP // 8):
            part = index[8 * g : 8 * g + 8]
            for a in range(3):
                for c in range(3):
                    o = 9 * a + 3 * b + c
                    put(
                        o,
                        pl.ds(8 * g, 8),
                        jnp.take_along_axis(table[o], part, axis=0, mode="promise_in_bounds"),
                    )


def spread_table(table, half, out):
    held = table[...]
    columns = [jnp.broadcast_to(held[:, o : o + 1], (8, W)) for o in range(27)]
    for o in range(27):
        out[o] = jnp.where(half == 0, columns[o], columns[o + 9 * (2 - 2 * (o // 9))])


def lean(row):
    lanes = lax.broadcasted_iota(jnp.int32, (YP, W), 1) % Z
    below = jnp.where(lanes > 0, pltpu.roll(row, 1, axis=1), 0.0)
    above = jnp.where(lanes < Z - 1, pltpu.roll(row, W - 1, axis=1), 0.0)
    return below, row, above


def operate(weight, moved, inside):
    sums = []
    for b in range(3):
        total = None
        for a in range(3):
            for c in range(3):
                term = weight(9 * a + 3 * b + c) * moved(a, c)
                total = term if total is None else total + term
        sums.append(total)
    result = pltpu.roll(sums[0], 1, axis=0) + sums[1] + pltpu.roll(sums[2], YP - 1, axis=0)
    return result * inside


def interior_kernel(
    place, field, kinds, table, matrix, drill, gain,
    weights, first, second, third, smooth, tables, held_matrix, held_rows,
    held_table, sems,
):
    copies = [
        pltpu.make_async_copy(matrix, held_matrix, sems.at[0]),
        pltpu.make_async_copy(drill, held_rows.at[0], sems.at[1]),
        pltpu.make_async_copy(gain, held_rows.at[1], sems.at[2]),
        pltpu.make_async_copy(table, held_table, sems.at[3]),
    ]
    for copy in reversed(copies):
        copy.start()
    copies[3].wait()
    spread_table(held_table, place[0], tables)
    for x in range(X):
        def put(o, rows, value, x=x):
            weights[o, x, rows, :] = value

        weigh(kinds[x], tables, put)
        for c, value in enumerate(lean(field[x])):
            first[c, x] = value

    def step(source, start, x):
        return operate(
            lambda o: weights[o, x],
            lambda a, c: source[c, x + a - 1 - start],
            jnp.minimum(kinds[x], 1.0),
        )

    for x in range(1, 7):
        for c, value in enumerate(lean(step(first, 0, x))):
            second[c, x - 1] = value
    for x in range(2, 6):
        value = 2.0 * step(second, 1, x) - first[1, x]
        for c, value in enumerate(lean(value)):
            third[c, x - 2] = value
    for x in range(3, 5):
        fourth = 2.0 * step(third, 2, x) - second[1, x - 1]
        result = (
            CHEB[0] * first[1, x] + CHEB[1] * second[1, x - 1] + CHEB[2] * third[1, x - 2] + CHEB[3] * fourth
        )
        for g in range(4):
            smooth[4 * (x - 3) + g] = result[OFF + 8 * g : OFF + 8 * g + 8]
    for copy in copies[:3]:
        copy.wait()


def fill_halo(message, tables, halo_kinds, halo_weights, halo_first):
    one, two = unpack(message[3])
    halo_kinds[0], halo_kinds[1] = one, two
    halo_kinds[:, 0:1, :] = jnp.zeros((2, 1, W), F32)
    halo_kinds[:, YP - 1 : YP, :] = jnp.zeros((2, 1, W), F32)
    for i in range(2):
        def put(o, part, value, i=i):
            halo_weights[o, i, part, :] = value

        weigh(halo_kinds[i], tables, put)
    for i in range(3):
        for c, value in enumerate(lean(message[i])):
            halo_first[c, i] = value


def side(
    high, kinds, weights, first, second, third, halo_kinds, halo_weights, halo_first, edge_second, edge_third, put
):
    def beyond(x):
        return x - X if high else -1 - x

    def weight(x):
        if 0 <= x < X:
            return (lambda o: weights[o, x]), jnp.minimum(kinds[x], 1.0)
        i = beyond(x)
        return (lambda o: halo_weights[o, i]), jnp.minimum(halo_kinds[i], 1.0)

    def at_first(x, c):
        return first[c, x] if 0 <= x < X else halo_first[c, beyond(x)]

    def at_second(x, c):
        return second[c, x - 1] if 1 <= x < 7 else edge_second[c, beyond(x) + 1]

    def at_third(x, c):
        return third[c, x - 2] if 2 <= x < 6 else edge_third[c, beyond(x) + 2]

    def step(at, x):
        of, inside = weight(x)
        return operate(of, lambda a, c: at(x + a - 1, c), inside)

    def row(n):
        return X - 1 - n if high else n

    for n in (-2, -1, 0):
        for c, value in enumerate(lean(step(at_first, row(n)))):
            edge_second[c, -n] = value
    for n in (-1, 0, 1):
        value = 2.0 * step(at_second, row(n)) - at_first(row(n), 1)
        for c, value in enumerate(lean(value)):
            edge_third[c, 1 - n] = value
    for n in (0, 1, 2):
        x = row(n)
        fourth = 2.0 * step(at_third, x) - at_second(x, 1)
        result = (
            CHEB[0] * at_first(x, 1) + CHEB[1] * at_second(x, 1) + CHEB[2] * at_third(x, 1) + CHEB[3] * fourth
        )
        for g in range(4):
            put(x, g, result[OFF + 8 * g : OFF + 8 * g + 8])


def lower_kernel(
    kinds, edges, weights, first, second, third, tables,
    lower,
    halo_kinds, halo_weights, halo_first, edge_second, edge_third,
):
    fill_halo(edges, tables, halo_kinds, halo_weights, halo_first)

    def put(x, g, value):
        lower[4 * x + g] = value

    side(
        False, kinds, weights, first, second, third,
        halo_kinds, halo_weights, halo_first, edge_second, edge_third, put,
    )


def finish_kernel(
    place, node_block, count, owner, kinds, edges, near,
    weights, first, second, third, middle, lower, tables, matrix, rows,
    smooth, payload, lists,
    halo_kinds, halo_weights, halo_first, edge_second, edge_third, chosen,
):
    half = place[0]
    lists[0:4] = near[0:4]
    lists[4:8] = jnp.zeros((4, W), F32)
    lists[2:3] = edges[3, 0:1, :]
    lists[3:4] = edges[3, YP - 1 : YP, :]
    fill_halo(edges, tables, halo_kinds, halo_weights, halo_first)

    def put(x, g, value):
        smooth[4 * mirrored(x, half) + g] = value

    side(
        True, kinds, weights, first, second, third,
        halo_kinds, halo_weights, halo_first, edge_second, edge_third, put,
    )
    for g in range(4):
        for x in (0, 1, 2):
            put(x, g, lower[4 * x + g])
        for x in (3, 4):
            put(x, g, middle[4 * (x - 3) + g])

    for b in range(BLOCKS):
        chosen[pl.ds(8 * b, 8), :] = smooth[node_block[b]]
    columns = rows_by_column(chosen)
    low = half_lanes((8, W))
    parts = ([], [])
    for j in range(4):
        one, two = columns[2 * j], columns[2 * j + 1]
        parts[0].append(jnp.where(low, one, swap_halves(two)))
        parts[1].append(jnp.where(low, swap_halves(one), two))
    values = [jnp.concatenate(p, axis=1) for p in parts]
    pieces = [split(v) for v in values]
    left = jnp.concatenate([pieces[0][0], pieces[1][0], pieces[0][1], pieces[1][1]], axis=0)
    block = lax.broadcasted_iota(jnp.int32, (BLOCKS, SAMPLES), 0)
    sums = [jnp.zeros((BLOCKS, SAMPLES), F32) for _ in range(2)]
    for b in range(BLOCKS):
        product = lax.dot_general(
            left, matrix[b], (((1,), (1,)), ((), ())), preferred_element_type=F32
        )
        for r in range(2):
            both = product[8 * r : 8 * r + 8] + product[16 + 8 * r : 24 + 8 * r]
            sums[r] = jnp.where(block == b, both, sums[r])
    live = is_live(count)
    for r in range(2):
        payload[8 * r : 8 * r + 8, :] = jnp.where(live, sums[r], 0.0)
    payload[16:24, :] = jnp.zeros((8, SAMPLES), F32)
    for k in range(2):
        for h in range(2):
            for kind in range(2):
                row = 16 + 4 * kind + 2 * k + h
                payload[row : row + 1, 0:W] = rows[kind, k : k + 1, h * W : h * W + W]
    lane = lax.broadcasted_iota(jnp.int32, (8, W), 1)
    names = jnp.zeros((8, W), F32)
    for b in range(BLOCKS):
        names = jnp.where(lane == 8 * place[2] + b, (owner[b] + 1).astype(F32), names)
    payload[16:17, W : 2 * W] = names[0:1]


def is_live(count):
    block = lax.broadcasted_iota(jnp.int32, (BLOCKS, SAMPLES), 0)
    limit = jnp.zeros((BLOCKS, SAMPLES), jnp.int32)
    for b in range(BLOCKS):
        limit = jnp.where(block == b, count[b], limit)
    return lax.broadcasted_iota(jnp.int32, (BLOCKS, SAMPLES), 1) < limit


def collect_kernel(place, lists, here, keep, send):
    names = here[0, 16:24, W : 2 * W]
    for n in range(1, 16):
        names = names + here[n, 16:24, W : 2 * W]
    names = jnp.broadcast_to(names[0:1], (8, W))
    lane = lax.broadcasted_iota(jnp.int32, (8, W), 1)
    row = lax.broadcasted_iota(jnp.int32, (8, W), 0)
    hits, spots = [], []
    for member in range(4):
        tile = place[4] ^ (1 if member & 1 else 0) ^ (8 if member & 2 else 0)
        held = jnp.broadcast_to(lists[member : member + 1], (8, W))
        name = jnp.sum(jnp.where(lane == row, held, 0.0), axis=1, keepdims=True)
        name = jnp.broadcast_to(name, (8, W))
        hits.append(name == names)
        hits.append((2 * tile + 1 + (row & 1)).astype(F32) == names)
        block = name.astype(jnp.int32) - 1
        holder = block >> 1
        spot = ((holder >> 4) * 4 + ((holder >> 1) & 3)) * 8 + 2 * (block & 1)
        mine = ((holder & 1) == place[1]) & (((holder >> 3) & 1) == place[0])
        spots.append(jnp.where(mine, spot, -1024))
    hit = jnp.concatenate([h.astype(F32) for h in hits], axis=0).astype(jnp.bfloat16)
    spots = jnp.concatenate(spots, axis=0)
    lane = lax.broadcasted_iota(jnp.int32, (32, W), 1)
    choose = jnp.concatenate(
        [(lane == spots + 4 * kind + h).astype(F32) for kind in range(2) for h in range(2)], axis=0
    ).astype(jnp.bfloat16)

    def gather(left, rows, lanes):
        data = jnp.concatenate([here[n, rows, lanes] for n in range(16)], axis=0)
        high, low = split(data)
        return jnp.dot(left, high, preferred_element_type=F32) + jnp.dot(
            left, low, preferred_element_type=F32
        )

    totals = [gather(hit, slice(8 * r, 8 * r + 8), slice(0, 2 * W)) for r in range(2)]
    found = gather(choose, slice(16, 24), slice(0, W))
    row = lax.broadcasted_iota(jnp.int32, (8, SAMPLES), 0)
    for member in range(4):
        out = (send if member & 1 else keep).at[member // 2]
        drill, gain = [
            jnp.concatenate(
                [found[64 * kind + 32 * h + 8 * member : 64 * kind + 32 * h + 8 * member + 8] for h in range(2)],
                axis=1,
            )
            for kind in range(2)
        ]
        for r in range(2):
            out[8 * r : 8 * r + 8, :] = drill - totals[r][16 * member : 16 * member + 8]
        out[16:24, :] = gain
        own = [totals[r][16 * member + 8 : 16 * member + 16] for r in range(2)]
        out[24:32, :] = jnp.where(row < 2, own[0], own[1])


def update_kernel(
    node_block, count, keep, near, far, smooth, matrix, rows,
    out, misfit,
    update,
):
    sums = keep[0] + near[0] + far[...]
    for k in range(2):
        for r in range(2):
            t = 24 + 2 * r + k
            misfit[k, r : r + 1, :] = rows[0, k : k + 1, :] - sums[t : t + 1, :]
    live = is_live(count)
    picked = [jnp.where(live, sums[16:24] * sums[8 * r : 8 * r + 8], 0.0) for r in range(2)]
    pieces = [split(v) for v in picked]
    left = jnp.concatenate([pieces[0][0], pieces[1][0], pieces[0][1], pieces[1][1]], axis=0)
    block = lax.broadcasted_iota(jnp.int32, (BLOCKS, NODES), 0)
    sums = [jnp.zeros((BLOCKS, NODES), F32) for _ in range(2)]
    for b in range(BLOCKS):
        product = jnp.dot(left, matrix[b], preferred_element_type=F32)
        for r in range(2):
            both = product[8 * r : 8 * r + 8] + product[16 + 8 * r : 24 + 8 * r]
            sums[r] = jnp.where(block == b, both, sums[r])
    low = half_lanes((8, W))
    for j in range(4):
        one, two = sums[0][:, j * W : j * W + W], sums[1][:, j * W : j * W + W]
        update[pl.ds(2 * j, 8, stride=8), :] = jnp.where(low, one, swap_halves(two))
        update[pl.ds(2 * j + 1, 8, stride=8), :] = jnp.where(low, swap_halves(one), two)
    out[...] = smooth[...]
    for b in range(BLOCKS):
        n = node_block[b]
        out[n] = out[n] + update[8 * b : 8 * b + 8, :]


def shape(*dims, dtype=F32):
    return jax.ShapeDtypeStruct(dims, dtype)


def call(kernel, outs, ins, name, scratch=()):
    return pl.pallas_call(
        kernel,
        out_shape=outs,
        in_specs=ins,
        out_specs=(VMEM,) * len(outs),
        scratch_shapes=scratch,
        compiler_params=pltpu.CompilerParams(vmem_limit_bytes=24 * 1024 * 1024),
        name=name,
    )


def shards(
    noise, classes, table, obs_matrix, node_block, sample_block, sample_count, drill_data, obs_gain
):
    place = jnp.stack(
        [
            lax.axis_index("zh"),
            lax.axis_index("core"),
            lax.axis_index(("x", "y")),
            lax.axis_index(("x", "y")),
            lax.axis_index(("x", "zh", "y", "core")),
        ]
    ).astype(jnp.int32)
    noise, classes, table, obs_matrix, owner, drill_data, obs_gain = [
        pltpu.with_memory_space_constraint(a, pltpu.HBM)
        for a in (noise, classes, table, obs_matrix, sample_block, drill_data, obs_gain)
    ]

    even, odd, near_noise, doubled, names = call(
        edge_y_kernel,
        (shape(X + 1, 4, W), shape(X, 4, W), shape(X, Y, W), shape(X, Y, W), shape(8, W)),
        [SMEM, HBM, HBM, HBM],
        "edge_y",
        [
            pltpu.VMEM((X, Y, Z), jnp.int32),
            pltpu.SMEM((BLOCKS,), jnp.int32),
            pltpu.SemaphoreType.DMA((3,)),
        ],
    )(place, noise, classes, owner)
    even = permute(even, ("y", "core"), even_pair)
    odd = permute(odd, ("y", "core"), odd_pair)
    field, kinds, odd, even, lists = call(
        edge_x_kernel,
        (shape(X, YP, W), shape(X, YP, W), shape(4, YP, W), shape(4, YP, W), shape(4, W)),
        [SMEM] + [VMEM] * 5,
        "edge_x",
        [pltpu.VMEM((X, YP, W), F32), pltpu.VMEM((X, YP, W), F32)],
    )(place, near_noise, doubled, names, even, odd)
    odd = permute(odd, ("x", "zh"), odd_pair)
    even = permute(even, ("x", "zh"), even_pair)
    weights, first, second, third, middle, tables, matrix, rows = call(
        interior_kernel,
        (
            shape(27, X, YP, W),
            shape(3, X, YP, W),
            shape(3, 6, YP, W),
            shape(3, 4, YP, W),
            shape(8, 8, W),
            shape(27, 8, W),
            shape(BLOCKS, SAMPLES, NODES, dtype=jnp.bfloat16),
            shape(2, 2, SAMPLES),
        ),
        [SMEM] + [VMEM] * 2 + [HBM] * 4,
        "interior",
        [pltpu.VMEM((8, 27), F32), pltpu.SemaphoreType.DMA((4,))],
    )(place, field, kinds, table, obs_matrix, drill_data, obs_gain)
    halo_scratch = [
        pltpu.VMEM((2, YP, W), F32),
        pltpu.VMEM((27, 2, YP, W), F32),
        pltpu.VMEM((3, 3, YP, W), F32),
        pltpu.VMEM((3, 3, YP, W), F32),
        pltpu.VMEM((3, 3, YP, W), F32),
    ]
    (lower,) = call(lower_kernel, (shape(12, 8, W),), [VMEM] * 7, "lower", halo_scratch)(
        kinds, odd, weights, first, second, third, tables
    )
    smooth, payload, lists = call(
        finish_kernel,
        (shape(32, 8, W), shape(ROWS, SAMPLES), shape(8, W)),
        [SMEM] * 4 + [VMEM] * 12,
        "finish",
        halo_scratch + [pltpu.VMEM((64, W), F32)],
    )(
        place, node_block, sample_count, sample_block, kinds, even, lists,
        weights, first, second, third, middle, lower, tables, matrix, rows,
    )
    here = lax.all_to_all(
        jnp.broadcast_to(payload[None], (16, ROWS, SAMPLES)), ("x", "y"), 0, 0, tiled=True
    )
    keep, send = call(
        collect_kernel, (shape(2, 32, SAMPLES), shape(2, 32, SAMPLES)), [SMEM, VMEM, VMEM], "collect"
    )(place, lists, here)
    near = permute(send, ("core",), lambda c: (c ^ 1,))
    far = permute(keep[1] + near[1], ("zh",), lambda z: (z ^ 1,))
    out, misfit = call(
        update_kernel,
        (shape(32, 8, W), shape(2, 2, SAMPLES)),
        [SMEM] * 2 + [VMEM] * 6,
        "update",
        [pltpu.VMEM((64, W), F32)],
    )(node_block, sample_count, keep, near, far, smooth, matrix, rows)
    return out.reshape(X, Y, W), misfit


def solution(mesh):
    fine = Mesh(
        mesh.devices.reshape(4, 4, 2, 4, 2), ("real", "x", "zh", "y", "core")
    )
    sx, sy = ("x", "zh"), ("y", "core")
    both = sx + sy
    in_specs = (
        P(sx, sy, "real"),
        P(sx, sy, None),
        P(),
        P(both, None, None),
        P(both),
        P(both),
        P(both),
        P(both, None),
        P(both, None),
    )
    out_specs = (P(sx, sy, "real"), P(both, "real", None))
    return jax.shard_map(shards, mesh=fine, in_specs=in_specs, out_specs=out_specs, check_vma=False)
```

```python
import itertools

import jax
import jax.numpy as jnp
from jax import lax
from jax.experimental import pallas as pl
from jax.experimental.pallas import tpu as pltpu
from jax.sharding import Mesh, PartitionSpec as P

CHEB = (0.6, 0.5, 0.3, 0.2)
X, Y, Z = 8, 32, 64
W = 2 * Z
YP = 40
OFF = 4
BLOCKS = 8
SAMPLES = 256
NODES = 512
ROWS = 24
F32 = jnp.float32
VMEM = pl.BlockSpec(memory_space=pltpu.VMEM)
HBM = pl.BlockSpec(memory_space=pltpu.HBM)
SIZES = {"x": 4, "zh": 2, "y": 4, "core": 2}


def permute(value, axes, target):
    dims = [SIZES[a] for a in axes]

    def flat(place):
        number = 0
        for coordinate, size in zip(place, dims):
            number = number * size + coordinate
        return number

    pairs = []
    for place in itertools.product(*[range(d) for d in dims]):
        other = target(*place)
        if other is not None:
            pairs.append((flat(place), flat(other)))
    return lax.ppermute(value, axes if len(axes) > 1 else axes[0], pairs)


def even_pair(a, b):
    return (a, b ^ 1)


def odd_pair(a, b):
    return ((a + 1) % 4, 0) if b == 1 else ((a + 3) % 4, 1)


def half_lanes(shape):
    return lax.broadcasted_iota(jnp.int32, shape, len(shape) - 1) < Z


def swap_halves(value):
    return pltpu.roll(value, Z, axis=value.ndim - 1)


def pack(first, second):
    return jnp.where(half_lanes(first.shape), first, second)


def unpack(row):
    low = half_lanes(row.shape)
    other = swap_halves(row)
    return jnp.where(low, row, other), jnp.where(low, other, row)


def whereabouts():
    x, zh, y, core = [lax.axis_index(axis) for axis in ("x", "zh", "y", "core")]
    return zh, core, 4 * x + y, ((x * 2 + zh) * 4 + y) * 2 + core


def has_odd_pair(outer, inner):
    return lax.axis_index(outer) != 3 * lax.axis_index(inner)


def edge_y_kernel(
    noise_far, classes_far, owner_far,
    odd, even, noise, classes, names,
    noise_edges, class_edges, owner, sems,
):
    first = [
        pltpu.make_async_copy(noise_far.at[:, 0:8, :], noise_edges.at[0], sems.at[0]),
        pltpu.make_async_copy(noise_far.at[:, Y - 8 : Y, :], noise_edges.at[1], sems.at[1]),
        pltpu.make_async_copy(classes_far.at[:, 0:8, :], class_edges.at[0], sems.at[2]),
        pltpu.make_async_copy(classes_far.at[:, Y - 8 : Y, :], class_edges.at[1], sems.at[3]),
        pltpu.make_async_copy(owner_far, owner, sems.at[4]),
    ]
    rest = [
        pltpu.make_async_copy(noise_far, noise, sems.at[5]),
        pltpu.make_async_copy(classes_far, classes, sems.at[6]),
    ]
    for copy in first + rest:
        copy.start()
    for copy in first:
        copy.wait()
    core = whereabouts()[1]
    lane = lax.broadcasted_iota(jnp.int32, (8, W), 1)
    own = jnp.zeros((8, W), F32)
    for b in range(BLOCKS):
        own = jnp.where(lane == b, (owner[b] + 1).astype(F32), own)
    names[...] = own
    odd[X] = own[0:4]
    even[X] = own[0:4]

    def message(out, end, start, one, two):
        out[0:X, 0:3, :] = noise_edges[end, :, start : start + 3, :]
        kinds = (class_edges[end] + 1).astype(F32)
        out[0:X, 3:4, :] = jnp.concatenate([kinds[:, one : one + 1], kinds[:, two : two + 1]], axis=-1)

    @pl.when(core == 0)
    def _():
        message(even, 1, 5, 6, 7)
        message(odd, 0, 0, 0, 1)

    @pl.when(core == 1)
    def _():
        message(even, 0, 0, 0, 1)
        message(odd, 1, 5, 6, 7)

    for copy in rest:
        copy.wait()


def prepare_kernel(noise, classes, field, kinds):
    half = whereabouts()[0]
    for out in (field, kinds):
        out[:, 0:8, :] = jnp.zeros((X, 8, W), F32)
        out[:, 32:40, :] = jnp.zeros((X, 8, W), F32)
    for x in range(X):
        true = mirrored(x, half)
        field[x, OFF : OFF + Y, :] = noise[true]
        kind = (classes[true] + 1).astype(F32)
        kinds[x, OFF : OFF + Y, :] = jnp.concatenate([kind, kind], axis=-1)


def edge_x_kernel(
    field_in, kinds_in, names, even_in, odd_in,
    field, kinds, odd, even, lists,
):
    half, core = whereabouts()[0:2]
    field[...] = field_in[...]
    kinds[...] = kinds_in[...]
    lists[0:4] = names[0:4]
    lists[1:2] = even_in[X, 0:1, :]

    inside = has_odd_pair("y", "core")

    def sides(low, high):
        for x in range(X):
            true = mirrored(x, half)
            for message, start, one in ((low, 1, 2), (high, 36, 36)):
                held = message[true]
                if message is odd_in:
                    held = jnp.where(inside, held, 0.0)
                field[x, start : start + 3, :] = held[0:3]
                first, second = unpack(held[3:4])
                kinds[x, one : one + 1, :] = first
                kinds[x, one + 1 : one + 2, :] = second

    @pl.when(core == 0)
    def _():
        sides(odd_in, even_in)

    @pl.when(core == 1)
    def _():
        sides(even_in, odd_in)

    for n in range(3):
        odd[n] = field[n]
        even[n] = field[X - 1 - n]
    odd[3] = pack(kinds[0], kinds[1])
    even[3] = pack(kinds[X - 1], kinds[X - 2])
    even[3, 0:1, :] = lists[0:1]
    even[3, YP - 1 : YP, :] = lists[1:2]


def mirrored(x, half):
    return x + half * (X - 1 - 2 * x)


def rows_by_column(block_rows):
    return [block_rows[pl.ds(c, 8, stride=8), :] for c in range(8)]


def split(value):
    high = value.astype(jnp.bfloat16)
    low = (value - high.astype(F32)).astype(jnp.bfloat16)
    return high, low


def weigh(kinds, table, put):
    for b in range(3):
        moved = kinds if b == 1 else pltpu.roll(kinds, (b - 1) % YP, axis=0)
        index = jnp.maximum(moved.astype(jnp.int32) - 1, 0)
        for g in range(YP // 8):
            part = index[8 * g : 8 * g + 8]
            for a in range(3):
                for c in range(3):
                    o = 9 * a + 3 * b + c
                    put(
                        o,
                        pl.ds(8 * g, 8),
                        jnp.take_along_axis(table[o], part, axis=0, mode="promise_in_bounds"),
                    )


def spread_table(table, half, out):
    held = table[...]
    columns = [jnp.broadcast_to(held[:, o : o + 1], (8, W)) for o in range(27)]
    for o in range(27):
        out[o] = jnp.where(half == 0, columns[o], columns[o + 9 * (2 - 2 * (o // 9))])


def lean(row):
    lanes = lax.broadcasted_iota(jnp.int32, (YP, W), 1) % Z
    below = jnp.where(lanes > 0, pltpu.roll(row, 1, axis=1), 0.0)
    above = jnp.where(lanes < Z - 1, pltpu.roll(row, W - 1, axis=1), 0.0)
    return below, row, above


def operate(weight, moved, inside):
    sums = []
    for b in range(3):
        total = None
        for a in range(3):
            for c in range(3):
                term = weight(9 * a + 3 * b + c) * moved(a, c)
                total = term if total is None else total + term
        sums.append(total)
    result = pltpu.roll(sums[0], 1, axis=0) + sums[1] + pltpu.roll(sums[2], YP - 1, axis=0)
    return result * inside


def interior_kernel(
    field, kinds, table, matrix, drill, gain, node_block, count, owner,
    weights, first, second, third, smooth, tables, held_matrix, held_rows, other, live, blocks,
    held_table, scalars, sems,
):
    copies = [
        pltpu.make_async_copy(matrix, held_matrix, sems.at[0]),
        pltpu.make_async_copy(drill, held_rows.at[0], sems.at[1]),
        pltpu.make_async_copy(gain, held_rows.at[1], sems.at[2]),
        pltpu.make_async_copy(node_block, scalars.at[0], sems.at[4]),
        pltpu.make_async_copy(count, scalars.at[1], sems.at[5]),
        pltpu.make_async_copy(owner, scalars.at[2], sems.at[6]),
        pltpu.make_async_copy(table, held_table, sems.at[3]),
    ]
    for copy in reversed(copies):
        copy.start()
    copies[-1].wait()
    half, _, plane, _ = whereabouts()
    spread_table(held_table, half, tables)
    for x in range(X):
        def put(o, rows, value, x=x):
            weights[o, x, rows, :] = value

        weigh(kinds[x], tables, put)
        for c, value in enumerate(lean(field[x])):
            first[c, x] = value

    def step(source, start, x):
        return operate(
            lambda o: weights[o, x],
            lambda a, c: source[c, x + a - 1 - start],
            jnp.minimum(kinds[x], 1.0),
        )

    for x in range(1, 7):
        for c, value in enumerate(lean(step(first, 0, x))):
            second[c, x - 1] = value
    for x in range(2, 6):
        value = 2.0 * step(second, 1, x) - first[1, x]
        for c, value in enumerate(lean(value)):
            third[c, x - 2] = value
    for x in range(3, 5):
        fourth = 2.0 * step(third, 2, x) - second[1, x - 1]
        result = (
            CHEB[0] * first[1, x] + CHEB[1] * second[1, x - 1] + CHEB[2] * third[1, x - 2] + CHEB[3] * fourth
        )
        for g in range(4):
            smooth[4 * (x - 3) + g] = result[OFF + 8 * g : OFF + 8 * g + 8]
    for copy in copies[:-1]:
        copy.wait()
    other[...] = jnp.zeros((8, SAMPLES), F32)
    for k in range(2):
        for h in range(2):
            for kind in range(2):
                row = 4 * kind + 2 * k + h
                other[row : row + 1, 0:W] = held_rows[kind, k : k + 1, h * W : h * W + W]
    lane = lax.broadcasted_iota(jnp.int32, (8, W), 1)
    names = jnp.zeros((8, W), F32)
    places = jnp.zeros((8, W), jnp.int32)
    limit = jnp.zeros((BLOCKS, SAMPLES), jnp.int32)
    block = lax.broadcasted_iota(jnp.int32, (BLOCKS, SAMPLES), 0)
    for b in range(BLOCKS):
        names = jnp.where(lane == 8 * plane + b, (scalars[2, b] + 1).astype(F32), names)
        places = jnp.where(lane == b, scalars[0, b], places)
        limit = jnp.where(block == b, scalars[1, b], limit)
    other[0:1, W : 2 * W] = names[0:1]
    blocks[...] = places
    sample = lax.broadcasted_iota(jnp.int32, (BLOCKS, SAMPLES), 1)
    live[...] = (sample < limit).astype(F32)


def fill_halo(message, inside, tables, halo_kinds, halo_weights, halo_first):
    one, two = unpack(jnp.where(inside, message[3], 0.0))
    halo_kinds[0], halo_kinds[1] = one, two
    halo_kinds[:, 0:1, :] = jnp.zeros((2, 1, W), F32)
    halo_kinds[:, YP - 1 : YP, :] = jnp.zeros((2, 1, W), F32)
    for i in range(2):
        def put(o, part, value, i=i):
            halo_weights[o, i, part, :] = value

        weigh(halo_kinds[i], tables, put)
    for i in range(3):
        for c, value in enumerate(lean(jnp.where(inside, message[i], 0.0))):
            halo_first[c, i] = value


def side(
    high, kinds, weights, first, second, third, halo_kinds, halo_weights, halo_first, edge_second, edge_third, put
):
    def beyond(x):
        return x - X if high else -1 - x

    def weight(x):
        if 0 <= x < X:
            return (lambda o: weights[o, x]), jnp.minimum(kinds[x], 1.0)
        i = beyond(x)
        return (lambda o: halo_weights[o, i]), jnp.minimum(halo_kinds[i], 1.0)

    def at_first(x, c):
        return first[c, x] if 0 <= x < X else halo_first[c, beyond(x)]

    def at_second(x, c):
        return second[c, x - 1] if 1 <= x < 7 else edge_second[c, beyond(x) + 1]

    def at_third(x, c):
        return third[c, x - 2] if 2 <= x < 6 else edge_third[c, beyond(x) + 2]

    def step(at, x):
        of, inside = weight(x)
        return operate(of, lambda a, c: at(x + a - 1, c), inside)

    def row(n):
        return X - 1 - n if high else n

    for n in (-2, -1, 0):
        for c, value in enumerate(lean(step(at_first, row(n)))):
            edge_second[c, -n] = value
    for n in (-1, 0, 1):
        value = 2.0 * step(at_second, row(n)) - at_first(row(n), 1)
        for c, value in enumerate(lean(value)):
            edge_third[c, 1 - n] = value
    for n in (0, 1, 2):
        x = row(n)
        fourth = 2.0 * step(at_third, x) - at_second(x, 1)
        result = (
            CHEB[0] * at_first(x, 1) + CHEB[1] * at_second(x, 1) + CHEB[2] * at_third(x, 1) + CHEB[3] * fourth
        )
        for g in range(4):
            put(x, g, result[OFF + 8 * g : OFF + 8 * g + 8])


def lower_kernel(
    kinds, edges, weights, first, second, third, tables,
    lower,
    halo_kinds, halo_weights, halo_first, edge_second, edge_third,
):
    fill_halo(edges, has_odd_pair("x", "zh"), tables, halo_kinds, halo_weights, halo_first)

    def put(x, g, value):
        lower[4 * x + g] = value

    side(
        False, kinds, weights, first, second, third,
        halo_kinds, halo_weights, halo_first, edge_second, edge_third, put,
    )


def finish_kernel(
    kinds, edges, near, weights, first, second, third, middle, lower, tables, matrix, other, live, blocks,
    smooth, payload, lists,
    halo_kinds, halo_weights, halo_first, edge_second, edge_third, chosen, node_block, sem,
):
    copy = pltpu.make_async_copy(blocks.at[0:1], node_block, sem)
    copy.start()
    half = whereabouts()[0]
    lists[0:4] = near[0:4]
    lists[4:8] = jnp.zeros((4, W), F32)
    lists[2:3] = edges[3, 0:1, :]
    lists[3:4] = edges[3, YP - 1 : YP, :]
    fill_halo(edges, True, tables, halo_kinds, halo_weights, halo_first)

    def put(x, g, value):
        smooth[4 * mirrored(x, half) + g] = value

    side(
        True, kinds, weights, first, second, third,
        halo_kinds, halo_weights, halo_first, edge_second, edge_third, put,
    )
    for g in range(4):
        for x in (0, 1, 2):
            put(x, g, lower[4 * x + g])
        for x in (3, 4):
            put(x, g, middle[4 * (x - 3) + g])

    copy.wait()
    for b in range(BLOCKS):
        chosen[pl.ds(8 * b, 8), :] = smooth[node_block[0, b]]
    columns = rows_by_column(chosen)
    low = half_lanes((8, W))
    parts = ([], [])
    for j in range(4):
        one, two = columns[2 * j], columns[2 * j + 1]
        parts[0].append(jnp.where(low, one, swap_halves(two)))
        parts[1].append(jnp.where(low, swap_halves(one), two))
    values = [jnp.concatenate(p, axis=1) for p in parts]
    pieces = [split(v) for v in values]
    left = jnp.concatenate([pieces[0][0], pieces[1][0], pieces[0][1], pieces[1][1]], axis=0)
    block = lax.broadcasted_iota(jnp.int32, (BLOCKS, SAMPLES), 0)
    sums = [jnp.zeros((BLOCKS, SAMPLES), F32) for _ in range(2)]
    for b in range(BLOCKS):
        product = lax.dot_general(
            left, matrix[b], (((1,), (1,)), ((), ())), preferred_element_type=F32
        )
        for r in range(2):
            both = product[8 * r : 8 * r + 8] + product[16 + 8 * r : 24 + 8 * r]
            sums[r] = jnp.where(block == b, both, sums[r])
    for r in range(2):
        payload[8 * r : 8 * r + 8, :] = jnp.where(live[...] > 0.0, sums[r], 0.0)
    payload[16:24, :] = other[...]


def collect_kernel(lists, here, keep, send):
    names = here[0, 16:24, W : 2 * W]
    for n in range(1, 16):
        names = names + here[n, 16:24, W : 2 * W]
    names = jnp.broadcast_to(names[0:1], (8, W))
    lane = lax.broadcasted_iota(jnp.int32, (8, W), 1)
    row = lax.broadcasted_iota(jnp.int32, (8, W), 0)
    hits, spots = [], []
    half, core, _, me = whereabouts()
    for member in range(4):
        tile = me ^ (1 if member & 1 else 0) ^ (8 if member & 2 else 0)
        held = jnp.broadcast_to(lists[member : member + 1], (8, W))
        name = jnp.sum(jnp.where(lane == row, held, 0.0), axis=1, keepdims=True)
        name = jnp.broadcast_to(name, (8, W))
        hits.append(name == names)
        hits.append((2 * tile + 1 + (row & 1)).astype(F32) == names)
        block = name.astype(jnp.int32) - 1
        holder = block >> 1
        spot = ((holder >> 4) * 4 + ((holder >> 1) & 3)) * 8 + 2 * (block & 1)
        mine = ((holder & 1) == core) & (((holder >> 3) & 1) == half)
        spots.append(jnp.where(mine, spot, -1024))
    hit = jnp.concatenate([h.astype(F32) for h in hits], axis=0).astype(jnp.bfloat16)
    spots = jnp.concatenate(spots, axis=0)
    lane = lax.broadcasted_iota(jnp.int32, (32, W), 1)
    choose = jnp.concatenate(
        [(lane == spots + 4 * kind + h).astype(F32) for kind in range(2) for h in range(2)], axis=0
    ).astype(jnp.bfloat16)

    def gather(left, rows, lanes):
        data = jnp.concatenate([here[n, rows, lanes] for n in range(16)], axis=0)
        high, low = split(data)
        return jnp.dot(left, high, preferred_element_type=F32) + jnp.dot(
            left, low, preferred_element_type=F32
        )

    totals = [gather(hit, slice(8 * r, 8 * r + 8), slice(0, 2 * W)) for r in range(2)]
    found = gather(choose, slice(16, 24), slice(0, W))
    row = lax.broadcasted_iota(jnp.int32, (8, SAMPLES), 0)
    for member in range(4):
        out = (send if member & 1 else keep).at[member // 2]
        drill, gain = [
            jnp.concatenate(
                [found[64 * kind + 32 * h + 8 * member : 64 * kind + 32 * h + 8 * member + 8] for h in range(2)],
                axis=1,
            )
            for kind in range(2)
        ]
        for r in range(2):
            out[8 * r : 8 * r + 8, :] = drill - totals[r][16 * member : 16 * member + 8]
        out[16:24, :] = gain
        own = [totals[r][16 * member + 8 : 16 * member + 16] for r in range(2)]
        out[24:32, :] = jnp.where(row < 2, own[0], own[1])


def update_kernel(
    keep, near, far, smooth, matrix, rows, live, blocks,
    out, misfit,
    update, node_block, sem,
):
    copy = pltpu.make_async_copy(blocks.at[0:1], node_block, sem)
    copy.start()
    sums = keep[0] + near[0] + far[...]
    for k in range(2):
        for r in range(2):
            t = 24 + 2 * r + k
            misfit[k, r : r + 1, :] = rows[0, k : k + 1, :] - sums[t : t + 1, :]
    picked = [jnp.where(live[...] > 0.0, sums[16:24] * sums[8 * r : 8 * r + 8], 0.0) for r in range(2)]
    pieces = [split(v) for v in picked]
    left = jnp.concatenate([pieces[0][0], pieces[1][0], pieces[0][1], pieces[1][1]], axis=0)
    block = lax.broadcasted_iota(jnp.int32, (BLOCKS, NODES), 0)
    sums = [jnp.zeros((BLOCKS, NODES), F32) for _ in range(2)]
    for b in range(BLOCKS):
        product = jnp.dot(left, matrix[b], preferred_element_type=F32)
        for r in range(2):
            both = product[8 * r : 8 * r + 8] + product[16 + 8 * r : 24 + 8 * r]
            sums[r] = jnp.where(block == b, both, sums[r])
    low = half_lanes((8, W))
    for j in range(4):
        one, two = sums[0][:, j * W : j * W + W], sums[1][:, j * W : j * W + W]
        update[pl.ds(2 * j, 8, stride=8), :] = jnp.where(low, one, swap_halves(two))
        update[pl.ds(2 * j + 1, 8, stride=8), :] = jnp.where(low, swap_halves(one), two)
    out[...] = smooth[...]
    copy.wait()
    for b in range(BLOCKS):
        n = node_block[0, b]
        out[n] = out[n] + update[8 * b : 8 * b + 8, :]


def shape(*dims, dtype=F32):
    return jax.ShapeDtypeStruct(dims, dtype)


def call(kernel, outs, ins, name, scratch=()):
    return pl.pallas_call(
        kernel,
        out_shape=outs,
        in_specs=ins,
        out_specs=(VMEM,) * len(outs),
        scratch_shapes=scratch,
        compiler_params=pltpu.CompilerParams(vmem_limit_bytes=24 * 1024 * 1024),
        name=name,
    )


def shards(
    noise, classes, table, obs_matrix, node_block, sample_block, sample_count, drill_data, obs_gain
):
    noise, classes, table, matrix, blocks, owner, count, drill, gain = [
        pltpu.with_memory_space_constraint(a, pltpu.HBM)
        for a in (
            noise, classes, table, obs_matrix, node_block, sample_block, sample_count, drill_data, obs_gain
        )
    ]
    odd, even, near_noise, near_classes, names = call(
        edge_y_kernel,
        (shape(X + 1, 4, W), shape(X + 1, 4, W), shape(X, Y, W), shape(X, Y, Z, dtype=jnp.int32), shape(8, W)),
        [HBM] * 3,
        "edge_y",
        [
            pltpu.VMEM((2, X, 8, W), F32),
            pltpu.VMEM((2, X, 8, Z), jnp.int32),
            pltpu.SMEM((BLOCKS,), jnp.int32),
            pltpu.SemaphoreType.DMA((7,)),
        ],
    )(noise, classes, owner)
    odd = permute(odd, ("y", "core"), odd_pair)
    even = permute(even, ("y", "core"), even_pair)
    field, kinds = call(
        prepare_kernel, (shape(X, YP, W), shape(X, YP, W)), [VMEM] * 2, "prepare"
    )(near_noise, near_classes)
    field, kinds, odd, even, lists = call(
        edge_x_kernel,
        (shape(X, YP, W), shape(X, YP, W), shape(4, YP, W), shape(4, YP, W), shape(4, W)),
        [VMEM] * 5,
        "edge_x",
    )(field, kinds, names, even, odd)
    odd = permute(odd, ("x", "zh"), odd_pair)
    even = permute(even, ("x", "zh"), even_pair)
    weights, first, second, third, middle, tables, matrix, rows, other, live, blocks = call(
        interior_kernel,
        (
            shape(27, X, YP, W),
            shape(3, X, YP, W),
            shape(3, 6, YP, W),
            shape(3, 4, YP, W),
            shape(8, 8, W),
            shape(27, 8, W),
            shape(BLOCKS, SAMPLES, NODES, dtype=jnp.bfloat16),
            shape(2, 2, SAMPLES),
            shape(8, SAMPLES),
            shape(BLOCKS, SAMPLES),
            shape(8, W, dtype=jnp.int32),
        ),
        [VMEM] * 2 + [HBM] * 7,
        "interior",
        [pltpu.VMEM((8, 27), F32), pltpu.SMEM((3, BLOCKS), jnp.int32), pltpu.SemaphoreType.DMA((7,))],
    )(field, kinds, table, matrix, drill, gain, blocks, count, owner)
    halo_scratch = [
        pltpu.VMEM((2, YP, W), F32),
        pltpu.VMEM((27, 2, YP, W), F32),
        pltpu.VMEM((3, 3, YP, W), F32),
        pltpu.VMEM((3, 3, YP, W), F32),
        pltpu.VMEM((3, 3, YP, W), F32),
    ]
    (lower,) = call(lower_kernel, (shape(12, 8, W),), [VMEM] * 7, "lower", halo_scratch)(
        kinds, odd, weights, first, second, third, tables
    )
    index_scratch = [pltpu.SMEM((1, W), jnp.int32), pltpu.SemaphoreType.DMA]
    smooth, payload, lists = call(
        finish_kernel,
        (shape(32, 8, W), shape(ROWS, SAMPLES), shape(8, W)),
        [VMEM] * 14,
        "finish",
        halo_scratch + [pltpu.VMEM((64, W), F32)] + index_scratch,
    )(
        kinds, even, lists, weights, first, second, third, middle, lower, tables, matrix,
        other, live, blocks,
    )
    here = lax.all_to_all(
        jnp.broadcast_to(payload[None], (16, ROWS, SAMPLES)), ("x", "y"), 0, 0, tiled=True
    )
    keep, send = call(
        collect_kernel, (shape(2, 32, SAMPLES), shape(2, 32, SAMPLES)), [VMEM] * 2, "collect"
    )(lists, here)
    near = permute(send, ("core",), lambda c: (c ^ 1,))
    far = permute(keep[1] + near[1], ("zh",), lambda z: (z ^ 1,))
    out, misfit = call(
        update_kernel,
        (shape(32, 8, W), shape(2, 2, SAMPLES)),
        [VMEM] * 8,
        "update",
        [pltpu.VMEM((64, W), F32)] + index_scratch,
    )(keep, near, far, smooth, matrix, rows, live, blocks)
    return out.reshape(X, Y, W), misfit


def solution(mesh):
    fine = Mesh(
        mesh.devices.reshape(4, 4, 2, 4, 2), ("real", "x", "zh", "y", "core")
    )
    sx, sy = ("x", "zh"), ("y", "core")
    both = sx + sy
    in_specs = (
        P(sx, sy, "real"),
        P(sx, sy, None),
        P(),
        P(both, None, None),
        P(both),
        P(both),
        P(both),
        P(both, None),
        P(both, None),
    )
    out_specs = (P(sx, sy, "real"), P(both, "real", None))
    return jax.shard_map(shards, mesh=fine, in_specs=in_specs, out_specs=out_specs, check_vma=False)
```

```python
import itertools

import jax
import jax.numpy as jnp
from jax import lax
from jax.experimental import pallas as pl
from jax.experimental.pallas import tpu as pltpu
from jax.sharding import Mesh, PartitionSpec as P

CHEB = (0.6, 0.5, 0.3, 0.2)
X, Y, Z = 8, 32, 64
W = 2 * Z
YP = 40
OFF = 4
BLOCKS = 8
SAMPLES = 256
NODES = 512
ROWS = 24
MESSAGE = 136
F32 = jnp.float32
VMEM = pl.BlockSpec(memory_space=pltpu.VMEM)
HBM = pl.BlockSpec(memory_space=pltpu.HBM)
SIZES = {"x": 4, "zh": 2, "y": 4, "core": 2}


def permute(value, axes, target):
    dims = [SIZES[a] for a in axes]

    def flat(place):
        number = 0
        for coordinate, size in zip(place, dims):
            number = number * size + coordinate
        return number

    pairs = []
    for place in itertools.product(*[range(d) for d in dims]):
        other = target(*place)
        if other is not None:
            pairs.append((flat(place), flat(other)))
    return lax.ppermute(value, axes if len(axes) > 1 else axes[0], pairs)


def even_pair(a, b):
    return (a, b ^ 1)


def odd_pair(a, b):
    if b == 1:
        return (a + 1, 0) if a < 3 else None
    return (a - 1, 1) if a > 0 else None


def odd_along_x(x, zh, core):
    other = odd_pair(x, zh)
    return other + (core,) if other else (x, zh, core ^ 1)


def odd_along_y(x, y, core):
    other = odd_pair(y, core)
    return (x,) + other if other else (x ^ 1, y, core)


def half_lanes(shape):
    return lax.broadcasted_iota(jnp.int32, shape, len(shape) - 1) < Z


def swap_halves(value):
    return pltpu.roll(value, Z, axis=value.ndim - 1)


def pack(first, second):
    return jnp.where(half_lanes(first.shape), first, second)


def unpack(row):
    low = half_lanes(row.shape)
    other = swap_halves(row)
    return jnp.where(low, row, other), jnp.where(low, other, row)


def whereabouts():
    x, zh, y, core = [lax.axis_index(axis) for axis in ("x", "zh", "y", "core")]
    return zh, core, 4 * x + y, ((x * 2 + zh) * 4 + y) * 2 + core


def has_odd_pair(outer, inner):
    return lax.axis_index(outer) != 3 * lax.axis_index(inner)


def edge_y_kernel(
    noise_far, classes_far, owner_far,
    odd, even, noise, classes, names,
    noise_edges, class_edges, owner, sems,
):
    first = [
        pltpu.make_async_copy(noise_far.at[:, 0:8, :], noise_edges.at[0], sems.at[0]),
        pltpu.make_async_copy(noise_far.at[:, Y - 8 : Y, :], noise_edges.at[1], sems.at[1]),
        pltpu.make_async_copy(classes_far.at[:, 0:8, :], class_edges.at[0], sems.at[2]),
        pltpu.make_async_copy(classes_far.at[:, Y - 8 : Y, :], class_edges.at[1], sems.at[3]),
        pltpu.make_async_copy(owner_far, owner, sems.at[4]),
    ]
    rest = [
        pltpu.make_async_copy(noise_far, noise, sems.at[5]),
        pltpu.make_async_copy(classes_far, classes, sems.at[6]),
    ]
    for copy in first + rest:
        copy.start()
    for copy in first:
        copy.wait()
    core = whereabouts()[1]
    lane = lax.broadcasted_iota(jnp.int32, (8, W), 1)
    own = jnp.zeros((8, W), F32)
    for b in range(BLOCKS):
        own = jnp.where(lane == b, (owner[b] + 1).astype(F32), own)
    names[...] = own
    odd[X] = own[0:4]
    even[X] = own[0:4]

    def message(out, end, start, one, two):
        out[0:X, 0:3, :] = noise_edges[end, :, start : start + 3, :]
        kinds = (class_edges[end] + 1).astype(F32)
        out[0:X, 3:4, :] = jnp.concatenate([kinds[:, one : one + 1], kinds[:, two : two + 1]], axis=-1)

    @pl.when(core == 0)
    def _():
        message(even, 1, 5, 6, 7)
        message(odd, 0, 0, 0, 1)

    @pl.when(core == 1)
    def _():
        message(even, 0, 0, 0, 1)
        message(odd, 1, 5, 6, 7)

    for copy in rest:
        copy.wait()


def prepare_kernel(noise, classes, table, field, kinds, tables, held_table, sem):
    copy = pltpu.make_async_copy(table, held_table, sem)
    copy.start()
    half = whereabouts()[0]
    for out in (field, kinds):
        out[:, 0:8, :] = jnp.zeros((X, 8, W), F32)
        out[:, 32:40, :] = jnp.zeros((X, 8, W), F32)
    for x in range(X):
        true = mirrored(x, half)
        field[x, OFF : OFF + Y, :] = noise[true]
        kind = (classes[true] + 1).astype(F32)
        kinds[x, OFF : OFF + Y, :] = jnp.concatenate([kind, kind], axis=-1)
    copy.wait()
    spread_table(held_table, half, tables)


def edge_x_kernel(
    field_in, kinds_in, names, even_in, odd_in, tables,
    field, kinds, odd, even, lists,
    weights, moved,
):
    half, core = whereabouts()[0:2]
    field[...] = field_in[...]
    kinds[...] = kinds_in[...]
    lists[0:4] = names[0:4]
    lists[1:2] = even_in[X, 0:1, :]

    inside = has_odd_pair("y", "core")

    def sides(low, high):
        for x in range(X):
            true = mirrored(x, half)
            for message, start, one in ((low, 1, 2), (high, 36, 36)):
                held = message[true]
                if message is odd_in:
                    held = jnp.where(inside, held, 0.0)
                field[x, start : start + 3, :] = held[0:3]
                first, second = unpack(held[3:4])
                kinds[x, one : one + 1, :] = first
                kinds[x, one + 1 : one + 2, :] = second

    @pl.when(core == 0)
    def _():
        sides(odd_in, even_in)

    @pl.when(core == 1)
    def _():
        sides(even_in, odd_in)

    for out, row, step in ((odd, 0, 1), (even, X - 1, -1)):
        def put(o, part, value):
            weights[o, part, :] = value

        weigh(kinds[row + step], tables, put)
        for n in range(3):
            for c, value in enumerate(lean(field[row + n * step])):
                moved[c, n] = value
        second = operate(
            lambda o: weights[o],
            lambda a, c: moved[c, a if step == 1 else 2 - a],
            jnp.minimum(kinds[row + step], 1.0),
        )
        out[0:38, :] = field[row][1:39]
        out[38:76, :] = field[row + step][1:39]
        out[76:112, :] = second[2:38]
        kind = kinds[row]
        out[112:130, :] = pack(kind[2:20], kind[20:38])
        out[130:132, :] = lists[0:2]
        out[132:MESSAGE, :] = jnp.zeros((MESSAGE - 132, W), F32)


def mirrored(x, half):
    return x + half * (X - 1 - 2 * x)


def rows_by_column(block_rows):
    return [block_rows[pl.ds(c, 8, stride=8), :] for c in range(8)]


def split(value):
    high = value.astype(jnp.bfloat16)
    low = (value - high.astype(F32)).astype(jnp.bfloat16)
    return high, low


def weigh(kinds, table, put):
    for b in range(3):
        moved = kinds if b == 1 else pltpu.roll(kinds, (b - 1) % YP, axis=0)
        index = jnp.maximum(moved.astype(jnp.int32) - 1, 0)
        for g in range(YP // 8):
            part = index[8 * g : 8 * g + 8]
            for a in range(3):
                for c in range(3):
                    o = 9 * a + 3 * b + c
                    put(
                        o,
                        pl.ds(8 * g, 8),
                        jnp.take_along_axis(table[o], part, axis=0, mode="promise_in_bounds"),
                    )


def spread_table(table, half, out):
    held = table[...]
    columns = [jnp.broadcast_to(held[:, o : o + 1], (8, W)) for o in range(27)]
    for o in range(27):
        out[o] = jnp.where(half == 0, columns[o], columns[o + 9 * (2 - 2 * (o // 9))])


def lean(row):
    lanes = lax.broadcasted_iota(jnp.int32, (YP, W), 1) % Z
    below = jnp.where(lanes > 0, pltpu.roll(row, 1, axis=1), 0.0)
    above = jnp.where(lanes < Z - 1, pltpu.roll(row, W - 1, axis=1), 0.0)
    return below, row, above


def operate(weight, moved, inside):
    sums = []
    for b in range(3):
        total = None
        for a in range(3):
            for c in range(3):
                term = weight(9 * a + 3 * b + c) * moved(a, c)
                total = term if total is None else total + term
        sums.append(total)
    result = pltpu.roll(sums[0], 1, axis=0) + sums[1] + pltpu.roll(sums[2], YP - 1, axis=0)
    return result * inside


def interior_kernel(
    field, kinds, tables, matrix, drill, gain, node_block, count, owner,
    weights, first, second, third, smooth, held_matrix, held_rows, other, live, blocks,
    scalars, sems,
):
    copies = [
        pltpu.make_async_copy(matrix, held_matrix, sems.at[0]),
        pltpu.make_async_copy(drill, held_rows.at[0], sems.at[1]),
        pltpu.make_async_copy(gain, held_rows.at[1], sems.at[2]),
        pltpu.make_async_copy(node_block, scalars.at[0], sems.at[3]),
        pltpu.make_async_copy(count, scalars.at[1], sems.at[4]),
        pltpu.make_async_copy(owner, scalars.at[2], sems.at[5]),
    ]
    for copy in reversed(copies):
        copy.start()
    plane = whereabouts()[2]
    for x in range(X):
        def put(o, rows, value, x=x):
            weights[o, x, rows, :] = value

        weigh(kinds[x], tables, put)
        for c, value in enumerate(lean(field[x])):
            first[c, x] = value

    def step(source, start, x):
        return operate(
            lambda o: weights[o, x],
            lambda a, c: source[c, x + a - 1 - start],
            jnp.minimum(kinds[x], 1.0),
        )

    for x in range(1, 7):
        for c, value in enumerate(lean(step(first, 0, x))):
            second[c, x - 1] = value
    for x in range(2, 6):
        value = 2.0 * step(second, 1, x) - first[1, x]
        for c, value in enumerate(lean(value)):
            third[c, x - 2] = value
    for x in range(3, 5):
        fourth = 2.0 * step(third, 2, x) - second[1, x - 1]
        result = (
            CHEB[0] * first[1, x] + CHEB[1] * second[1, x - 1] + CHEB[2] * third[1, x - 2] + CHEB[3] * fourth
        )
        for g in range(4):
            smooth[4 * (x - 3) + g] = result[OFF + 8 * g : OFF + 8 * g + 8]
    for copy in copies:
        copy.wait()
    other[...] = jnp.zeros((8, SAMPLES), F32)
    for k in range(2):
        for h in range(2):
            for kind in range(2):
                row = 4 * kind + 2 * k + h
                other[row : row + 1, 0:W] = held_rows[kind, k : k + 1, h * W : h * W + W]
    lane = lax.broadcasted_iota(jnp.int32, (8, W), 1)
    names = jnp.zeros((8, W), F32)
    places = jnp.zeros((8, W), jnp.int32)
    limit = jnp.zeros((BLOCKS, SAMPLES), jnp.int32)
    block = lax.broadcasted_iota(jnp.int32, (BLOCKS, SAMPLES), 0)
    for b in range(BLOCKS):
        names = jnp.where(lane == 8 * plane + b, (scalars[2, b] + 1).astype(F32), names)
        places = jnp.where(lane == b, scalars[0, b], places)
        limit = jnp.where(block == b, scalars[1, b], limit)
    other[0:1, W : 2 * W] = names[0:1]
    blocks[...] = places
    sample = lax.broadcasted_iota(jnp.int32, (BLOCKS, SAMPLES), 1)
    live[...] = (sample < limit).astype(F32)


def fill_halo(message, inside, tables, halo_kinds, halo_weights, halo_first, edge_second):
    held = jnp.where(inside, message[...], 0.0)
    one, two = [jnp.zeros((n, W), F32) for n in (1, 2)]
    low, high = unpack(held[112:130])
    halo_kinds[...] = jnp.concatenate([two, low, high, two], axis=0)

    def put(o, part, value):
        halo_weights[o, part, :] = value

    weigh(halo_kinds[...], tables, put)
    for i in range(2):
        for c, value in enumerate(lean(jnp.concatenate([one, held[38 * i : 38 * i + 38], one], axis=0))):
            halo_first[c, i] = value
    for c, value in enumerate(lean(jnp.concatenate([two, held[76:112], two], axis=0))):
        edge_second[c, 2] = value


def side(
    high, kinds, weights, first, second, third, halo_kinds, halo_weights, halo_first, edge_second, edge_third, put
):
    def beyond(x):
        return x - X if high else -1 - x

    def weight(x):
        if 0 <= x < X:
            return (lambda o: weights[o, x]), jnp.minimum(kinds[x], 1.0)
        return (lambda o: halo_weights[o]), jnp.minimum(halo_kinds[...], 1.0)

    def at_first(x, c):
        return first[c, x] if 0 <= x < X else halo_first[c, beyond(x)]

    def at_second(x, c):
        return second[c, x - 1] if 1 <= x < 7 else edge_second[c, beyond(x) + 1]

    def at_third(x, c):
        return third[c, x - 2] if 2 <= x < 6 else edge_third[c, beyond(x) + 2]

    def step(at, x):
        of, inside = weight(x)
        return operate(of, lambda a, c: at(x + a - 1, c), inside)

    def row(n):
        return X - 1 - n if high else n

    for n in (-1, 0):
        for c, value in enumerate(lean(step(at_first, row(n)))):
            edge_second[c, -n] = value
    for n in (-1, 0, 1):
        value = 2.0 * step(at_second, row(n)) - at_first(row(n), 1)
        for c, value in enumerate(lean(value)):
            edge_third[c, 1 - n] = value
    for n in (0, 1, 2):
        x = row(n)
        fourth = 2.0 * step(at_third, x) - at_second(x, 1)
        result = (
            CHEB[0] * at_first(x, 1) + CHEB[1] * at_second(x, 1) + CHEB[2] * at_third(x, 1) + CHEB[3] * fourth
        )
        for g in range(4):
            put(x, g, result[OFF + 8 * g : OFF + 8 * g + 8])


def lower_kernel(
    kinds, edges, weights, first, second, third, tables,
    lower,
    halo_kinds, halo_weights, halo_first, edge_second, edge_third,
):
    fill_halo(edges, has_odd_pair("x", "zh"), tables, halo_kinds, halo_weights, halo_first, edge_second)

    def put(x, g, value):
        lower[4 * x + g] = value

    side(
        False, kinds, weights, first, second, third,
        halo_kinds, halo_weights, halo_first, edge_second, edge_third, put,
    )


def finish_kernel(
    kinds, edges, near, weights, first, second, third, middle, lower, tables, matrix, other, live, blocks,
    smooth, payload, lists,
    halo_kinds, halo_weights, halo_first, edge_second, edge_third, chosen, node_block, sem,
):
    copy = pltpu.make_async_copy(blocks.at[0:1], node_block, sem)
    copy.start()
    half = whereabouts()[0]
    lists[0:4] = near[0:4]
    lists[4:8] = jnp.zeros((4, W), F32)
    lists[2:4] = edges[130:132]
    fill_halo(edges, True, tables, halo_kinds, halo_weights, halo_first, edge_second)

    def put(x, g, value):
        smooth[4 * mirrored(x, half) + g] = value

    side(
        True, kinds, weights, first, second, third,
        halo_kinds, halo_weights, halo_first, edge_second, edge_third, put,
    )
    for g in range(4):
        for x in (0, 1, 2):
            put(x, g, lower[4 * x + g])
        for x in (3, 4):
            put(x, g, middle[4 * (x - 3) + g])

    copy.wait()
    for b in range(BLOCKS):
        chosen[pl.ds(8 * b, 8), :] = smooth[node_block[0, b]]
    columns = rows_by_column(chosen)
    low = half_lanes((8, W))
    parts = ([], [])
    for j in range(4):
        one, two = columns[2 * j], columns[2 * j + 1]
        parts[0].append(jnp.where(low, one, swap_halves(two)))
        parts[1].append(jnp.where(low, swap_halves(one), two))
    values = [jnp.concatenate(p, axis=1) for p in parts]
    pieces = [split(v) for v in values]
    left = jnp.concatenate([pieces[0][0], pieces[1][0], pieces[0][1], pieces[1][1]], axis=0)
    block = lax.broadcasted_iota(jnp.int32, (BLOCKS, SAMPLES), 0)
    sums = [jnp.zeros((BLOCKS, SAMPLES), F32) for _ in range(2)]
    for b in range(BLOCKS):
        product = lax.dot_general(
            left, matrix[b], (((1,), (1,)), ((), ())), preferred_element_type=F32
        )
        for r in range(2):
            both = product[8 * r : 8 * r + 8] + product[16 + 8 * r : 24 + 8 * r]
            sums[r] = jnp.where(block == b, both, sums[r])
    for r in range(2):
        payload[8 * r : 8 * r + 8, :] = jnp.where(live[...] > 0.0, sums[r], 0.0)
    payload[16:24, :] = other[...]


def collect_kernel(lists, here, keep, send):
    names = here[0, 16:24, W : 2 * W]
    for n in range(1, 16):
        names = names + here[n, 16:24, W : 2 * W]
    names = jnp.broadcast_to(names[0:1], (8, W))
    lane = lax.broadcasted_iota(jnp.int32, (8, W), 1)
    row = lax.broadcasted_iota(jnp.int32, (8, W), 0)
    hits, spots = [], []
    half, core, _, me = whereabouts()
    for member in range(4):
        tile = me ^ (1 if member & 1 else 0) ^ (8 if member & 2 else 0)
        held = jnp.broadcast_to(lists[member : member + 1], (8, W))
        name = jnp.sum(jnp.where(lane == row, held, 0.0), axis=1, keepdims=True)
        name = jnp.broadcast_to(name, (8, W))
        hits.append(name == names)
        hits.append((2 * tile + 1 + (row & 1)).astype(F32) == names)
        block = name.astype(jnp.int32) - 1
        holder = block >> 1
        spot = ((holder >> 4) * 4 + ((holder >> 1) & 3)) * 8 + 2 * (block & 1)
        mine = ((holder & 1) == core) & (((holder >> 3) & 1) == half)
        spots.append(jnp.where(mine, spot, -1024))
    hit = jnp.concatenate([h.astype(F32) for h in hits], axis=0).astype(jnp.bfloat16)
    spots = jnp.concatenate(spots, axis=0)
    lane = lax.broadcasted_iota(jnp.int32, (32, W), 1)
    choose = jnp.concatenate(
        [(lane == spots + 4 * kind + h).astype(F32) for kind in range(2) for h in range(2)], axis=0
    ).astype(jnp.bfloat16)

    def gather(left, rows, lanes):
        data = jnp.concatenate([here[n, rows, lanes] for n in range(16)], axis=0)
        high, low = split(data)
        return jnp.dot(left, high, preferred_element_type=F32) + jnp.dot(
            left, low, preferred_element_type=F32
        )

    totals = [gather(hit, slice(8 * r, 8 * r + 8), slice(0, 2 * W)) for r in range(2)]
    found = gather(choose, slice(16, 24), slice(0, W))
    row = lax.broadcasted_iota(jnp.int32, (8, SAMPLES), 0)
    for member in range(4):
        out = (send if member & 1 else keep).at[member // 2]
        drill, gain = [
            jnp.concatenate(
                [found[64 * kind + 32 * h + 8 * member : 64 * kind + 32 * h + 8 * member + 8] for h in range(2)],
                axis=1,
            )
            for kind in range(2)
        ]
        for r in range(2):
            out[8 * r : 8 * r + 8, :] = drill - totals[r][16 * member : 16 * member + 8]
        out[16:24, :] = gain
        own = [totals[r][16 * member + 8 : 16 * member + 16] for r in range(2)]
        out[24:32, :] = jnp.where(row < 2, own[0], own[1])


def update_kernel(
    keep, near, far, smooth, matrix, rows, live, blocks,
    out, misfit,
    update, node_block, sem,
):
    copy = pltpu.make_async_copy(blocks.at[0:1], node_block, sem)
    copy.start()
    sums = keep[0] + near[0] + far[...]
    for k in range(2):
        for r in range(2):
            t = 24 + 2 * r + k
            misfit[k, r : r + 1, :] = rows[0, k : k + 1, :] - sums[t : t + 1, :]
    picked = [jnp.where(live[...] > 0.0, sums[16:24] * sums[8 * r : 8 * r + 8], 0.0) for r in range(2)]
    pieces = [split(v) for v in picked]
    left = jnp.concatenate([pieces[0][0], pieces[1][0], pieces[0][1], pieces[1][1]], axis=0)
    block = lax.broadcasted_iota(jnp.int32, (BLOCKS, NODES), 0)
    sums = [jnp.zeros((BLOCKS, NODES), F32) for _ in range(2)]
    for b in range(BLOCKS):
        product = jnp.dot(left, matrix[b], preferred_element_type=F32)
        for r in range(2):
            both = product[8 * r : 8 * r + 8] + product[16 + 8 * r : 24 + 8 * r]
            sums[r] = jnp.where(block == b, both, sums[r])
    low = half_lanes((8, W))
    for j in range(4):
        one, two = sums[0][:, j * W : j * W + W], sums[1][:, j * W : j * W + W]
        update[pl.ds(2 * j, 8, stride=8), :] = jnp.where(low, one, swap_halves(two))
        update[pl.ds(2 * j + 1, 8, stride=8), :] = jnp.where(low, swap_halves(one), two)
    out[...] = smooth[...]
    copy.wait()
    for b in range(BLOCKS):
        n = node_block[0, b]
        out[n] = out[n] + update[8 * b : 8 * b + 8, :]


def shape(*dims, dtype=F32):
    return jax.ShapeDtypeStruct(dims, dtype)


def call(kernel, outs, ins, name, scratch=()):
    return pl.pallas_call(
        kernel,
        out_shape=outs,
        in_specs=ins,
        out_specs=(VMEM,) * len(outs),
        scratch_shapes=scratch,
        compiler_params=pltpu.CompilerParams(vmem_limit_bytes=24 * 1024 * 1024),
        name=name,
    )


def shards(
    noise, classes, table, obs_matrix, node_block, sample_block, sample_count, drill_data, obs_gain
):
    noise, classes, table, matrix, blocks, owner, count, drill, gain = [
        pltpu.with_memory_space_constraint(a, pltpu.HBM)
        for a in (
            noise, classes, table, obs_matrix, node_block, sample_block, sample_count, drill_data, obs_gain
        )
    ]
    odd, even, near_noise, near_classes, names = call(
        edge_y_kernel,
        (shape(X + 1, 4, W), shape(X + 1, 4, W), shape(X, Y, W), shape(X, Y, Z, dtype=jnp.int32), shape(8, W)),
        [HBM] * 3,
        "edge_y",
        [
            pltpu.VMEM((2, X, 8, W), F32),
            pltpu.VMEM((2, X, 8, Z), jnp.int32),
            pltpu.SMEM((BLOCKS,), jnp.int32),
            pltpu.SemaphoreType.DMA((7,)),
        ],
    )(noise, classes, owner)
    odd = permute(odd, ("x", "y", "core"), odd_along_y)
    even = permute(even, ("y", "core"), even_pair)
    field, kinds, tables = call(
        prepare_kernel,
        (shape(X, YP, W), shape(X, YP, W), shape(27, 8, W)),
        [VMEM] * 2 + [HBM],
        "prepare",
        [pltpu.VMEM((8, 27), F32), pltpu.SemaphoreType.DMA],
    )(near_noise, near_classes, table)
    field, kinds, odd, even, lists = call(
        edge_x_kernel,
        (shape(X, YP, W), shape(X, YP, W), shape(MESSAGE, W), shape(MESSAGE, W), shape(4, W)),
        [VMEM] * 6,
        "edge_x",
        [pltpu.VMEM((27, YP, W), F32), pltpu.VMEM((3, 3, YP, W), F32)],
    )(field, kinds, names, even, odd, tables)
    odd = permute(odd, ("x", "zh", "core"), odd_along_x)
    even = permute(even, ("x", "zh"), even_pair)
    weights, first, second, third, middle, matrix, rows, other, live, blocks = call(
        interior_kernel,
        (
            shape(27, X, YP, W),
            shape(3, X, YP, W),
            shape(3, 6, YP, W),
            shape(3, 4, YP, W),
            shape(8, 8, W),
            shape(BLOCKS, SAMPLES, NODES, dtype=jnp.bfloat16),
            shape(2, 2, SAMPLES),
            shape(8, SAMPLES),
            shape(BLOCKS, SAMPLES),
            shape(8, W, dtype=jnp.int32),
        ),
        [VMEM] * 3 + [HBM] * 6,
        "interior",
        [pltpu.SMEM((3, BLOCKS), jnp.int32), pltpu.SemaphoreType.DMA((6,))],
    )(field, kinds, tables, matrix, drill, gain, blocks, count, owner)
    halo_scratch = [
        pltpu.VMEM((YP, W), F32),
        pltpu.VMEM((27, YP, W), F32),
        pltpu.VMEM((3, 2, YP, W), F32),
        pltpu.VMEM((3, 3, YP, W), F32),
        pltpu.VMEM((3, 3, YP, W), F32),
    ]
    (lower,) = call(lower_kernel, (shape(12, 8, W),), [VMEM] * 7, "lower", halo_scratch)(
        kinds, odd, weights, first, second, third, tables
    )
    index_scratch = [pltpu.SMEM((1, W), jnp.int32), pltpu.SemaphoreType.DMA]
    smooth, payload, lists = call(
        finish_kernel,
        (shape(32, 8, W), shape(ROWS, SAMPLES), shape(8, W)),
        [VMEM] * 14,
        "finish",
        halo_scratch + [pltpu.VMEM((64, W), F32)] + index_scratch,
    )(
        kinds, even, lists, weights, first, second, third, middle, lower, tables, matrix,
        other, live, blocks,
    )
    here = lax.all_to_all(
        jnp.broadcast_to(payload[None], (16, ROWS, SAMPLES)), ("x", "y"), 0, 0, tiled=True
    )
    keep, send = call(
        collect_kernel, (shape(2, 32, SAMPLES), shape(2, 32, SAMPLES)), [VMEM] * 2, "collect"
    )(lists, here)
    near = permute(send, ("core",), lambda c: (c ^ 1,))
    far = permute(keep[1] + near[1], ("zh",), lambda z: (z ^ 1,))
    out, misfit = call(
        update_kernel,
        (shape(32, 8, W), shape(2, 2, SAMPLES)),
        [VMEM] * 8,
        "update",
        [pltpu.VMEM((64, W), F32)] + index_scratch,
    )(keep, near, far, smooth, matrix, rows, live, blocks)
    return out.reshape(X, Y, W), misfit


def solution(mesh):
    fine = Mesh(
        mesh.devices.reshape(4, 4, 2, 4, 2), ("real", "x", "zh", "y", "core")
    )
    sx, sy = ("x", "zh"), ("y", "core")
    both = sx + sy
    in_specs = (
        P(sx, sy, "real"),
        P(sx, sy, None),
        P(),
        P(both, None, None),
        P(both),
        P(both),
        P(both),
        P(both, None),
        P(both, None),
    )
    out_specs = (P(sx, sy, "real"), P(both, "real", None))
    return jax.shard_map(shards, mesh=fine, in_specs=in_specs, out_specs=out_specs, check_vma=False)
```

```python
import itertools

import jax
import jax.numpy as jnp
from jax import lax
from jax.experimental import pallas as pl
from jax.experimental.pallas import tpu as pltpu
from jax.sharding import Mesh, PartitionSpec as P

CHEB = (0.6, 0.5, 0.3, 0.2)
X, Y, Z = 8, 32, 64
W = 2 * Z
YP = 40
OFF = 4
BLOCKS = 8
SAMPLES = 256
NODES = 512
ROWS = 24
MESSAGE = 136
F32 = jnp.float32
VMEM = pl.BlockSpec(memory_space=pltpu.VMEM)
HBM = pl.BlockSpec(memory_space=pltpu.HBM)
SIZES = {"x": 4, "zh": 2, "y": 4, "core": 2}


def permute(value, axes, target):
    dims = [SIZES[a] for a in axes]

    def flat(place):
        number = 0
        for coordinate, size in zip(place, dims):
            number = number * size + coordinate
        return number

    pairs = []
    for place in itertools.product(*[range(d) for d in dims]):
        other = target(*place)
        if other is not None:
            pairs.append((flat(place), flat(other)))
    return lax.ppermute(value, axes if len(axes) > 1 else axes[0], pairs)


def even_pair(a, b):
    return (a, b ^ 1)


def odd_pair(a, b):
    if b == 1:
        return (a + 1, 0) if a < 3 else None
    return (a - 1, 1) if a > 0 else None


def odd_along_x(x, zh, core):
    other = odd_pair(x, zh)
    return other + (core,) if other else (x, zh, core ^ 1)


def odd_along_y(x, y, core):
    other = odd_pair(y, core)
    return (x,) + other if other else (x ^ 1, y, core)


def half_lanes(shape):
    return lax.broadcasted_iota(jnp.int32, shape, len(shape) - 1) < Z


def swap_halves(value):
    return pltpu.roll(value, Z, axis=value.ndim - 1)


def pack(first, second):
    return jnp.where(half_lanes(first.shape), first, second)


def unpack(row):
    low = half_lanes(row.shape)
    other = swap_halves(row)
    return jnp.where(low, row, other), jnp.where(low, other, row)


def whereabouts():
    x, zh, y, core = [lax.axis_index(axis) for axis in ("x", "zh", "y", "core")]
    return zh, core, 4 * x + y, ((x * 2 + zh) * 4 + y) * 2 + core


def has_odd_pair(outer, inner):
    return lax.axis_index(outer) != 3 * lax.axis_index(inner)


def edge_y_kernel(
    noise_far, classes_far, owner_far,
    odd, even, names,
    noise_edges, class_edges, owner, sems,
):
    copies = [
        pltpu.make_async_copy(noise_far.at[:, 0:8, :], noise_edges.at[0], sems.at[0]),
        pltpu.make_async_copy(noise_far.at[:, Y - 8 : Y, :], noise_edges.at[1], sems.at[1]),
        pltpu.make_async_copy(classes_far.at[:, 0:8, :], class_edges.at[0], sems.at[2]),
        pltpu.make_async_copy(classes_far.at[:, Y - 8 : Y, :], class_edges.at[1], sems.at[3]),
        pltpu.make_async_copy(owner_far, owner, sems.at[4]),
    ]
    for copy in copies:
        copy.start()
    for copy in copies:
        copy.wait()
    core = whereabouts()[1]
    lane = lax.broadcasted_iota(jnp.int32, (8, W), 1)
    own = jnp.zeros((8, W), F32)
    for b in range(BLOCKS):
        own = jnp.where(lane == b, (owner[b] + 1).astype(F32), own)
    names[...] = own
    odd[X] = own[0:4]
    even[X] = own[0:4]

    def message(out, end, start, one, two):
        out[0:X, 0:3, :] = noise_edges[end, :, start : start + 3, :]
        kinds = (class_edges[end] + 1).astype(F32)
        out[0:X, 3:4, :] = jnp.concatenate([kinds[:, one : one + 1], kinds[:, two : two + 1]], axis=-1)

    @pl.when(core == 0)
    def _():
        message(even, 1, 5, 6, 7)
        message(odd, 0, 0, 0, 1)

    @pl.when(core == 1)
    def _():
        message(even, 0, 0, 0, 1)
        message(odd, 1, 5, 6, 7)


def prepare_kernel(
    noise_far, classes_far, table, field, kinds, tables, noise, classes, held_table, sems
):
    copies = [
        pltpu.make_async_copy(noise_far, noise, sems.at[0]),
        pltpu.make_async_copy(classes_far, classes, sems.at[1]),
        pltpu.make_async_copy(table, held_table, sems.at[2]),
    ]
    for copy in copies:
        copy.start()
    for copy in copies:
        copy.wait()
    half = whereabouts()[0]
    for out in (field, kinds):
        out[:, 0:8, :] = jnp.zeros((X, 8, W), F32)
        out[:, 32:40, :] = jnp.zeros((X, 8, W), F32)
    for x in range(X):
        true = mirrored(x, half)
        field[x, OFF : OFF + Y, :] = noise[true]
        kind = (classes[true] + 1).astype(F32)
        kinds[x, OFF : OFF + Y, :] = jnp.concatenate([kind, kind], axis=-1)
    spread_table(held_table, half, tables)


def edge_x_kernel(
    odd_in, even_in, field_in, kinds_in, names, tables,
    field, kinds, odd, even, lists,
    weights, moved,
):
    half, core = whereabouts()[0:2]
    field[...] = field_in[...]
    kinds[...] = kinds_in[...]
    lists[0:4] = names[0:4]
    lists[1:2] = even_in[X, 0:1, :]

    inside = has_odd_pair("y", "core")

    def sides(low, high):
        for x in range(X):
            true = mirrored(x, half)
            for message, start, one in ((low, 1, 2), (high, 36, 36)):
                held = message[true]
                if message is odd_in:
                    held = jnp.where(inside, held, 0.0)
                field[x, start : start + 3, :] = held[0:3]
                first, second = unpack(held[3:4])
                kinds[x, one : one + 1, :] = first
                kinds[x, one + 1 : one + 2, :] = second

    @pl.when(core == 0)
    def _():
        sides(odd_in, even_in)

    @pl.when(core == 1)
    def _():
        sides(even_in, odd_in)

    for out, row, step in ((odd, 0, 1), (even, X - 1, -1)):
        def put(o, part, value):
            weights[o, part, :] = value

        weigh(kinds[row + step], tables, put)
        for n in range(3):
            for c, value in enumerate(lean(field[row + n * step])):
                moved[c, n] = value
        second = operate(
            lambda o: weights[o],
            lambda a, c: moved[c, a if step == 1 else 2 - a],
            jnp.minimum(kinds[row + step], 1.0),
        )
        out[0:38, :] = field[row][1:39]
        out[38:76, :] = field[row + step][1:39]
        out[76:112, :] = second[2:38]
        kind = kinds[row]
        out[112:130, :] = pack(kind[2:20], kind[20:38])
        out[130:132, :] = lists[0:2]
        out[132:MESSAGE, :] = jnp.zeros((MESSAGE - 132, W), F32)


def mirrored(x, half):
    return x + half * (X - 1 - 2 * x)


def rows_by_column(block_rows):
    return [block_rows[pl.ds(c, 8, stride=8), :] for c in range(8)]


def split(value):
    high = value.astype(jnp.bfloat16)
    low = (value - high.astype(F32)).astype(jnp.bfloat16)
    return high, low


def weigh(kinds, table, put):
    for b in range(3):
        moved = kinds if b == 1 else pltpu.roll(kinds, (b - 1) % YP, axis=0)
        index = jnp.maximum(moved.astype(jnp.int32) - 1, 0)
        for g in range(YP // 8):
            part = index[8 * g : 8 * g + 8]
            for a in range(3):
                for c in range(3):
                    o = 9 * a + 3 * b + c
                    put(
                        o,
                        pl.ds(8 * g, 8),
                        jnp.take_along_axis(table[o], part, axis=0, mode="promise_in_bounds"),
                    )


def spread_table(table, half, out):
    held = table[...]
    columns = [jnp.broadcast_to(held[:, o : o + 1], (8, W)) for o in range(27)]
    for o in range(27):
        out[o] = jnp.where(half == 0, columns[o], columns[o + 9 * (2 - 2 * (o // 9))])


def lean(row):
    lanes = lax.broadcasted_iota(jnp.int32, (YP, W), 1) % Z
    below = jnp.where(lanes > 0, pltpu.roll(row, 1, axis=1), 0.0)
    above = jnp.where(lanes < Z - 1, pltpu.roll(row, W - 1, axis=1), 0.0)
    return below, row, above


def operate(weight, moved, inside):
    sums = []
    for b in range(3):
        total = None
        for a in range(3):
            for c in range(3):
                term = weight(9 * a + 3 * b + c) * moved(a, c)
                total = term if total is None else total + term
        sums.append(total)
    result = pltpu.roll(sums[0], 1, axis=0) + sums[1] + pltpu.roll(sums[2], YP - 1, axis=0)
    return result * inside


def interior_kernel(
    field, kinds, tables, matrix, drill, gain, node_block, count, owner,
    weights, first, second, third, smooth, held_matrix, held_rows, other, live, blocks,
    scalars, sems,
):
    copies = [
        pltpu.make_async_copy(matrix, held_matrix, sems.at[0]),
        pltpu.make_async_copy(drill, held_rows.at[0], sems.at[1]),
        pltpu.make_async_copy(gain, held_rows.at[1], sems.at[2]),
        pltpu.make_async_copy(node_block, scalars.at[0], sems.at[3]),
        pltpu.make_async_copy(count, scalars.at[1], sems.at[4]),
        pltpu.make_async_copy(owner, scalars.at[2], sems.at[5]),
    ]
    for copy in reversed(copies):
        copy.start()
    plane = whereabouts()[2]
    for x in range(X):
        def put(o, rows, value, x=x):
            weights[o, x, rows, :] = value

        weigh(kinds[x], tables, put)
        for c, value in enumerate(lean(field[x])):
            first[c, x] = value

    def step(source, start, x):
        return operate(
            lambda o: weights[o, x],
            lambda a, c: source[c, x + a - 1 - start],
            jnp.minimum(kinds[x], 1.0),
        )

    for x in range(1, 7):
        for c, value in enumerate(lean(step(first, 0, x))):
            second[c, x - 1] = value
    for x in range(2, 6):
        value = 2.0 * step(second, 1, x) - first[1, x]
        for c, value in enumerate(lean(value)):
            third[c, x - 2] = value
    for x in range(3, 5):
        fourth = 2.0 * step(third, 2, x) - second[1, x - 1]
        result = (
            CHEB[0] * first[1, x] + CHEB[1] * second[1, x - 1] + CHEB[2] * third[1, x - 2] + CHEB[3] * fourth
        )
        for g in range(4):
            smooth[4 * (x - 3) + g] = result[OFF + 8 * g : OFF + 8 * g + 8]
    for copy in copies:
        copy.wait()
    other[...] = jnp.zeros((8, SAMPLES), F32)
    for k in range(2):
        for h in range(2):
            for kind in range(2):
                row = 4 * kind + 2 * k + h
                other[row : row + 1, 0:W] = held_rows[kind, k : k + 1, h * W : h * W + W]
    lane = lax.broadcasted_iota(jnp.int32, (8, W), 1)
    names = jnp.zeros((8, W), F32)
    places = jnp.zeros((8, W), jnp.int32)
    limit = jnp.zeros((BLOCKS, SAMPLES), jnp.int32)
    block = lax.broadcasted_iota(jnp.int32, (BLOCKS, SAMPLES), 0)
    for b in range(BLOCKS):
        names = jnp.where(lane == 8 * plane + b, (scalars[2, b] + 1).astype(F32), names)
        places = jnp.where(lane == b, scalars[0, b], places)
        limit = jnp.where(block == b, scalars[1, b], limit)
    other[0:1, W : 2 * W] = names[0:1]
    blocks[...] = places
    sample = lax.broadcasted_iota(jnp.int32, (BLOCKS, SAMPLES), 1)
    live[...] = (sample < limit).astype(F32)


def fill_halo(message, inside, tables, halo_kinds, halo_weights, halo_first, edge_second):
    held = jnp.where(inside, message[...], 0.0)
    one, two = [jnp.zeros((n, W), F32) for n in (1, 2)]
    low, high = unpack(held[112:130])
    halo_kinds[...] = jnp.concatenate([two, low, high, two], axis=0)

    def put(o, part, value):
        halo_weights[o, part, :] = value

    weigh(halo_kinds[...], tables, put)
    for i in range(2):
        for c, value in enumerate(lean(jnp.concatenate([one, held[38 * i : 38 * i + 38], one], axis=0))):
            halo_first[c, i] = value
    for c, value in enumerate(lean(jnp.concatenate([two, held[76:112], two], axis=0))):
        edge_second[c, 2] = value


def side(
    high, kinds, weights, first, second, third, halo_kinds, halo_weights, halo_first, edge_second, edge_third, put
):
    def beyond(x):
        return x - X if high else -1 - x

    def weight(x):
        if 0 <= x < X:
            return (lambda o: weights[o, x]), jnp.minimum(kinds[x], 1.0)
        return (lambda o: halo_weights[o]), jnp.minimum(halo_kinds[...], 1.0)

    def at_first(x, c):
        return first[c, x] if 0 <= x < X else halo_first[c, beyond(x)]

    def at_second(x, c):
        return second[c, x - 1] if 1 <= x < 7 else edge_second[c, beyond(x) + 1]

    def at_third(x, c):
        return third[c, x - 2] if 2 <= x < 6 else edge_third[c, beyond(x) + 2]

    def step(at, x):
        of, inside = weight(x)
        return operate(of, lambda a, c: at(x + a - 1, c), inside)

    def row(n):
        return X - 1 - n if high else n

    for n in (-1, 0):
        for c, value in enumerate(lean(step(at_first, row(n)))):
            edge_second[c, -n] = value
    for n in (-1, 0, 1):
        value = 2.0 * step(at_second, row(n)) - at_first(row(n), 1)
        for c, value in enumerate(lean(value)):
            edge_third[c, 1 - n] = value
    for n in (0, 1, 2):
        x = row(n)
        fourth = 2.0 * step(at_third, x) - at_second(x, 1)
        result = (
            CHEB[0] * at_first(x, 1) + CHEB[1] * at_second(x, 1) + CHEB[2] * at_third(x, 1) + CHEB[3] * fourth
        )
        for g in range(4):
            put(x, g, result[OFF + 8 * g : OFF + 8 * g + 8])


def lower_kernel(
    kinds, edges, weights, first, second, third, tables,
    lower,
    halo_kinds, halo_weights, halo_first, edge_second, edge_third,
):
    fill_halo(edges, has_odd_pair("x", "zh"), tables, halo_kinds, halo_weights, halo_first, edge_second)

    def put(x, g, value):
        lower[4 * x + g] = value

    side(
        False, kinds, weights, first, second, third,
        halo_kinds, halo_weights, halo_first, edge_second, edge_third, put,
    )


def finish_kernel(
    kinds, edges, near, weights, first, second, third, middle, lower, tables, matrix, other, live, blocks,
    smooth, payload, lists,
    halo_kinds, halo_weights, halo_first, edge_second, edge_third, chosen, node_block, sem,
):
    copy = pltpu.make_async_copy(blocks.at[0:1], node_block, sem)
    copy.start()
    half = whereabouts()[0]
    lists[0:4] = near[0:4]
    lists[4:8] = jnp.zeros((4, W), F32)
    lists[2:4] = edges[130:132]
    fill_halo(edges, True, tables, halo_kinds, halo_weights, halo_first, edge_second)

    def put(x, g, value):
        smooth[4 * mirrored(x, half) + g] = value

    side(
        True, kinds, weights, first, second, third,
        halo_kinds, halo_weights, halo_first, edge_second, edge_third, put,
    )
    for g in range(4):
        for x in (0, 1, 2):
            put(x, g, lower[4 * x + g])
        for x in (3, 4):
            put(x, g, middle[4 * (x - 3) + g])

    copy.wait()
    for b in range(BLOCKS):
        chosen[pl.ds(8 * b, 8), :] = smooth[node_block[0, b]]
    columns = rows_by_column(chosen)
    low = half_lanes((8, W))
    parts = ([], [])
    for j in range(4):
        one, two = columns[2 * j], columns[2 * j + 1]
        parts[0].append(jnp.where(low, one, swap_halves(two)))
        parts[1].append(jnp.where(low, swap_halves(one), two))
    values = [jnp.concatenate(p, axis=1) for p in parts]
    pieces = [split(v) for v in values]
    left = jnp.concatenate([pieces[0][0], pieces[1][0], pieces[0][1], pieces[1][1]], axis=0)
    block = lax.broadcasted_iota(jnp.int32, (BLOCKS, SAMPLES), 0)
    sums = [jnp.zeros((BLOCKS, SAMPLES), F32) for _ in range(2)]
    for b in range(BLOCKS):
        product = lax.dot_general(
            left, matrix[b], (((1,), (1,)), ((), ())), preferred_element_type=F32
        )
        for r in range(2):
            both = product[8 * r : 8 * r + 8] + product[16 + 8 * r : 24 + 8 * r]
            sums[r] = jnp.where(block == b, both, sums[r])
    for r in range(2):
        payload[8 * r : 8 * r + 8, :] = jnp.where(live[...] > 0.0, sums[r], 0.0)
    payload[16:24, :] = other[...]


def collect_kernel(lists, here, keep, send):
    names = here[0, 16:24, W : 2 * W]
    for n in range(1, 16):
        names = names + here[n, 16:24, W : 2 * W]
    names = jnp.broadcast_to(names[0:1], (8, W))
    lane = lax.broadcasted_iota(jnp.int32, (8, W), 1)
    row = lax.broadcasted_iota(jnp.int32, (8, W), 0)
    hits, spots = [], []
    half, core, _, me = whereabouts()
    for member in range(4):
        tile = me ^ (1 if member & 1 else 0) ^ (8 if member & 2 else 0)
        held = jnp.broadcast_to(lists[member : member + 1], (8, W))
        name = jnp.sum(jnp.where(lane == row, held, 0.0), axis=1, keepdims=True)
        name = jnp.broadcast_to(name, (8, W))
        hits.append(name == names)
        hits.append((2 * tile + 1 + (row & 1)).astype(F32) == names)
        block = name.astype(jnp.int32) - 1
        holder = block >> 1
        spot = ((holder >> 4) * 4 + ((holder >> 1) & 3)) * 8 + 2 * (block & 1)
        mine = ((holder & 1) == core) & (((holder >> 3) & 1) == half)
        spots.append(jnp.where(mine, spot, -1024))
    hit = jnp.concatenate([h.astype(F32) for h in hits], axis=0).astype(jnp.bfloat16)
    spots = jnp.concatenate(spots, axis=0)
    lane = lax.broadcasted_iota(jnp.int32, (32, W), 1)
    choose = jnp.concatenate(
        [(lane == spots + 4 * kind + h).astype(F32) for kind in range(2) for h in range(2)], axis=0
    ).astype(jnp.bfloat16)

    def gather(left, rows, lanes):
        data = jnp.concatenate([here[n, rows, lanes] for n in range(16)], axis=0)
        high, low = split(data)
        return jnp.dot(left, high, preferred_element_type=F32) + jnp.dot(
            left, low, preferred_element_type=F32
        )

    totals = [gather(hit, slice(8 * r, 8 * r + 8), slice(0, 2 * W)) for r in range(2)]
    found = gather(choose, slice(16, 24), slice(0, W))
    row = lax.broadcasted_iota(jnp.int32, (8, SAMPLES), 0)
    for member in range(4):
        out = (send if member & 1 else keep).at[member // 2]
        drill, gain = [
            jnp.concatenate(
                [found[64 * kind + 32 * h + 8 * member : 64 * kind + 32 * h + 8 * member + 8] for h in range(2)],
                axis=1,
            )
            for kind in range(2)
        ]
        for r in range(2):
            out[8 * r : 8 * r + 8, :] = drill - totals[r][16 * member : 16 * member + 8]
        out[16:24, :] = gain
        own = [totals[r][16 * member + 8 : 16 * member + 16] for r in range(2)]
        out[24:32, :] = jnp.where(row < 2, own[0], own[1])


def update_kernel(
    keep, near, far, smooth, matrix, rows, live, blocks,
    out, misfit,
    update, node_block, sem,
):
    copy = pltpu.make_async_copy(blocks.at[0:1], node_block, sem)
    copy.start()
    sums = keep[0] + near[0] + far[...]
    for k in range(2):
        for r in range(2):
            t = 24 + 2 * r + k
            misfit[k, r : r + 1, :] = rows[0, k : k + 1, :] - sums[t : t + 1, :]
    picked = [jnp.where(live[...] > 0.0, sums[16:24] * sums[8 * r : 8 * r + 8], 0.0) for r in range(2)]
    pieces = [split(v) for v in picked]
    left = jnp.concatenate([pieces[0][0], pieces[1][0], pieces[0][1], pieces[1][1]], axis=0)
    block = lax.broadcasted_iota(jnp.int32, (BLOCKS, NODES), 0)
    sums = [jnp.zeros((BLOCKS, NODES), F32) for _ in range(2)]
    for b in range(BLOCKS):
        product = jnp.dot(left, matrix[b], preferred_element_type=F32)
        for r in range(2):
            both = product[8 * r : 8 * r + 8] + product[16 + 8 * r : 24 + 8 * r]
            sums[r] = jnp.where(block == b, both, sums[r])
    low = half_lanes((8, W))
    for j in range(4):
        one, two = sums[0][:, j * W : j * W + W], sums[1][:, j * W : j * W + W]
        update[pl.ds(2 * j, 8, stride=8), :] = jnp.where(low, one, swap_halves(two))
        update[pl.ds(2 * j + 1, 8, stride=8), :] = jnp.where(low, swap_halves(one), two)
    out[...] = smooth[...]
    copy.wait()
    for b in range(BLOCKS):
        n = node_block[0, b]
        out[n] = out[n] + update[8 * b : 8 * b + 8, :]


def shape(*dims, dtype=F32):
    return jax.ShapeDtypeStruct(dims, dtype)


def call(kernel, outs, ins, name, scratch=()):
    return pl.pallas_call(
        kernel,
        out_shape=outs,
        in_specs=ins,
        out_specs=(VMEM,) * len(outs),
        scratch_shapes=scratch,
        compiler_params=pltpu.CompilerParams(vmem_limit_bytes=24 * 1024 * 1024),
        name=name,
    )


def shards(
    noise, classes, table, obs_matrix, node_block, sample_block, sample_count, drill_data, obs_gain
):
    noise, classes, table, matrix, blocks, owner, count, drill, gain = [
        pltpu.with_memory_space_constraint(a, pltpu.HBM)
        for a in (
            noise, classes, table, obs_matrix, node_block, sample_block, sample_count, drill_data, obs_gain
        )
    ]
    odd, even, names = call(
        edge_y_kernel,
        (shape(X + 1, 4, W), shape(X + 1, 4, W), shape(8, W)),
        [HBM] * 3,
        "edge_y",
        [
            pltpu.VMEM((2, X, 8, W), F32),
            pltpu.VMEM((2, X, 8, Z), jnp.int32),
            pltpu.SMEM((BLOCKS,), jnp.int32),
            pltpu.SemaphoreType.DMA((5,)),
        ],
    )(noise, classes, owner)
    odd = permute(odd, ("x", "y", "core"), odd_along_y)
    even = permute(even, ("y", "core"), even_pair)
    field, kinds, tables = call(
        prepare_kernel,
        (shape(X, YP, W), shape(X, YP, W), shape(27, 8, W)),
        [HBM] * 3,
        "prepare",
        [
            pltpu.VMEM((X, Y, W), F32),
            pltpu.VMEM((X, Y, Z), jnp.int32),
            pltpu.VMEM((8, 27), F32),
            pltpu.SemaphoreType.DMA((3,)),
        ],
    )(noise, classes, table)
    field, kinds, odd, even, lists = call(
        edge_x_kernel,
        (shape(X, YP, W), shape(X, YP, W), shape(MESSAGE, W), shape(MESSAGE, W), shape(4, W)),
        [VMEM] * 6,
        "edge_x",
        [pltpu.VMEM((27, YP, W), F32), pltpu.VMEM((3, 3, YP, W), F32)],
    )(odd, even, field, kinds, names, tables)
    odd = permute(odd, ("x", "zh", "core"), odd_along_x)
    even = permute(even, ("x", "zh"), even_pair)
    weights, first, second, third, middle, matrix, rows, other, live, blocks = call(
        interior_kernel,
        (
            shape(27, X, YP, W),
            shape(3, X, YP, W),
            shape(3, 6, YP, W),
            shape(3, 4, YP, W),
            shape(8, 8, W),
            shape(BLOCKS, SAMPLES, NODES, dtype=jnp.bfloat16),
            shape(2, 2, SAMPLES),
            shape(8, SAMPLES),
            shape(BLOCKS, SAMPLES),
            shape(8, W, dtype=jnp.int32),
        ),
        [VMEM] * 3 + [HBM] * 6,
        "interior",
        [pltpu.SMEM((3, BLOCKS), jnp.int32), pltpu.SemaphoreType.DMA((6,))],
    )(field, kinds, tables, matrix, drill, gain, blocks, count, owner)
    halo_scratch = [
        pltpu.VMEM((YP, W), F32),
        pltpu.VMEM((27, YP, W), F32),
        pltpu.VMEM((3, 2, YP, W), F32),
        pltpu.VMEM((3, 3, YP, W), F32),
        pltpu.VMEM((3, 3, YP, W), F32),
    ]
    (lower,) = call(lower_kernel, (shape(12, 8, W),), [VMEM] * 7, "lower", halo_scratch)(
        kinds, odd, weights, first, second, third, tables
    )
    index_scratch = [pltpu.SMEM((1, W), jnp.int32), pltpu.SemaphoreType.DMA]
    smooth, payload, lists = call(
        finish_kernel,
        (shape(32, 8, W), shape(ROWS, SAMPLES), shape(8, W)),
        [VMEM] * 14,
        "finish",
        halo_scratch + [pltpu.VMEM((64, W), F32)] + index_scratch,
    )(
        kinds, even, lists, weights, first, second, third, middle, lower, tables, matrix,
        other, live, blocks,
    )
    here = lax.all_to_all(
        jnp.broadcast_to(payload[None], (16, ROWS, SAMPLES)), ("x", "y"), 0, 0, tiled=True
    )
    keep, send = call(
        collect_kernel, (shape(2, 32, SAMPLES), shape(2, 32, SAMPLES)), [VMEM] * 2, "collect"
    )(lists, here)
    near = permute(send, ("core",), lambda c: (c ^ 1,))
    far = permute(keep[1] + near[1], ("zh",), lambda z: (z ^ 1,))
    out, misfit = call(
        update_kernel,
        (shape(32, 8, W), shape(2, 2, SAMPLES)),
        [VMEM] * 8,
        "update",
        [pltpu.VMEM((64, W), F32)] + index_scratch,
    )(keep, near, far, smooth, matrix, rows, live, blocks)
    return out.reshape(X, Y, W), misfit


def solution(mesh):
    fine = Mesh(
        mesh.devices.reshape(4, 4, 2, 4, 2), ("real", "x", "zh", "y", "core")
    )
    sx, sy = ("x", "zh"), ("y", "core")
    both = sx + sy
    in_specs = (
        P(sx, sy, "real"),
        P(sx, sy, None),
        P(),
        P(both, None, None),
        P(both),
        P(both),
        P(both),
        P(both, None),
        P(both, None),
    )
    out_specs = (P(sx, sy, "real"), P(both, "real", None))
    return jax.shard_map(shards, mesh=fine, in_specs=in_specs, out_specs=out_specs, check_vma=False)
```

```python
import itertools

import jax
import jax.numpy as jnp
from jax import lax
from jax.experimental import pallas as pl
from jax.experimental.pallas import tpu as pltpu
from jax.sharding import Mesh, PartitionSpec as P

CHEB = (0.6, 0.5, 0.3, 0.2)
X, Y, Z = 8, 32, 64
W = 2 * Z
YP = 40
OFF = 4
BLOCKS = 8
SAMPLES = 256
NODES = 512
GROUPS = 11
MESSAGE = 136
F32 = jnp.float32
VMEM = pl.BlockSpec(memory_space=pltpu.VMEM)
HBM = pl.BlockSpec(memory_space=pltpu.HBM)
SIZES = {"x": 4, "zh": 2, "y": 4, "core": 2}


def permute(value, axes, target):
    dims = [SIZES[a] for a in axes]

    def flat(place):
        number = 0
        for coordinate, size in zip(place, dims):
            number = number * size + coordinate
        return number

    pairs = []
    for place in itertools.product(*[range(d) for d in dims]):
        other = target(*place)
        if other is not None:
            pairs.append((flat(place), flat(other)))
    return lax.ppermute(value, axes if len(axes) > 1 else axes[0], pairs)


def even_pair(a, b):
    return (a, b ^ 1)


def odd_pair(a, b):
    if b == 1:
        return (a + 1, 0) if a < 3 else None
    return (a - 1, 1) if a > 0 else None


def odd_along_x(x, zh, core):
    other = odd_pair(x, zh)
    return other + (core,) if other else (x, zh, core ^ 1)


def odd_along_y(x, y, core):
    other = odd_pair(y, core)
    return (x,) + other if other else (x ^ 1, y, core)


def half_lanes(shape):
    return lax.broadcasted_iota(jnp.int32, shape, len(shape) - 1) < Z


def swap_halves(value):
    return pltpu.roll(value, Z, axis=value.ndim - 1)


def pack(first, second):
    return jnp.where(half_lanes(first.shape), first, second)


def unpack(row):
    low = half_lanes(row.shape)
    other = swap_halves(row)
    return jnp.where(low, row, other), jnp.where(low, other, row)


def whereabouts():
    x, zh, y, core = [lax.axis_index(axis) for axis in ("x", "zh", "y", "core")]
    return zh, core, 4 * x + y, ((x * 2 + zh) * 4 + y) * 2 + core


def has_odd_pair(outer, inner):
    return lax.axis_index(outer) != 3 * lax.axis_index(inner)


def edge_y_kernel(
    noise_far, classes_far, owner_far,
    odd, even, names,
    noise_edges, class_edges, owner, sems,
):
    copies = [
        pltpu.make_async_copy(noise_far.at[:, 0:8, :], noise_edges.at[0], sems.at[0]),
        pltpu.make_async_copy(noise_far.at[:, Y - 8 : Y, :], noise_edges.at[1], sems.at[1]),
        pltpu.make_async_copy(classes_far.at[:, 0:8, :], class_edges.at[0], sems.at[2]),
        pltpu.make_async_copy(classes_far.at[:, Y - 8 : Y, :], class_edges.at[1], sems.at[3]),
        pltpu.make_async_copy(owner_far, owner, sems.at[4]),
    ]
    for copy in copies:
        copy.start()
    for copy in copies:
        copy.wait()
    core = whereabouts()[1]
    lane = lax.broadcasted_iota(jnp.int32, (8, W), 1)
    own = jnp.zeros((8, W), F32)
    for b in range(BLOCKS):
        own = jnp.where(lane == b, (owner[b] + 1).astype(F32), own)
    names[...] = own
    odd[X] = own[0:4]
    even[X] = own[0:4]

    def message(out, end, start, one, two):
        out[0:X, 0:3, :] = noise_edges[end, :, start : start + 3, :]
        kinds = (class_edges[end] + 1).astype(F32)
        out[0:X, 3:4, :] = jnp.concatenate([kinds[:, one : one + 1], kinds[:, two : two + 1]], axis=-1)

    @pl.when(core == 0)
    def _():
        message(even, 1, 5, 6, 7)
        message(odd, 0, 0, 0, 1)

    @pl.when(core == 1)
    def _():
        message(even, 0, 0, 0, 1)
        message(odd, 1, 5, 6, 7)


def prepare_kernel(
    noise_far, classes_far, table, field, kinds, tables, noise, classes, held_table, sems
):
    copies = [
        pltpu.make_async_copy(noise_far, noise, sems.at[0]),
        pltpu.make_async_copy(classes_far, classes, sems.at[1]),
        pltpu.make_async_copy(table, held_table, sems.at[2]),
    ]
    for copy in copies:
        copy.start()
    for copy in copies:
        copy.wait()
    half = whereabouts()[0]
    for out in (field, kinds):
        out[:, 0:8, :] = jnp.zeros((X, 8, W), F32)
        out[:, 32:40, :] = jnp.zeros((X, 8, W), F32)
    for x in range(X):
        true = mirrored(x, half)
        field[x, OFF : OFF + Y, :] = noise[true]
        kind = (classes[true] + 1).astype(F32)
        kinds[x, OFF : OFF + Y, :] = jnp.concatenate([kind, kind], axis=-1)
    spread_table(held_table, half, tables)


def edge_x_kernel(
    odd_in, even_in, field_in, kinds_in, names, tables,
    field, kinds, odd, even, lists,
    weights, moved,
):
    half, core = whereabouts()[0:2]
    field[...] = field_in[...]
    kinds[...] = kinds_in[...]
    lists[0:4] = names[0:4]
    lists[1:2] = even_in[X, 0:1, :]

    inside = has_odd_pair("y", "core")

    def sides(low, high):
        for x in range(X):
            true = mirrored(x, half)
            for message, start, one in ((low, 1, 2), (high, 36, 36)):
                held = message[true]
                if message is odd_in:
                    held = jnp.where(inside, held, 0.0)
                field[x, start : start + 3, :] = held[0:3]
                first, second = unpack(held[3:4])
                kinds[x, one : one + 1, :] = first
                kinds[x, one + 1 : one + 2, :] = second

    @pl.when(core == 0)
    def _():
        sides(odd_in, even_in)

    @pl.when(core == 1)
    def _():
        sides(even_in, odd_in)

    for out, row, step in ((odd, 0, 1), (even, X - 1, -1)):
        def put(o, part, value):
            weights[o, part, :] = value

        weigh(kinds[row + step], tables, put)
        for n in range(3):
            for c, value in enumerate(lean(field[row + n * step])):
                moved[c, n] = value
        second = operate(
            lambda o: weights[o],
            lambda a, c: moved[c, a if step == 1 else 2 - a],
            jnp.minimum(kinds[row + step], 1.0),
        )
        out[0:38, :] = field[row][1:39]
        out[38:76, :] = field[row + step][1:39]
        out[76:112, :] = second[2:38]
        kind = kinds[row]
        out[112:130, :] = pack(kind[2:20], kind[20:38])
        out[130:132, :] = lists[0:2]
        out[132:MESSAGE, :] = jnp.zeros((MESSAGE - 132, W), F32)


def mirrored(x, half):
    return x + half * (X - 1 - 2 * x)


def rows_by_column(block_rows):
    return [block_rows[pl.ds(c, 8, stride=8), :] for c in range(8)]


def split(value):
    high = value.astype(jnp.bfloat16)
    low = (value - high.astype(F32)).astype(jnp.bfloat16)
    return high, low


def weigh(kinds, table, put):
    for b in range(3):
        moved = kinds if b == 1 else pltpu.roll(kinds, (b - 1) % YP, axis=0)
        index = jnp.maximum(moved.astype(jnp.int32) - 1, 0)
        for g in range(YP // 8):
            part = index[8 * g : 8 * g + 8]
            for a in range(3):
                for c in range(3):
                    o = 9 * a + 3 * b + c
                    put(
                        o,
                        pl.ds(8 * g, 8),
                        jnp.take_along_axis(table[o], part, axis=0, mode="promise_in_bounds"),
                    )


def spread_table(table, half, out):
    held = table[...]
    columns = [jnp.broadcast_to(held[:, o : o + 1], (8, W)) for o in range(27)]
    for o in range(27):
        out[o] = jnp.where(half == 0, columns[o], columns[o + 9 * (2 - 2 * (o // 9))])


def lean(row):
    lanes = lax.broadcasted_iota(jnp.int32, (YP, W), 1) % Z
    below = jnp.where(lanes > 0, pltpu.roll(row, 1, axis=1), 0.0)
    above = jnp.where(lanes < Z - 1, pltpu.roll(row, W - 1, axis=1), 0.0)
    return below, row, above


def operate(weight, moved, inside):
    sums = []
    for b in range(3):
        total = None
        for a in range(3):
            for c in range(3):
                term = weight(9 * a + 3 * b + c) * moved(a, c)
                total = term if total is None else total + term
        sums.append(total)
    result = pltpu.roll(sums[0], 1, axis=0) + sums[1] + pltpu.roll(sums[2], YP - 1, axis=0)
    return result * inside


def interior_kernel(
    field, kinds, tables, matrix, drill, gain, node_block, count, owner,
    weights, first, second, third, smooth, held_matrix, turned, held_rows, other, live, blocks,
    scalars, sems,
):
    copies = [
        pltpu.make_async_copy(matrix, held_matrix, sems.at[0]),
        pltpu.make_async_copy(drill, held_rows.at[0], sems.at[1]),
        pltpu.make_async_copy(gain, held_rows.at[1], sems.at[2]),
        pltpu.make_async_copy(node_block, scalars.at[0], sems.at[3]),
        pltpu.make_async_copy(count, scalars.at[1], sems.at[4]),
        pltpu.make_async_copy(owner, scalars.at[2], sems.at[5]),
    ]
    for copy in copies:
        copy.start()
    plane = whereabouts()[2]
    for x in range(X):
        def put(o, rows, value, x=x):
            weights[o, x, rows, :] = value

        weigh(kinds[x], tables, put)
        for c, value in enumerate(lean(field[x])):
            first[c, x] = value

    def step(source, start, x):
        return operate(
            lambda o: weights[o, x],
            lambda a, c: source[c, x + a - 1 - start],
            jnp.minimum(kinds[x], 1.0),
        )

    for x in range(1, 7):
        for c, value in enumerate(lean(step(first, 0, x))):
            second[c, x - 1] = value
    for x in range(2, 6):
        value = 2.0 * step(second, 1, x) - first[1, x]
        for c, value in enumerate(lean(value)):
            third[c, x - 2] = value
    for x in range(3, 5):
        fourth = 2.0 * step(third, 2, x) - second[1, x - 1]
        result = (
            CHEB[0] * first[1, x] + CHEB[1] * second[1, x - 1] + CHEB[2] * third[1, x - 2] + CHEB[3] * fourth
        )
        for g in range(4):
            smooth[4 * (x - 3) + g] = result[OFF + 8 * g : OFF + 8 * g + 8]
    for copy in copies:
        copy.wait()
    for b in range(BLOCKS):
        turned[b] = held_matrix[b].T
    other[...] = jnp.zeros((8, SAMPLES), F32)
    for k in range(2):
        for h in range(2):
            for kind in range(2):
                row = 4 * kind + 2 * k + h
                other[row : row + 1, 0:W] = held_rows[kind, k : k + 1, h * W : h * W + W]
    lane = lax.broadcasted_iota(jnp.int32, (8, W), 1)
    names = jnp.zeros((8, W), F32)
    places = jnp.zeros((8, W), jnp.int32)
    limit = jnp.zeros((BLOCKS, SAMPLES), jnp.int32)
    block = lax.broadcasted_iota(jnp.int32, (BLOCKS, SAMPLES), 0)
    for b in range(BLOCKS):
        names = jnp.where(lane == 8 * plane + b, (scalars[2, b] + 1).astype(F32), names)
        places = jnp.where(lane == b, scalars[0, b], places)
        limit = jnp.where(block == b, scalars[1, b], limit)
    other[0:1, W : 2 * W] = names[0:1]
    blocks[...] = places
    sample = lax.broadcasted_iota(jnp.int32, (BLOCKS, SAMPLES), 1)
    live[...] = (sample < limit).astype(F32)


def fill_halo(message, inside, tables, halo_kinds, halo_weights, halo_first, edge_second):
    held = jnp.where(inside, message[...], 0.0)
    one, two = [jnp.zeros((n, W), F32) for n in (1, 2)]
    low, high = unpack(held[112:130])
    halo_kinds[...] = jnp.concatenate([two, low, high, two], axis=0)

    def put(o, part, value):
        halo_weights[o, part, :] = value

    weigh(halo_kinds[...], tables, put)
    for i in range(2):
        for c, value in enumerate(lean(jnp.concatenate([one, held[38 * i : 38 * i + 38], one], axis=0))):
            halo_first[c, i] = value
    for c, value in enumerate(lean(jnp.concatenate([two, held[76:112], two], axis=0))):
        edge_second[c, 2] = value


def side(
    high, kinds, weights, first, second, third, halo_kinds, halo_weights, halo_first, edge_second, edge_third, put
):
    def beyond(x):
        return x - X if high else -1 - x

    def weight(x):
        if 0 <= x < X:
            return (lambda o: weights[o, x]), jnp.minimum(kinds[x], 1.0)
        return (lambda o: halo_weights[o]), jnp.minimum(halo_kinds[...], 1.0)

    def at_first(x, c):
        return first[c, x] if 0 <= x < X else halo_first[c, beyond(x)]

    def at_second(x, c):
        return second[c, x - 1] if 1 <= x < 7 else edge_second[c, beyond(x) + 1]

    def at_third(x, c):
        return third[c, x - 2] if 2 <= x < 6 else edge_third[c, beyond(x) + 2]

    def step(at, x):
        of, inside = weight(x)
        return operate(of, lambda a, c: at(x + a - 1, c), inside)

    def row(n):
        return X - 1 - n if high else n

    for n in (-1, 0):
        for c, value in enumerate(lean(step(at_first, row(n)))):
            edge_second[c, -n] = value
    for n in (-1, 0, 1):
        value = 2.0 * step(at_second, row(n)) - at_first(row(n), 1)
        for c, value in enumerate(lean(value)):
            edge_third[c, 1 - n] = value
    for n in (0, 1, 2):
        x = row(n)
        fourth = 2.0 * step(at_third, x) - at_second(x, 1)
        result = (
            CHEB[0] * at_first(x, 1) + CHEB[1] * at_second(x, 1) + CHEB[2] * at_third(x, 1) + CHEB[3] * fourth
        )
        for g in range(4):
            put(x, g, result[OFF + 8 * g : OFF + 8 * g + 8])


def lower_kernel(
    kinds, edges, weights, first, second, third, tables,
    lower,
    halo_kinds, halo_weights, halo_first, edge_second, edge_third,
):
    fill_halo(edges, has_odd_pair("x", "zh"), tables, halo_kinds, halo_weights, halo_first, edge_second)

    def put(x, g, value):
        lower[4 * x + g] = value

    side(
        False, kinds, weights, first, second, third,
        halo_kinds, halo_weights, halo_first, edge_second, edge_third, put,
    )


def finish_kernel(
    kinds, edges, near, weights, first, second, third, middle, lower, tables, turned, other, live, blocks,
    smooth, payload, lists,
    halo_kinds, halo_weights, halo_first, edge_second, edge_third, chosen, node_block, sem,
):
    copy = pltpu.make_async_copy(blocks.at[0:1], node_block, sem)
    copy.start()
    half = whereabouts()[0]
    lists[0:4] = near[0:4]
    lists[4:8] = jnp.zeros((4, W), F32)
    lists[2:4] = edges[130:132]
    fill_halo(edges, True, tables, halo_kinds, halo_weights, halo_first, edge_second)

    def put(x, g, value):
        smooth[4 * mirrored(x, half) + g] = value

    side(
        True, kinds, weights, first, second, third,
        halo_kinds, halo_weights, halo_first, edge_second, edge_third, put,
    )
    for g in range(4):
        for x in (0, 1, 2):
            put(x, g, lower[4 * x + g])
        for x in (3, 4):
            put(x, g, middle[4 * (x - 3) + g])

    copy.wait()
    for b in range(BLOCKS):
        chosen[pl.ds(8 * b, 8), :] = smooth[node_block[0, b]]
    columns = rows_by_column(chosen)
    low = half_lanes((8, W))
    parts = ([], [])
    for j in range(4):
        one, two = columns[2 * j], columns[2 * j + 1]
        parts[0].append(jnp.where(low, one, swap_halves(two)))
        parts[1].append(jnp.where(low, swap_halves(one), two))
    values = [jnp.concatenate(p, axis=1) for p in parts]
    pieces = [split(v) for v in values]
    left = jnp.concatenate([pieces[0][0], pieces[1][0], pieces[0][1], pieces[1][1]], axis=0)
    block = lax.broadcasted_iota(jnp.int32, (BLOCKS, SAMPLES), 0)
    sums = [jnp.zeros((BLOCKS, SAMPLES), F32) for _ in range(2)]
    for b in range(BLOCKS):
        product = jnp.dot(left, turned[b], preferred_element_type=F32)
        for r in range(2):
            both = product[8 * r : 8 * r + 8] + product[16 + 8 * r : 24 + 8 * r]
            sums[r] = jnp.where(block == b, both, sums[r])
    tiles = []
    for r in range(2):
        told = jnp.where(live[...] > 0.0, sums[r], 0.0)
        tiles += [told[:, 0:W], told[:, W : 2 * W]]
    tiles.append(other[:, 0:W])
    for n, tile in enumerate(tiles):
        payload[2 * n] = tile[0:4]
        payload[2 * n + 1] = tile[4:8]
    payload[10] = other[0:4, W : 2 * W]


def collect_kernel(lists, here, keep, send):
    names = here[0, 10]
    for n in range(1, 16):
        names = names + here[n, 10]
    names = jnp.broadcast_to(names[0:1], (8, W))
    lane = lax.broadcasted_iota(jnp.int32, (8, W), 1)
    row = lax.broadcasted_iota(jnp.int32, (8, W), 0)
    hits, spots = [], []
    half, core, _, me = whereabouts()
    for member in range(4):
        tile = me ^ (1 if member & 1 else 0) ^ (8 if member & 2 else 0)
        held = jnp.broadcast_to(lists[member : member + 1], (8, W))
        name = jnp.sum(jnp.where(lane == row, held, 0.0), axis=1, keepdims=True)
        name = jnp.broadcast_to(name, (8, W))
        hits.append(name == names)
        hits.append((2 * tile + 1 + (row & 1)).astype(F32) == names)
        block = name.astype(jnp.int32) - 1
        holder = block >> 1
        spot = ((holder >> 4) * 4 + ((holder >> 1) & 3)) * 8 + 2 * (block & 1)
        mine = ((holder & 1) == core) & (((holder >> 3) & 1) == half)
        spots.append(jnp.where(mine, spot, -1024))
    hit = jnp.concatenate([h.astype(F32) for h in hits], axis=0).astype(jnp.bfloat16)
    spots = jnp.concatenate(spots, axis=0)
    lane = lax.broadcasted_iota(jnp.int32, (32, W), 1)
    choose = jnp.concatenate(
        [(lane == spots + 4 * kind + h).astype(F32) for kind in range(2) for h in range(2)], axis=0
    ).astype(jnp.bfloat16)

    def column(tile):
        return jnp.concatenate([here[n, 2 * tile + k] for n in range(16) for k in range(2)], axis=0)

    def gather(left, data):
        high, low = split(data)
        return jnp.dot(left, high, preferred_element_type=F32) + jnp.dot(
            left, low, preferred_element_type=F32
        )

    totals = [
        gather(hit, jnp.concatenate([column(2 * r), column(2 * r + 1)], axis=1)) for r in range(2)
    ]
    found = gather(choose, column(4))
    row = lax.broadcasted_iota(jnp.int32, (8, SAMPLES), 0)
    for member in range(4):
        out = (send if member & 1 else keep).at[member // 2]
        drill, gain = [
            jnp.concatenate(
                [found[64 * kind + 32 * h + 8 * member : 64 * kind + 32 * h + 8 * member + 8] for h in range(2)],
                axis=1,
            )
            for kind in range(2)
        ]
        for r in range(2):
            out[8 * r : 8 * r + 8, :] = drill - totals[r][16 * member : 16 * member + 8]
        out[16:24, :] = gain
        own = [totals[r][16 * member + 8 : 16 * member + 16] for r in range(2)]
        out[24:32, :] = jnp.where(row < 2, own[0], own[1])


def update_kernel(
    keep, near, far, smooth, matrix, rows, live, blocks,
    out, misfit,
    update, node_block, sem,
):
    copy = pltpu.make_async_copy(blocks.at[0:1], node_block, sem)
    copy.start()
    sums = keep[0] + near[0] + far[...]
    for k in range(2):
        for r in range(2):
            t = 24 + 2 * r + k
            misfit[k, r : r + 1, :] = rows[0, k : k + 1, :] - sums[t : t + 1, :]
    picked = [jnp.where(live[...] > 0.0, sums[16:24] * sums[8 * r : 8 * r + 8], 0.0) for r in range(2)]
    pieces = [split(v) for v in picked]
    left = jnp.concatenate([pieces[0][0], pieces[1][0], pieces[0][1], pieces[1][1]], axis=0)
    block = lax.broadcasted_iota(jnp.int32, (BLOCKS, NODES), 0)
    sums = [jnp.zeros((BLOCKS, NODES), F32) for _ in range(2)]
    for b in range(BLOCKS):
        product = jnp.dot(left, matrix[b], preferred_element_type=F32)
        for r in range(2):
            both = product[8 * r : 8 * r + 8] + product[16 + 8 * r : 24 + 8 * r]
            sums[r] = jnp.where(block == b, both, sums[r])
    low = half_lanes((8, W))
    for j in range(4):
        one, two = sums[0][:, j * W : j * W + W], sums[1][:, j * W : j * W + W]
        update[pl.ds(2 * j, 8, stride=8), :] = jnp.where(low, one, swap_halves(two))
        update[pl.ds(2 * j + 1, 8, stride=8), :] = jnp.where(low, swap_halves(one), two)
    out[...] = smooth[...]
    copy.wait()
    for b in range(BLOCKS):
        n = node_block[0, b]
        out[n] = out[n] + update[8 * b : 8 * b + 8, :]


def shape(*dims, dtype=F32):
    return jax.ShapeDtypeStruct(dims, dtype)


def call(kernel, outs, ins, name, scratch=()):
    return pl.pallas_call(
        kernel,
        out_shape=outs,
        in_specs=ins,
        out_specs=(VMEM,) * len(outs),
        scratch_shapes=scratch,
        compiler_params=pltpu.CompilerParams(vmem_limit_bytes=24 * 1024 * 1024),
        name=name,
    )


def shards(
    noise, classes, table, obs_matrix, node_block, sample_block, sample_count, drill_data, obs_gain
):
    noise, classes, table, matrix, blocks, owner, count, drill, gain = [
        pltpu.with_memory_space_constraint(a, pltpu.HBM)
        for a in (
            noise, classes, table, obs_matrix, node_block, sample_block, sample_count, drill_data, obs_gain
        )
    ]
    odd, even, names = call(
        edge_y_kernel,
        (shape(X + 1, 4, W), shape(X + 1, 4, W), shape(8, W)),
        [HBM] * 3,
        "edge_y",
        [
            pltpu.VMEM((2, X, 8, W), F32),
            pltpu.VMEM((2, X, 8, Z), jnp.int32),
            pltpu.SMEM((BLOCKS,), jnp.int32),
            pltpu.SemaphoreType.DMA((5,)),
        ],
    )(noise, classes, owner)
    odd = permute(odd, ("x", "y", "core"), odd_along_y)
    even = permute(even, ("y", "core"), even_pair)
    field, kinds, tables = call(
        prepare_kernel,
        (shape(X, YP, W), shape(X, YP, W), shape(27, 8, W)),
        [HBM] * 3,
        "prepare",
        [
            pltpu.VMEM((X, Y, W), F32),
            pltpu.VMEM((X, Y, Z), jnp.int32),
            pltpu.VMEM((8, 27), F32),
            pltpu.SemaphoreType.DMA((3,)),
        ],
    )(noise, classes, table)
    field, kinds, odd, even, lists = call(
        edge_x_kernel,
        (shape(X, YP, W), shape(X, YP, W), shape(MESSAGE, W), shape(MESSAGE, W), shape(4, W)),
        [VMEM] * 6,
        "edge_x",
        [pltpu.VMEM((27, YP, W), F32), pltpu.VMEM((3, 3, YP, W), F32)],
    )(odd, even, field, kinds, names, tables)
    odd = permute(odd, ("x", "zh", "core"), odd_along_x)
    even = permute(even, ("x", "zh"), even_pair)
    weights, first, second, third, middle, matrix, turned, rows, other, live, blocks = call(
        interior_kernel,
        (
            shape(27, X, YP, W),
            shape(3, X, YP, W),
            shape(3, 6, YP, W),
            shape(3, 4, YP, W),
            shape(8, 8, W),
            shape(BLOCKS, SAMPLES, NODES, dtype=jnp.bfloat16),
            shape(BLOCKS, NODES, SAMPLES, dtype=jnp.bfloat16),
            shape(2, 2, SAMPLES),
            shape(8, SAMPLES),
            shape(BLOCKS, SAMPLES),
            shape(8, W, dtype=jnp.int32),
        ),
        [VMEM] * 3 + [HBM] * 6,
        "interior",
        [pltpu.SMEM((3, BLOCKS), jnp.int32), pltpu.SemaphoreType.DMA((6,))],
    )(field, kinds, tables, matrix, drill, gain, blocks, count, owner)
    halo_scratch = [
        pltpu.VMEM((YP, W), F32),
        pltpu.VMEM((27, YP, W), F32),
        pltpu.VMEM((3, 2, YP, W), F32),
        pltpu.VMEM((3, 3, YP, W), F32),
        pltpu.VMEM((3, 3, YP, W), F32),
    ]
    (lower,) = call(lower_kernel, (shape(12, 8, W),), [VMEM] * 7, "lower", halo_scratch)(
        kinds, odd, weights, first, second, third, tables
    )
    index_scratch = [pltpu.SMEM((1, W), jnp.int32), pltpu.SemaphoreType.DMA]
    smooth, payload, lists = call(
        finish_kernel,
        (shape(32, 8, W), shape(GROUPS, 4, W), shape(8, W)),
        [VMEM] * 14,
        "finish",
        halo_scratch + [pltpu.VMEM((64, W), F32)] + index_scratch,
    )(
        kinds, even, lists, weights, first, second, third, middle, lower, tables, turned,
        other, live, blocks,
    )
    here = lax.all_to_all(
        jnp.broadcast_to(payload[None], (16, GROUPS, 4, W)), ("x", "y"), 0, 0, tiled=True
    )
    keep, send = call(
        collect_kernel, (shape(2, 32, SAMPLES), shape(2, 32, SAMPLES)), [VMEM] * 2, "collect"
    )(lists, here)
    near = permute(send, ("core",), lambda c: (c ^ 1,))
    far = permute(keep[1] + near[1], ("zh",), lambda z: (z ^ 1,))
    out, misfit = call(
        update_kernel,
        (shape(32, 8, W), shape(2, 2, SAMPLES)),
        [VMEM] * 8,
        "update",
        [pltpu.VMEM((64, W), F32)] + index_scratch,
    )(keep, near, far, smooth, matrix, rows, live, blocks)
    return out.reshape(X, Y, W), misfit


def solution(mesh):
    fine = Mesh(
        mesh.devices.reshape(4, 4, 2, 4, 2), ("real", "x", "zh", "y", "core")
    )
    sx, sy = ("x", "zh"), ("y", "core")
    both = sx + sy
    in_specs = (
        P(sx, sy, "real"),
        P(sx, sy, None),
        P(),
        P(both, None, None),
        P(both),
        P(both),
        P(both),
        P(both, None),
        P(both, None),
    )
    out_specs = (P(sx, sy, "real"), P(both, "real", None))
    return jax.shard_map(shards, mesh=fine, in_specs=in_specs, out_specs=out_specs, check_vma=False)
```

```python
import itertools

import jax
import jax.numpy as jnp
from jax import lax
from jax.experimental import pallas as pl
from jax.experimental.pallas import tpu as pltpu
from jax.sharding import Mesh, PartitionSpec as P

CHEB = (0.6, 0.5, 0.3, 0.2)
X, Y, Z = 8, 32, 64
W = 2 * Z
YP = 40
OFF = 4
BLOCKS = 8
SAMPLES = 256
NODES = 512
GROUPS = 11
MESSAGE = 136
F32 = jnp.float32
VMEM = pl.BlockSpec(memory_space=pltpu.VMEM)
HBM = pl.BlockSpec(memory_space=pltpu.HBM)
SIZES = {"x": 4, "zh": 2, "y": 4, "core": 2}


def permute(value, axes, target):
    dims = [SIZES[a] for a in axes]

    def flat(place):
        number = 0
        for coordinate, size in zip(place, dims):
            number = number * size + coordinate
        return number

    pairs = []
    for place in itertools.product(*[range(d) for d in dims]):
        other = target(*place)
        if other is not None:
            pairs.append((flat(place), flat(other)))
    return lax.ppermute(value, axes if len(axes) > 1 else axes[0], pairs)


def even_pair(a, b):
    return (a, b ^ 1)


def odd_pair(a, b):
    if b == 1:
        return (a + 1, 0) if a < 3 else None
    return (a - 1, 1) if a > 0 else None


def odd_along_x(x, zh, core):
    other = odd_pair(x, zh)
    return other + (core,) if other else (x, zh, core ^ 1)


def odd_along_y(x, y, core):
    other = odd_pair(y, core)
    return (x,) + other if other else (x ^ 1, y, core)


def half_lanes(shape):
    return lax.broadcasted_iota(jnp.int32, shape, len(shape) - 1) < Z


def swap_halves(value):
    return pltpu.roll(value, Z, axis=value.ndim - 1)


def pack(first, second):
    return jnp.where(half_lanes(first.shape), first, second)


def unpack(row):
    low = half_lanes(row.shape)
    other = swap_halves(row)
    return jnp.where(low, row, other), jnp.where(low, other, row)


def whereabouts():
    x, zh, y, core = [lax.axis_index(axis) for axis in ("x", "zh", "y", "core")]
    return zh, core, 4 * x + y, ((x * 2 + zh) * 4 + y) * 2 + core


def has_odd_pair(outer, inner):
    return lax.axis_index(outer) != 3 * lax.axis_index(inner)


def edge_y_kernel(
    noise_far, classes_far, owner_far,
    odd, even, names,
    noise_edges, class_edges, owner, sems,
):
    copies = [
        pltpu.make_async_copy(noise_far.at[:, 0:8, :], noise_edges.at[0], sems.at[0]),
        pltpu.make_async_copy(noise_far.at[:, Y - 8 : Y, :], noise_edges.at[1], sems.at[1]),
        pltpu.make_async_copy(classes_far.at[:, 0:8, :], class_edges.at[0], sems.at[2]),
        pltpu.make_async_copy(classes_far.at[:, Y - 8 : Y, :], class_edges.at[1], sems.at[3]),
        pltpu.make_async_copy(owner_far, owner, sems.at[4]),
    ]
    for copy in copies:
        copy.start()
    for copy in copies:
        copy.wait()
    core = whereabouts()[1]
    lane = lax.broadcasted_iota(jnp.int32, (8, W), 1)
    own = jnp.zeros((8, W), F32)
    for b in range(BLOCKS):
        own = jnp.where(lane == b, (owner[b] + 1).astype(F32), own)
    names[...] = own
    odd[X] = own[0:4]
    even[X] = own[0:4]

    def message(out, end, start, one, two):
        out[0:X, 0:3, :] = noise_edges[end, :, start : start + 3, :]
        kinds = (class_edges[end] + 1).astype(F32)
        out[0:X, 3:4, :] = jnp.concatenate([kinds[:, one : one + 1], kinds[:, two : two + 1]], axis=-1)

    @pl.when(core == 0)
    def _():
        message(even, 1, 5, 6, 7)
        message(odd, 0, 0, 0, 1)

    @pl.when(core == 1)
    def _():
        message(even, 0, 0, 0, 1)
        message(odd, 1, 5, 6, 7)


def prepare_kernel(
    noise_far, classes_far, table, field, kinds, tables, noise, classes, held_table, sems
):
    copies = [
        pltpu.make_async_copy(noise_far, noise, sems.at[0]),
        pltpu.make_async_copy(classes_far, classes, sems.at[1]),
        pltpu.make_async_copy(table, held_table, sems.at[2]),
    ]
    for copy in copies:
        copy.start()
    for copy in copies:
        copy.wait()
    half = whereabouts()[0]
    for out in (field, kinds):
        out[:, 0:8, :] = jnp.zeros((X, 8, W), F32)
        out[:, 32:40, :] = jnp.zeros((X, 8, W), F32)
    for x in range(X):
        true = mirrored(x, half)
        field[x, OFF : OFF + Y, :] = noise[true]
        kind = (classes[true] + 1).astype(F32)
        kinds[x, OFF : OFF + Y, :] = jnp.concatenate([kind, kind], axis=-1)
    spread_table(held_table, half, tables)


def edge_x_kernel(
    odd_in, even_in, field_in, kinds_in, names, tables,
    field, kinds, odd, even, lists,
    weights, moved,
):
    half, core = whereabouts()[0:2]
    field[...] = field_in[...]
    kinds[...] = kinds_in[...]
    lists[0:4] = names[0:4]
    lists[1:2] = even_in[X, 0:1, :]

    inside = has_odd_pair("y", "core")

    def sides(low, high):
        for x in range(X):
            true = mirrored(x, half)
            for message, start, one in ((low, 1, 2), (high, 36, 36)):
                held = message[true]
                if message is odd_in:
                    held = jnp.where(inside, held, 0.0)
                field[x, start : start + 3, :] = held[0:3]
                first, second = unpack(held[3:4])
                kinds[x, one : one + 1, :] = first
                kinds[x, one + 1 : one + 2, :] = second

    @pl.when(core == 0)
    def _():
        sides(odd_in, even_in)

    @pl.when(core == 1)
    def _():
        sides(even_in, odd_in)

    for out, row, step in ((odd, 0, 1), (even, X - 1, -1)):
        def put(o, part, value):
            weights[o, part, :] = value

        weigh(kinds[row + step], tables, put)
        for n in range(3):
            for c, value in enumerate(lean(field[row + n * step])):
                moved[c, n] = value
        second = operate(
            lambda o: weights[o],
            lambda a, c: moved[c, a if step == 1 else 2 - a],
            jnp.minimum(kinds[row + step], 1.0),
        )
        out[0:38, :] = field[row][1:39]
        out[38:76, :] = field[row + step][1:39]
        out[76:112, :] = second[2:38]
        kind = kinds[row]
        out[112:130, :] = pack(kind[2:20], kind[20:38])
        out[130:132, :] = lists[0:2]
        out[132:MESSAGE, :] = jnp.zeros((MESSAGE - 132, W), F32)


def mirrored(x, half):
    return x + half * (X - 1 - 2 * x)


def rows_by_column(block_rows):
    return [block_rows[pl.ds(c, 8, stride=8), :] for c in range(8)]


def split(value):
    high = value.astype(jnp.bfloat16)
    low = (value - high.astype(F32)).astype(jnp.bfloat16)
    return high, low


def weigh(kinds, table, put):
    for b in range(3):
        moved = kinds if b == 1 else pltpu.roll(kinds, (b - 1) % YP, axis=0)
        index = jnp.maximum(moved.astype(jnp.int32) - 1, 0)
        for g in range(YP // 8):
            part = index[8 * g : 8 * g + 8]
            for a in range(3):
                for c in range(3):
                    o = 9 * a + 3 * b + c
                    put(
                        o,
                        pl.ds(8 * g, 8),
                        jnp.take_along_axis(table[o], part, axis=0, mode="promise_in_bounds"),
                    )


def spread_table(table, half, out):
    held = table[...]
    columns = [jnp.broadcast_to(held[:, o : o + 1], (8, W)) for o in range(27)]
    for o in range(27):
        out[o] = jnp.where(half == 0, columns[o], columns[o + 9 * (2 - 2 * (o // 9))])


def lean(row):
    lanes = lax.broadcasted_iota(jnp.int32, (YP, W), 1) % Z
    below = jnp.where(lanes > 0, pltpu.roll(row, 1, axis=1), 0.0)
    above = jnp.where(lanes < Z - 1, pltpu.roll(row, W - 1, axis=1), 0.0)
    return below, row, above


def operate(weight, moved, inside):
    sums = []
    for b in range(3):
        total = None
        for a in range(3):
            for c in range(3):
                term = weight(9 * a + 3 * b + c) * moved(a, c)
                total = term if total is None else total + term
        sums.append(total)
    result = pltpu.roll(sums[0], 1, axis=0) + sums[1] + pltpu.roll(sums[2], YP - 1, axis=0)
    return result * inside


def interior_kernel(
    field, kinds, tables, matrix, drill, gain, node_block, count, owner,
    weights, first, second, third, smooth, held_matrix, turned, held_rows, other, live, blocks,
    scalars, sems,
):
    copies = [
        pltpu.make_async_copy(matrix, held_matrix, sems.at[0]),
        pltpu.make_async_copy(drill, held_rows.at[0], sems.at[1]),
        pltpu.make_async_copy(gain, held_rows.at[1], sems.at[2]),
        pltpu.make_async_copy(node_block, scalars.at[0], sems.at[3]),
        pltpu.make_async_copy(count, scalars.at[1], sems.at[4]),
        pltpu.make_async_copy(owner, scalars.at[2], sems.at[5]),
    ]
    for copy in copies:
        copy.start()
    plane = whereabouts()[2]
    for x in range(X):
        def put(o, rows, value, x=x):
            weights[o, x, rows, :] = value

        weigh(kinds[x], tables, put)
        for c, value in enumerate(lean(field[x])):
            first[c, x] = value

    def step(source, start, x):
        return operate(
            lambda o: weights[o, x],
            lambda a, c: source[c, x + a - 1 - start],
            jnp.minimum(kinds[x], 1.0),
        )

    for x in range(1, 7):
        for c, value in enumerate(lean(step(first, 0, x))):
            second[c, x - 1] = value
    for x in range(2, 6):
        value = 2.0 * step(second, 1, x) - first[1, x]
        for c, value in enumerate(lean(value)):
            third[c, x - 2] = value
    for x in range(3, 5):
        fourth = 2.0 * step(third, 2, x) - second[1, x - 1]
        result = (
            CHEB[0] * first[1, x] + CHEB[1] * second[1, x - 1] + CHEB[2] * third[1, x - 2] + CHEB[3] * fourth
        )
        for g in range(4):
            smooth[4 * (x - 3) + g] = result[OFF + 8 * g : OFF + 8 * g + 8]
    for copy in copies:
        copy.wait()
    for b in range(BLOCKS):
        turned[b] = held_matrix[b].T
    other[...] = jnp.zeros((8, SAMPLES), F32)
    for k in range(2):
        for h in range(2):
            for kind in range(2):
                row = 4 * kind + 2 * k + h
                other[row : row + 1, 0:W] = held_rows[kind, k : k + 1, h * W : h * W + W]
    lane = lax.broadcasted_iota(jnp.int32, (8, W), 1)
    names = jnp.zeros((8, W), F32)
    places = jnp.zeros((8, W), jnp.int32)
    limit = jnp.zeros((BLOCKS, SAMPLES), jnp.int32)
    block = lax.broadcasted_iota(jnp.int32, (BLOCKS, SAMPLES), 0)
    for b in range(BLOCKS):
        names = jnp.where(lane == 8 * plane + b, (scalars[2, b] + 1).astype(F32), names)
        places = jnp.where(lane == b, scalars[0, b], places)
        limit = jnp.where(block == b, scalars[1, b], limit)
    other[0:1, W : 2 * W] = names[0:1]
    blocks[...] = places
    sample = lax.broadcasted_iota(jnp.int32, (BLOCKS, SAMPLES), 1)
    live[...] = (sample < limit).astype(F32)


def fill_halo(message, inside, tables, halo_kinds, halo_weights, halo_first, edge_second):
    held = jnp.where(inside, message[...], 0.0)
    one, two = [jnp.zeros((n, W), F32) for n in (1, 2)]
    low, high = unpack(held[112:130])
    halo_kinds[...] = jnp.concatenate([two, low, high, two], axis=0)

    def put(o, part, value):
        halo_weights[o, part, :] = value

    weigh(halo_kinds[...], tables, put)
    for i in range(2):
        for c, value in enumerate(lean(jnp.concatenate([one, held[38 * i : 38 * i + 38], one], axis=0))):
            halo_first[c, i] = value
    for c, value in enumerate(lean(jnp.concatenate([two, held[76:112], two], axis=0))):
        edge_second[c, 2] = value


def side(
    high, kinds, weights, first, second, third, halo_kinds, halo_weights, halo_first, edge_second, edge_third, put
):
    def beyond(x):
        return x - X if high else -1 - x

    def weight(x):
        if 0 <= x < X:
            return (lambda o: weights[o, x]), jnp.minimum(kinds[x], 1.0)
        return (lambda o: halo_weights[o]), jnp.minimum(halo_kinds[...], 1.0)

    def at_first(x, c):
        return first[c, x] if 0 <= x < X else halo_first[c, beyond(x)]

    def at_second(x, c):
        return second[c, x - 1] if 1 <= x < 7 else edge_second[c, beyond(x) + 1]

    def at_third(x, c):
        return third[c, x - 2] if 2 <= x < 6 else edge_third[c, beyond(x) + 2]

    def step(at, x):
        of, inside = weight(x)
        return operate(of, lambda a, c: at(x + a - 1, c), inside)

    def row(n):
        return X - 1 - n if high else n

    for n in (-1, 0):
        for c, value in enumerate(lean(step(at_first, row(n)))):
            edge_second[c, -n] = value
    for n in (-1, 0, 1):
        value = 2.0 * step(at_second, row(n)) - at_first(row(n), 1)
        for c, value in enumerate(lean(value)):
            edge_third[c, 1 - n] = value
    for n in (0, 1, 2):
        x = row(n)
        fourth = 2.0 * step(at_third, x) - at_second(x, 1)
        result = (
            CHEB[0] * at_first(x, 1) + CHEB[1] * at_second(x, 1) + CHEB[2] * at_third(x, 1) + CHEB[3] * fourth
        )
        for g in range(4):
            put(x, g, result[OFF + 8 * g : OFF + 8 * g + 8])


def lower_kernel(
    kinds, edges, weights, first, second, third, tables,
    lower,
    halo_kinds, halo_weights, halo_first, edge_second, edge_third,
):
    fill_halo(edges, has_odd_pair("x", "zh"), tables, halo_kinds, halo_weights, halo_first, edge_second)

    def put(x, g, value):
        lower[4 * x + g] = value

    side(
        False, kinds, weights, first, second, third,
        halo_kinds, halo_weights, halo_first, edge_second, edge_third, put,
    )


def finish_kernel(
    kinds, edges, near, weights, first, second, third, middle, lower, tables, turned, other, live, blocks,
    smooth, payload, lists,
    halo_kinds, halo_weights, halo_first, edge_second, edge_third, chosen, node_block, sem,
):
    copy = pltpu.make_async_copy(blocks.at[0:1], node_block, sem)
    copy.start()
    half = whereabouts()[0]
    lists[0:4] = near[0:4]
    lists[4:8] = jnp.zeros((4, W), F32)
    lists[2:4] = edges[130:132]
    fill_halo(edges, True, tables, halo_kinds, halo_weights, halo_first, edge_second)

    def put(x, g, value):
        smooth[4 * mirrored(x, half) + g] = value

    side(
        True, kinds, weights, first, second, third,
        halo_kinds, halo_weights, halo_first, edge_second, edge_third, put,
    )
    for g in range(4):
        for x in (0, 1, 2):
            put(x, g, lower[4 * x + g])
        for x in (3, 4):
            put(x, g, middle[4 * (x - 3) + g])

    copy.wait()
    for b in range(BLOCKS):
        chosen[pl.ds(8 * b, 8), :] = smooth[node_block[0, b]]
    columns = rows_by_column(chosen)
    low = half_lanes((8, W))
    parts = ([], [])
    for j in range(4):
        one, two = columns[2 * j], columns[2 * j + 1]
        parts[0].append(jnp.where(low, one, swap_halves(two)))
        parts[1].append(jnp.where(low, swap_halves(one), two))
    values = [jnp.concatenate(p, axis=1) for p in parts]
    pieces = [split(v) for v in values]
    left = jnp.concatenate([pieces[0][0], pieces[1][0], pieces[0][1], pieces[1][1]], axis=0)
    block = lax.broadcasted_iota(jnp.int32, (BLOCKS, SAMPLES), 0)
    sums = [jnp.zeros((BLOCKS, SAMPLES), F32) for _ in range(2)]
    for b in range(BLOCKS):
        product = jnp.dot(left, turned[b], preferred_element_type=F32)
        for r in range(2):
            both = product[8 * r : 8 * r + 8] + product[16 + 8 * r : 24 + 8 * r]
            sums[r] = jnp.where(block == b, both, sums[r])
    tiles = []
    for r in range(2):
        told = jnp.where(live[...] > 0.0, sums[r], 0.0)
        tiles += [told[:, 0:W], told[:, W : 2 * W]]
    tiles.append(other[:, 0:W])
    for n, tile in enumerate(tiles):
        payload[2 * n] = tile[0:4]
        payload[2 * n + 1] = tile[4:8]
    payload[10] = other[0:4, W : 2 * W]


def collect_kernel(lists, here, keep, send):
    names = here[0, 10]
    for n in range(1, 16):
        names = names + here[n, 10]
    names = jnp.broadcast_to(names[0:1], (8, W))
    lane = lax.broadcasted_iota(jnp.int32, (8, W), 1)
    row = lax.broadcasted_iota(jnp.int32, (8, W), 0)
    hits, spots = [], []
    half, core, _, me = whereabouts()
    for member in range(4):
        tile = me ^ (1 if member & 1 else 0) ^ (8 if member & 2 else 0)
        held = jnp.broadcast_to(lists[member : member + 1], (8, W))
        name = jnp.sum(jnp.where(lane == row, held, 0.0), axis=1, keepdims=True)
        name = jnp.broadcast_to(name, (8, W))
        hits.append(name == names)
        hits.append((2 * tile + 1 + (row & 1)).astype(F32) == names)
        block = name.astype(jnp.int32) - 1
        holder = block >> 1
        spot = ((holder >> 4) * 4 + ((holder >> 1) & 3)) * 8 + 2 * (block & 1)
        mine = ((holder & 1) == core) & (((holder >> 3) & 1) == half)
        spots.append(jnp.where(mine, spot, -1024))
    hit = jnp.concatenate([h.astype(F32) for h in hits], axis=0).astype(jnp.bfloat16)
    spots = jnp.concatenate(spots, axis=0)
    lane = lax.broadcasted_iota(jnp.int32, (32, W), 1)
    choose = jnp.concatenate(
        [(lane == spots + 4 * kind + h).astype(F32) for kind in range(2) for h in range(2)], axis=0
    ).astype(jnp.bfloat16)

    def column(tile):
        return jnp.concatenate([here[n, 2 * tile + k] for n in range(16) for k in range(2)], axis=0)

    def gather(left, data):
        high, low = split(data)
        return jnp.dot(left, high, preferred_element_type=F32) + jnp.dot(
            left, low, preferred_element_type=F32
        )

    totals = [
        gather(hit, jnp.concatenate([column(2 * r), column(2 * r + 1)], axis=1)) for r in range(2)
    ]
    found = gather(choose, column(4))
    row = lax.broadcasted_iota(jnp.int32, (8, W), 0)
    for member in range(4):
        out = (send if member & 1 else keep).at[member // 2]
        own = []
        for h in range(2):
            lanes = slice(h * W, h * W + W)
            drill, gain = [
                found[64 * kind + 32 * h + 8 * member : 64 * kind + 32 * h + 8 * member + 8]
                for kind in range(2)
            ]
            for r in range(2):
                out[16 * r + 8 * h : 16 * r + 8 * h + 8, :] = drill - totals[r][16 * member : 16 * member + 8, lanes]
                own.append(totals[r][16 * member + 8 : 16 * member + 16, lanes])
            out[32 + 8 * h : 40 + 8 * h, :] = gain
        out[48:56, :] = jnp.where(
            row < 4, jnp.where(row < 2, own[0], own[1]), jnp.where(row < 6, own[2], own[3])
        )


def update_kernel(
    keep, near, far, smooth, matrix, rows, live, blocks,
    out, misfit,
    update, node_block, sem,
):
    copy = pltpu.make_async_copy(blocks.at[0:1], node_block, sem)
    copy.start()
    sums = keep[0] + near[0] + far[...]
    for k in range(2):
        for r in range(2):
            for h in range(2):
                t = 48 + 4 * h + 2 * r + k
                lanes = slice(h * W, h * W + W)
                misfit[k, r : r + 1, lanes] = rows[0, k : k + 1, lanes] - sums[t : t + 1, :]
    gain = jnp.concatenate([sums[32:40], sums[40:48]], axis=1)
    picked = [
        jnp.where(
            live[...] > 0.0,
            gain * jnp.concatenate([sums[16 * r : 16 * r + 8], sums[16 * r + 8 : 16 * r + 16]], axis=1),
            0.0,
        )
        for r in range(2)
    ]
    pieces = [split(v) for v in picked]
    left = jnp.concatenate([pieces[0][0], pieces[1][0], pieces[0][1], pieces[1][1]], axis=0)
    block = lax.broadcasted_iota(jnp.int32, (BLOCKS, NODES), 0)
    sums = [jnp.zeros((BLOCKS, NODES), F32) for _ in range(2)]
    for b in range(BLOCKS):
        product = jnp.dot(left, matrix[b], preferred_element_type=F32)
        for r in range(2):
            both = product[8 * r : 8 * r + 8] + product[16 + 8 * r : 24 + 8 * r]
            sums[r] = jnp.where(block == b, both, sums[r])
    low = half_lanes((8, W))
    for j in range(4):
        one, two = sums[0][:, j * W : j * W + W], sums[1][:, j * W : j * W + W]
        update[pl.ds(2 * j, 8, stride=8), :] = jnp.where(low, one, swap_halves(two))
        update[pl.ds(2 * j + 1, 8, stride=8), :] = jnp.where(low, swap_halves(one), two)
    out[...] = smooth[...]
    copy.wait()
    for b in range(BLOCKS):
        n = node_block[0, b]
        out[n] = out[n] + update[8 * b : 8 * b + 8, :]


def shape(*dims, dtype=F32):
    return jax.ShapeDtypeStruct(dims, dtype)


def call(kernel, outs, ins, name, scratch=()):
    return pl.pallas_call(
        kernel,
        out_shape=outs,
        in_specs=ins,
        out_specs=(VMEM,) * len(outs),
        scratch_shapes=scratch,
        compiler_params=pltpu.CompilerParams(vmem_limit_bytes=24 * 1024 * 1024),
        name=name,
    )


def shards(
    noise, classes, table, obs_matrix, node_block, sample_block, sample_count, drill_data, obs_gain
):
    noise, classes, table, matrix, blocks, owner, count, drill, gain = [
        pltpu.with_memory_space_constraint(a, pltpu.HBM)
        for a in (
            noise, classes, table, obs_matrix, node_block, sample_block, sample_count, drill_data, obs_gain
        )
    ]
    odd, even, names = call(
        edge_y_kernel,
        (shape(X + 1, 4, W), shape(X + 1, 4, W), shape(8, W)),
        [HBM] * 3,
        "edge_y",
        [
            pltpu.VMEM((2, X, 8, W), F32),
            pltpu.VMEM((2, X, 8, Z), jnp.int32),
            pltpu.SMEM((BLOCKS,), jnp.int32),
            pltpu.SemaphoreType.DMA((5,)),
        ],
    )(noise, classes, owner)
    odd = permute(odd, ("x", "y", "core"), odd_along_y)
    even = permute(even, ("y", "core"), even_pair)
    field, kinds, tables = call(
        prepare_kernel,
        (shape(X, YP, W), shape(X, YP, W), shape(27, 8, W)),
        [HBM] * 3,
        "prepare",
        [
            pltpu.VMEM((X, Y, W), F32),
            pltpu.VMEM((X, Y, Z), jnp.int32),
            pltpu.VMEM((8, 27), F32),
            pltpu.SemaphoreType.DMA((3,)),
        ],
    )(noise, classes, table)
    field, kinds, odd, even, lists = call(
        edge_x_kernel,
        (shape(X, YP, W), shape(X, YP, W), shape(MESSAGE, W), shape(MESSAGE, W), shape(4, W)),
        [VMEM] * 6,
        "edge_x",
        [pltpu.VMEM((27, YP, W), F32), pltpu.VMEM((3, 3, YP, W), F32)],
    )(odd, even, field, kinds, names, tables)
    odd = permute(odd, ("x", "zh", "core"), odd_along_x)
    even = permute(even, ("x", "zh"), even_pair)
    weights, first, second, third, middle, matrix, turned, rows, other, live, blocks = call(
        interior_kernel,
        (
            shape(27, X, YP, W),
            shape(3, X, YP, W),
            shape(3, 6, YP, W),
            shape(3, 4, YP, W),
            shape(8, 8, W),
            shape(BLOCKS, SAMPLES, NODES, dtype=jnp.bfloat16),
            shape(BLOCKS, NODES, SAMPLES, dtype=jnp.bfloat16),
            shape(2, 2, SAMPLES),
            shape(8, SAMPLES),
            shape(BLOCKS, SAMPLES),
            shape(8, W, dtype=jnp.int32),
        ),
        [VMEM] * 3 + [HBM] * 6,
        "interior",
        [pltpu.SMEM((3, BLOCKS), jnp.int32), pltpu.SemaphoreType.DMA((6,))],
    )(field, kinds, tables, matrix, drill, gain, blocks, count, owner)
    halo_scratch = [
        pltpu.VMEM((YP, W), F32),
        pltpu.VMEM((27, YP, W), F32),
        pltpu.VMEM((3, 2, YP, W), F32),
        pltpu.VMEM((3, 3, YP, W), F32),
        pltpu.VMEM((3, 3, YP, W), F32),
    ]
    (lower,) = call(lower_kernel, (shape(12, 8, W),), [VMEM] * 7, "lower", halo_scratch)(
        kinds, odd, weights, first, second, third, tables
    )
    index_scratch = [pltpu.SMEM((1, W), jnp.int32), pltpu.SemaphoreType.DMA]
    smooth, payload, lists = call(
        finish_kernel,
        (shape(32, 8, W), shape(GROUPS, 4, W), shape(8, W)),
        [VMEM] * 14,
        "finish",
        halo_scratch + [pltpu.VMEM((64, W), F32)] + index_scratch,
    )(
        kinds, even, lists, weights, first, second, third, middle, lower, tables, turned,
        other, live, blocks,
    )
    here = lax.all_to_all(
        jnp.broadcast_to(payload[None], (16, GROUPS, 4, W)), ("x", "y"), 0, 0, tiled=True
    )
    keep, send = call(
        collect_kernel, (shape(2, 56, W), shape(2, 56, W)), [VMEM] * 2, "collect"
    )(lists, here)
    near = permute(send, ("core",), lambda c: (c ^ 1,))
    far = permute(keep[1] + near[1], ("zh",), lambda z: (z ^ 1,))
    out, misfit = call(
        update_kernel,
        (shape(32, 8, W), shape(2, 2, SAMPLES)),
        [VMEM] * 8,
        "update",
        [pltpu.VMEM((64, W), F32)] + index_scratch,
    )(keep, near, far, smooth, matrix, rows, live, blocks)
    return out.reshape(X, Y, W), misfit


def solution(mesh):
    fine = Mesh(
        mesh.devices.reshape(4, 4, 2, 4, 2), ("real", "x", "zh", "y", "core")
    )
    sx, sy = ("x", "zh"), ("y", "core")
    both = sx + sy
    in_specs = (
        P(sx, sy, "real"),
        P(sx, sy, None),
        P(),
        P(both, None, None),
        P(both),
        P(both),
        P(both),
        P(both, None),
        P(both, None),
    )
    out_specs = (P(sx, sy, "real"), P(both, "real", None))
    return jax.shard_map(shards, mesh=fine, in_specs=in_specs, out_specs=out_specs, check_vma=False)
```

```python
import itertools

import jax
import jax.numpy as jnp
from jax import lax
from jax.experimental import pallas as pl
from jax.experimental.pallas import tpu as pltpu
from jax.sharding import Mesh, PartitionSpec as P

CHEB = (0.6, 0.5, 0.3, 0.2)
X, Y, Z = 8, 32, 64
W = 2 * Z
YP = 40
OFF = 4
BLOCKS = 8
SAMPLES = 256
NODES = 512
GROUPS = 11
MESSAGE = 128
F32 = jnp.float32
VMEM = pl.BlockSpec(memory_space=pltpu.VMEM)
HBM = pl.BlockSpec(memory_space=pltpu.HBM)
SIZES = {"x": 4, "zh": 2, "y": 4, "core": 2}


def permute(value, axes, target):
    dims = [SIZES[a] for a in axes]

    def flat(place):
        number = 0
        for coordinate, size in zip(place, dims):
            number = number * size + coordinate
        return number

    pairs = []
    for place in itertools.product(*[range(d) for d in dims]):
        other = target(*place)
        if other is not None:
            pairs.append((flat(place), flat(other)))
    return lax.ppermute(value, axes if len(axes) > 1 else axes[0], pairs)


def even_pair(a, b):
    return (a, b ^ 1)


def odd_pair(a, b):
    if b == 1:
        return (a + 1, 0) if a < 3 else None
    return (a - 1, 1) if a > 0 else None


def odd_along_x(x, zh, core):
    other = odd_pair(x, zh)
    return other + (core,) if other else (x, zh, core ^ 1)


def odd_along_y(x, y, core):
    other = odd_pair(y, core)
    return (x,) + other if other else (x ^ 1, y, core)


def half_lanes(shape):
    return lax.broadcasted_iota(jnp.int32, shape, len(shape) - 1) < Z


def swap_halves(value):
    return pltpu.roll(value, Z, axis=value.ndim - 1)


def pack(first, second):
    return jnp.where(half_lanes(first.shape), first, second)


def unpack(row):
    low = half_lanes(row.shape)
    other = swap_halves(row)
    return jnp.where(low, row, other), jnp.where(low, other, row)


def whereabouts():
    x, zh, y, core = [lax.axis_index(axis) for axis in ("x", "zh", "y", "core")]
    return zh, core, 4 * x + y, ((x * 2 + zh) * 4 + y) * 2 + core


def has_odd_pair(outer, inner):
    return lax.axis_index(outer) != 3 * lax.axis_index(inner)


def edge_y_kernel(
    noise_far, classes_far, owner_far,
    odd, even, names,
    noise_edges, class_edges, owner, sems,
):
    copies = [
        pltpu.make_async_copy(noise_far.at[:, 0:8, :], noise_edges.at[0], sems.at[0]),
        pltpu.make_async_copy(noise_far.at[:, Y - 8 : Y, :], noise_edges.at[1], sems.at[1]),
        pltpu.make_async_copy(classes_far.at[:, 0:8, :], class_edges.at[0], sems.at[2]),
        pltpu.make_async_copy(classes_far.at[:, Y - 8 : Y, :], class_edges.at[1], sems.at[3]),
        pltpu.make_async_copy(owner_far, owner, sems.at[4]),
    ]
    for copy in copies:
        copy.start()
    for copy in copies:
        copy.wait()
    core = whereabouts()[1]
    lane = lax.broadcasted_iota(jnp.int32, (8, W), 1)
    own = jnp.zeros((8, W), F32)
    for b in range(BLOCKS):
        own = jnp.where(lane == b, (owner[b] + 1).astype(F32), own)
    names[...] = own
    odd[X] = own[0:4]
    even[X] = own[0:4]

    def message(out, end, start, one, two):
        out[0:X, 0:3, :] = noise_edges[end, :, start : start + 3, :]
        kinds = (class_edges[end] + 1).astype(F32)
        out[0:X, 3:4, :] = jnp.concatenate([kinds[:, one : one + 1], kinds[:, two : two + 1]], axis=-1)

    @pl.when(core == 0)
    def _():
        message(even, 1, 5, 6, 7)
        message(odd, 0, 0, 0, 1)

    @pl.when(core == 1)
    def _():
        message(even, 0, 0, 0, 1)
        message(odd, 1, 5, 6, 7)


def prepare_kernel(
    noise_far, classes_far, table, field, kinds, tables, noise, classes, held_table, sems
):
    copies = [
        pltpu.make_async_copy(noise_far, noise, sems.at[0]),
        pltpu.make_async_copy(classes_far, classes, sems.at[1]),
        pltpu.make_async_copy(table, held_table, sems.at[2]),
    ]
    for copy in copies:
        copy.start()
    for copy in copies:
        copy.wait()
    half = whereabouts()[0]
    for out in (field, kinds):
        out[:, 0:8, :] = jnp.zeros((X, 8, W), F32)
        out[:, 32:40, :] = jnp.zeros((X, 8, W), F32)
    for x in range(X):
        true = mirrored(x, half)
        field[x, OFF : OFF + Y, :] = noise[true]
        kind = (classes[true] + 1).astype(F32)
        kinds[x, OFF : OFF + Y, :] = jnp.concatenate([kind, kind], axis=-1)
    spread_table(held_table, half, tables)


def edge_x_kernel(
    odd_in, even_in, field_in, kinds_in, names, tables,
    field, kinds, odd, even, lists,
    weights, moved,
):
    half, core = whereabouts()[0:2]
    field[...] = field_in[...]
    kinds[...] = kinds_in[...]
    lists[0:4] = names[0:4]
    lists[1:2] = even_in[X, 0:1, :]

    inside = has_odd_pair("y", "core")

    def sides(low, high):
        for x in range(X):
            true = mirrored(x, half)
            for message, start, one in ((low, 1, 2), (high, 36, 36)):
                held = message[true]
                if message is odd_in:
                    held = jnp.where(inside, held, 0.0)
                field[x, start : start + 3, :] = held[0:3]
                first, second = unpack(held[3:4])
                kinds[x, one : one + 1, :] = first
                kinds[x, one + 1 : one + 2, :] = second

    @pl.when(core == 0)
    def _():
        sides(odd_in, even_in)

    @pl.when(core == 1)
    def _():
        sides(even_in, odd_in)

    for out, row, step in ((odd, 0, 1), (even, X - 1, -1)):
        for n in range(2):
            def put(o, part, value, n=n):
                weights[n, o, part, :] = value

            weigh(kinds[row + n * step], tables, put)
        for n in range(3):
            for c, value in enumerate(lean(field[row + n * step])):
                moved[c, n] = value
        second = operate(
            lambda o: weights[1, o],
            lambda a, c: moved[c, a if step == 1 else 2 - a],
            jnp.minimum(kinds[row + step], 1.0),
        )
        for c, value in enumerate(lean(second)):
            moved[c, 3] = value
        kind = kinds[row]
        inside = jnp.minimum(kind, 1.0)
        known = operate(
            lambda o: weights[0, o],
            lambda a, c: moved[c, (a - 1) * step],
            inside,
            (1, 2) if step == 1 else (0, 1),
        )
        onward = operate(
            lambda o: weights[0, o], lambda a, c: moved[c, 3], inside, (2,) if step == 1 else (0,)
        )
        out[0:38, :] = field[row][1:39]
        out[38:74, :] = known[2:38]
        out[74:108, :] = (2.0 * onward - field[row])[3:37]
        out[108:126, :] = pack(kind[2:20], kind[20:38])
        out[126:128, :] = lists[0:2]


def mirrored(x, half):
    return x + half * (X - 1 - 2 * x)


def rows_by_column(block_rows):
    return [block_rows[pl.ds(c, 8, stride=8), :] for c in range(8)]


def split(value):
    high = value.astype(jnp.bfloat16)
    low = (value - high.astype(F32)).astype(jnp.bfloat16)
    return high, low


def weigh(kinds, table, put):
    for b in range(3):
        moved = kinds if b == 1 else pltpu.roll(kinds, (b - 1) % YP, axis=0)
        index = jnp.maximum(moved.astype(jnp.int32) - 1, 0)
        for g in range(YP // 8):
            part = index[8 * g : 8 * g + 8]
            for a in range(3):
                for c in range(3):
                    o = 9 * a + 3 * b + c
                    put(
                        o,
                        pl.ds(8 * g, 8),
                        jnp.take_along_axis(table[o], part, axis=0, mode="promise_in_bounds"),
                    )


def spread_table(table, half, out):
    held = table[...]
    columns = [jnp.broadcast_to(held[:, o : o + 1], (8, W)) for o in range(27)]
    for o in range(27):
        out[o] = jnp.where(half == 0, columns[o], columns[o + 9 * (2 - 2 * (o // 9))])


def lean(row):
    lanes = lax.broadcasted_iota(jnp.int32, (YP, W), 1) % Z
    below = jnp.where(lanes > 0, pltpu.roll(row, 1, axis=1), 0.0)
    above = jnp.where(lanes < Z - 1, pltpu.roll(row, W - 1, axis=1), 0.0)
    return below, row, above


def operate(weight, moved, inside, rows=(0, 1, 2)):
    sums = []
    for b in range(3):
        total = None
        for a in rows:
            for c in range(3):
                term = weight(9 * a + 3 * b + c) * moved(a, c)
                total = term if total is None else total + term
        sums.append(total)
    result = pltpu.roll(sums[0], 1, axis=0) + sums[1] + pltpu.roll(sums[2], YP - 1, axis=0)
    return result * inside


def interior_kernel(
    field, kinds, tables, matrix, drill, gain, node_block, count, owner,
    weights, first, second, third, smooth, held_matrix, turned, held_rows, other, live, blocks,
    scalars, sems,
):
    copies = [
        pltpu.make_async_copy(matrix, held_matrix, sems.at[0]),
        pltpu.make_async_copy(drill, held_rows.at[0], sems.at[1]),
        pltpu.make_async_copy(gain, held_rows.at[1], sems.at[2]),
        pltpu.make_async_copy(node_block, scalars.at[0], sems.at[3]),
        pltpu.make_async_copy(count, scalars.at[1], sems.at[4]),
        pltpu.make_async_copy(owner, scalars.at[2], sems.at[5]),
    ]
    for copy in copies:
        copy.start()
    plane = whereabouts()[2]
    for x in range(X):
        def put(o, rows, value, x=x):
            weights[o, x, rows, :] = value

        weigh(kinds[x], tables, put)
        for c, value in enumerate(lean(field[x])):
            first[c, x] = value

    def step(source, start, x):
        return operate(
            lambda o: weights[o, x],
            lambda a, c: source[c, x + a - 1 - start],
            jnp.minimum(kinds[x], 1.0),
        )

    for x in range(1, 7):
        for c, value in enumerate(lean(step(first, 0, x))):
            second[c, x - 1] = value
    for x in range(2, 6):
        value = 2.0 * step(second, 1, x) - first[1, x]
        for c, value in enumerate(lean(value)):
            third[c, x - 2] = value
    for x in range(3, 5):
        fourth = 2.0 * step(third, 2, x) - second[1, x - 1]
        result = (
            CHEB[0] * first[1, x] + CHEB[1] * second[1, x - 1] + CHEB[2] * third[1, x - 2] + CHEB[3] * fourth
        )
        for g in range(4):
            smooth[4 * (x - 3) + g] = result[OFF + 8 * g : OFF + 8 * g + 8]
    for copy in copies:
        copy.wait()
    for b in range(BLOCKS):
        turned[b] = held_matrix[b].T
    other[...] = jnp.zeros((8, SAMPLES), F32)
    for k in range(2):
        for h in range(2):
            for kind in range(2):
                row = 4 * kind + 2 * k + h
                other[row : row + 1, 0:W] = held_rows[kind, k : k + 1, h * W : h * W + W]
    lane = lax.broadcasted_iota(jnp.int32, (8, W), 1)
    names = jnp.zeros((8, W), F32)
    places = jnp.zeros((8, W), jnp.int32)
    limit = jnp.zeros((BLOCKS, SAMPLES), jnp.int32)
    block = lax.broadcasted_iota(jnp.int32, (BLOCKS, SAMPLES), 0)
    for b in range(BLOCKS):
        names = jnp.where(lane == 8 * plane + b, (scalars[2, b] + 1).astype(F32), names)
        places = jnp.where(lane == b, scalars[0, b], places)
        limit = jnp.where(block == b, scalars[1, b], limit)
    other[0:1, W : 2 * W] = names[0:1]
    blocks[...] = places
    sample = lax.broadcasted_iota(jnp.int32, (BLOCKS, SAMPLES), 1)
    live[...] = (sample < limit).astype(F32)


def fill_halo(message, inside, tables, halo_kinds, halo_weights, halo_first, partial):
    held = jnp.where(inside, message[...], 0.0)
    one, two, three = [jnp.zeros((n, W), F32) for n in (1, 2, 3)]
    low, high = unpack(held[108:126])
    halo_kinds[...] = jnp.concatenate([two, low, high, two], axis=0)

    def put(o, part, value):
        halo_weights[o, part, :] = value

    weigh(halo_kinds[...], tables, put)
    for c, value in enumerate(lean(jnp.concatenate([one, held[0:38], one], axis=0))):
        halo_first[c, 0] = value
    partial[0] = jnp.concatenate([two, held[38:74], two], axis=0)
    partial[1] = jnp.concatenate([three, held[74:108], three], axis=0)


def side(
    high, kinds, weights, first, second, third, halo_kinds, halo_weights, halo_first, edge_second, edge_third, partial, put
):
    def beyond(x):
        return x - X if high else -1 - x

    def weight(x):
        if 0 <= x < X:
            return (lambda o: weights[o, x]), jnp.minimum(kinds[x], 1.0)
        return (lambda o: halo_weights[o]), jnp.minimum(halo_kinds[...], 1.0)

    def at_first(x, c):
        return first[c, x] if 0 <= x < X else halo_first[c, beyond(x)]

    def at_second(x, c):
        return second[c, x - 1] if 1 <= x < 7 else edge_second[c, beyond(x) + 1]

    def at_third(x, c):
        return third[c, x - 2] if 2 <= x < 6 else edge_third[c, beyond(x) + 2]

    def step(at, x, rows=(0, 1, 2)):
        of, inside = weight(x)
        return operate(of, lambda a, c: at(x + a - 1, c), inside, rows)

    def row(n):
        return X - 1 - n if high else n

    inward, itself = ((0,), (0, 1)) if high else ((2,), (1, 2))
    for n in (-1, 0):
        if n < 0:
            value = partial[0] + step(at_first, row(n), inward)
        else:
            value = step(at_first, row(n))
        for c, value in enumerate(lean(value)):
            edge_second[c, -n] = value
    for n in (-1, 0, 1):
        if n < 0:
            value = partial[1] + 2.0 * step(at_second, row(n), itself)
        else:
            value = 2.0 * step(at_second, row(n)) - at_first(row(n), 1)
        for c, value in enumerate(lean(value)):
            edge_third[c, 1 - n] = value
    for n in (0, 1, 2):
        x = row(n)
        fourth = 2.0 * step(at_third, x) - at_second(x, 1)
        result = (
            CHEB[0] * at_first(x, 1) + CHEB[1] * at_second(x, 1) + CHEB[2] * at_third(x, 1) + CHEB[3] * fourth
        )
        for g in range(4):
            put(x, g, result[OFF + 8 * g : OFF + 8 * g + 8])


def lower_kernel(
    kinds, edges, weights, first, second, third, tables,
    lower,
    halo_kinds, halo_weights, halo_first, edge_second, edge_third, partial,
):
    fill_halo(edges, has_odd_pair("x", "zh"), tables, halo_kinds, halo_weights, halo_first, partial)

    def put(x, g, value):
        lower[4 * x + g] = value

    side(
        False, kinds, weights, first, second, third,
        halo_kinds, halo_weights, halo_first, edge_second, edge_third, partial, put,
    )


def finish_kernel(
    kinds, edges, near, weights, first, second, third, middle, lower, tables, turned, other, live, blocks,
    smooth, payload, lists,
    halo_kinds, halo_weights, halo_first, edge_second, edge_third, partial, chosen, node_block, sem,
):
    copy = pltpu.make_async_copy(blocks.at[0:1], node_block, sem)
    copy.start()
    half = whereabouts()[0]
    lists[0:4] = near[0:4]
    lists[4:8] = jnp.zeros((4, W), F32)
    lists[2:4] = edges[126:128]
    fill_halo(edges, True, tables, halo_kinds, halo_weights, halo_first, partial)

    def put(x, g, value):
        smooth[4 * mirrored(x, half) + g] = value

    side(
        True, kinds, weights, first, second, third,
        halo_kinds, halo_weights, halo_first, edge_second, edge_third, partial, put,
    )
    for g in range(4):
        for x in (0, 1, 2):
            put(x, g, lower[4 * x + g])
        for x in (3, 4):
            put(x, g, middle[4 * (x - 3) + g])

    copy.wait()
    for b in range(BLOCKS):
        chosen[pl.ds(8 * b, 8), :] = smooth[node_block[0, b]]
    columns = rows_by_column(chosen)
    low = half_lanes((8, W))
    parts = ([], [])
    for j in range(4):
        one, two = columns[2 * j], columns[2 * j + 1]
        parts[0].append(jnp.where(low, one, swap_halves(two)))
        parts[1].append(jnp.where(low, swap_halves(one), two))
    values = [jnp.concatenate(p, axis=1) for p in parts]
    pieces = [split(v) for v in values]
    left = jnp.concatenate([pieces[0][0], pieces[1][0], pieces[0][1], pieces[1][1]], axis=0)
    block = lax.broadcasted_iota(jnp.int32, (BLOCKS, SAMPLES), 0)
    sums = [jnp.zeros((BLOCKS, SAMPLES), F32) for _ in range(2)]
    for b in range(BLOCKS):
        product = jnp.dot(left, turned[b], preferred_element_type=F32)
        for r in range(2):
            both = product[8 * r : 8 * r + 8] + product[16 + 8 * r : 24 + 8 * r]
            sums[r] = jnp.where(block == b, both, sums[r])
    tiles = []
    for r in range(2):
        told = jnp.where(live[...] > 0.0, sums[r], 0.0)
        tiles += [told[:, 0:W], told[:, W : 2 * W]]
    tiles.append(other[:, 0:W])
    for n, tile in enumerate(tiles):
        payload[2 * n] = tile[0:4]
        payload[2 * n + 1] = tile[4:8]
    payload[10] = other[0:4, W : 2 * W]


def collect_kernel(lists, here, keep, send):
    names = here[0, 10]
    for n in range(1, 16):
        names = names + here[n, 10]
    names = jnp.broadcast_to(names[0:1], (8, W))
    lane = lax.broadcasted_iota(jnp.int32, (8, W), 1)
    row = lax.broadcasted_iota(jnp.int32, (8, W), 0)
    hits, spots = [], []
    half, core, _, me = whereabouts()
    for member in range(4):
        tile = me ^ (1 if member & 1 else 0) ^ (8 if member & 2 else 0)
        held = jnp.broadcast_to(lists[member : member + 1], (8, W))
        name = jnp.sum(jnp.where(lane == row, held, 0.0), axis=1, keepdims=True)
        name = jnp.broadcast_to(name, (8, W))
        hits.append(name == names)
        hits.append((2 * tile + 1 + (row & 1)).astype(F32) == names)
        block = name.astype(jnp.int32) - 1
        holder = block >> 1
        spot = ((holder >> 4) * 4 + ((holder >> 1) & 3)) * 8 + 2 * (block & 1)
        mine = ((holder & 1) == core) & (((holder >> 3) & 1) == half)
        spots.append(jnp.where(mine, spot, -1024))
    hit = jnp.concatenate([h.astype(F32) for h in hits], axis=0).astype(jnp.bfloat16)
    spots = jnp.concatenate(spots, axis=0)
    lane = lax.broadcasted_iota(jnp.int32, (32, W), 1)
    choose = jnp.concatenate(
        [(lane == spots + 4 * kind + h).astype(F32) for kind in range(2) for h in range(2)], axis=0
    ).astype(jnp.bfloat16)

    def column(tile):
        return jnp.concatenate([here[n, 2 * tile + k] for n in range(16) for k in range(2)], axis=0)

    def gather(left, data):
        high, low = split(data)
        return jnp.dot(left, high, preferred_element_type=F32) + jnp.dot(
            left, low, preferred_element_type=F32
        )

    totals = [
        gather(hit, jnp.concatenate([column(2 * r), column(2 * r + 1)], axis=1)) for r in range(2)
    ]
    found = gather(choose, column(4))
    row = lax.broadcasted_iota(jnp.int32, (8, W), 0)
    for member in range(4):
        out = (send if member & 1 else keep).at[member // 2]
        own = []
        for h in range(2):
            lanes = slice(h * W, h * W + W)
            drill, gain = [
                found[64 * kind + 32 * h + 8 * member : 64 * kind + 32 * h + 8 * member + 8]
                for kind in range(2)
            ]
            for r in range(2):
                out[16 * r + 8 * h : 16 * r + 8 * h + 8, :] = drill - totals[r][16 * member : 16 * member + 8, lanes]
                own.append(totals[r][16 * member + 8 : 16 * member + 16, lanes])
            out[32 + 8 * h : 40 + 8 * h, :] = gain
        out[48:56, :] = jnp.where(
            row < 4, jnp.where(row < 2, own[0], own[1]), jnp.where(row < 6, own[2], own[3])
        )


def update_kernel(
    keep, near, far, smooth, matrix, rows, live, blocks,
    out, misfit,
    update, node_block, sem,
):
    copy = pltpu.make_async_copy(blocks.at[0:1], node_block, sem)
    copy.start()
    sums = keep[0] + near[0] + far[...]
    for k in range(2):
        for r in range(2):
            for h in range(2):
                t = 48 + 4 * h + 2 * r + k
                lanes = slice(h * W, h * W + W)
                misfit[k, r : r + 1, lanes] = rows[0, k : k + 1, lanes] - sums[t : t + 1, :]
    gain = jnp.concatenate([sums[32:40], sums[40:48]], axis=1)
    picked = [
        jnp.where(
            live[...] > 0.0,
            gain * jnp.concatenate([sums[16 * r : 16 * r + 8], sums[16 * r + 8 : 16 * r + 16]], axis=1),
            0.0,
        )
        for r in range(2)
    ]
    pieces = [split(v) for v in picked]
    left = jnp.concatenate([pieces[0][0], pieces[1][0], pieces[0][1], pieces[1][1]], axis=0)
    block = lax.broadcasted_iota(jnp.int32, (BLOCKS, NODES), 0)
    sums = [jnp.zeros((BLOCKS, NODES), F32) for _ in range(2)]
    for b in range(BLOCKS):
        product = jnp.dot(left, matrix[b], preferred_element_type=F32)
        for r in range(2):
            both = product[8 * r : 8 * r + 8] + product[16 + 8 * r : 24 + 8 * r]
            sums[r] = jnp.where(block == b, both, sums[r])
    low = half_lanes((8, W))
    for j in range(4):
        one, two = sums[0][:, j * W : j * W + W], sums[1][:, j * W : j * W + W]
        update[pl.ds(2 * j, 8, stride=8), :] = jnp.where(low, one, swap_halves(two))
        update[pl.ds(2 * j + 1, 8, stride=8), :] = jnp.where(low, swap_halves(one), two)
    out[...] = smooth[...]
    copy.wait()
    for b in range(BLOCKS):
        n = node_block[0, b]
        out[n] = out[n] + update[8 * b : 8 * b + 8, :]


def shape(*dims, dtype=F32):
    return jax.ShapeDtypeStruct(dims, dtype)


def call(kernel, outs, ins, name, scratch=()):
    return pl.pallas_call(
        kernel,
        out_shape=outs,
        in_specs=ins,
        out_specs=(VMEM,) * len(outs),
        scratch_shapes=scratch,
        compiler_params=pltpu.CompilerParams(vmem_limit_bytes=24 * 1024 * 1024),
        name=name,
    )


def shards(
    noise, classes, table, obs_matrix, node_block, sample_block, sample_count, drill_data, obs_gain
):
    noise, classes, table, matrix, blocks, owner, count, drill, gain = [
        pltpu.with_memory_space_constraint(a, pltpu.HBM)
        for a in (
            noise, classes, table, obs_matrix, node_block, sample_block, sample_count, drill_data, obs_gain
        )
    ]
    odd, even, names = call(
        edge_y_kernel,
        (shape(X + 1, 4, W), shape(X + 1, 4, W), shape(8, W)),
        [HBM] * 3,
        "edge_y",
        [
            pltpu.VMEM((2, X, 8, W), F32),
            pltpu.VMEM((2, X, 8, Z), jnp.int32),
            pltpu.SMEM((BLOCKS,), jnp.int32),
            pltpu.SemaphoreType.DMA((5,)),
        ],
    )(noise, classes, owner)
    odd = permute(odd, ("x", "y", "core"), odd_along_y)
    even = permute(even, ("y", "core"), even_pair)
    field, kinds, tables = call(
        prepare_kernel,
        (shape(X, YP, W), shape(X, YP, W), shape(27, 8, W)),
        [HBM] * 3,
        "prepare",
        [
            pltpu.VMEM((X, Y, W), F32),
            pltpu.VMEM((X, Y, Z), jnp.int32),
            pltpu.VMEM((8, 27), F32),
            pltpu.SemaphoreType.DMA((3,)),
        ],
    )(noise, classes, table)
    field, kinds, odd, even, lists = call(
        edge_x_kernel,
        (shape(X, YP, W), shape(X, YP, W), shape(MESSAGE, W), shape(MESSAGE, W), shape(4, W)),
        [VMEM] * 6,
        "edge_x",
        [pltpu.VMEM((2, 27, YP, W), F32), pltpu.VMEM((3, 4, YP, W), F32)],
    )(odd, even, field, kinds, names, tables)
    odd = permute(odd, ("x", "zh", "core"), odd_along_x)
    even = permute(even, ("x", "zh"), even_pair)
    weights, first, second, third, middle, matrix, turned, rows, other, live, blocks = call(
        interior_kernel,
        (
            shape(27, X, YP, W),
            shape(3, X, YP, W),
            shape(3, 6, YP, W),
            shape(3, 4, YP, W),
            shape(8, 8, W),
            shape(BLOCKS, SAMPLES, NODES, dtype=jnp.bfloat16),
            shape(BLOCKS, NODES, SAMPLES, dtype=jnp.bfloat16),
            shape(2, 2, SAMPLES),
            shape(8, SAMPLES),
            shape(BLOCKS, SAMPLES),
            shape(8, W, dtype=jnp.int32),
        ),
        [VMEM] * 3 + [HBM] * 6,
        "interior",
        [pltpu.SMEM((3, BLOCKS), jnp.int32), pltpu.SemaphoreType.DMA((6,))],
    )(field, kinds, tables, matrix, drill, gain, blocks, count, owner)
    halo_scratch = [
        pltpu.VMEM((YP, W), F32),
        pltpu.VMEM((27, YP, W), F32),
        pltpu.VMEM((3, 1, YP, W), F32),
        pltpu.VMEM((3, 2, YP, W), F32),
        pltpu.VMEM((3, 3, YP, W), F32),
        pltpu.VMEM((2, YP, W), F32),
    ]
    (lower,) = call(lower_kernel, (shape(12, 8, W),), [VMEM] * 7, "lower", halo_scratch)(
        kinds, odd, weights, first, second, third, tables
    )
    index_scratch = [pltpu.SMEM((1, W), jnp.int32), pltpu.SemaphoreType.DMA]
    smooth, payload, lists = call(
        finish_kernel,
        (shape(32, 8, W), shape(GROUPS, 4, W), shape(8, W)),
        [VMEM] * 14,
        "finish",
        halo_scratch + [pltpu.VMEM((64, W), F32)] + index_scratch,
    )(
        kinds, even, lists, weights, first, second, third, middle, lower, tables, turned,
        other, live, blocks,
    )
    here = lax.all_to_all(
        jnp.broadcast_to(payload[None], (16, GROUPS, 4, W)), ("x", "y"), 0, 0, tiled=True
    )
    keep, send = call(
        collect_kernel, (shape(2, 56, W), shape(2, 56, W)), [VMEM] * 2, "collect"
    )(lists, here)
    near = permute(send, ("core",), lambda c: (c ^ 1,))
    far = permute(keep[1] + near[1], ("zh",), lambda z: (z ^ 1,))
    out, misfit = call(
        update_kernel,
        (shape(32, 8, W), shape(2, 2, SAMPLES)),
        [VMEM] * 8,
        "update",
        [pltpu.VMEM((64, W), F32)] + index_scratch,
    )(keep, near, far, smooth, matrix, rows, live, blocks)
    return out.reshape(X, Y, W), misfit


def solution(mesh):
    fine = Mesh(
        mesh.devices.reshape(4, 4, 2, 4, 2), ("real", "x", "zh", "y", "core")
    )
    sx, sy = ("x", "zh"), ("y", "core")
    both = sx + sy
    in_specs = (
        P(sx, sy, "real"),
        P(sx, sy, None),
        P(),
        P(both, None, None),
        P(both),
        P(both),
        P(both),
        P(both, None),
        P(both, None),
    )
    out_specs = (P(sx, sy, "real"), P(both, "real", None))
    return jax.shard_map(shards, mesh=fine, in_specs=in_specs, out_specs=out_specs, check_vma=False)
```

```python
import itertools

import jax
import jax.numpy as jnp
from jax import lax
from jax.experimental import pallas as pl
from jax.experimental.pallas import tpu as pltpu
from jax.sharding import Mesh, PartitionSpec as P

CHEB = (0.6, 0.5, 0.3, 0.2)
X, Y, Z = 8, 32, 64
W = 2 * Z
YP = 40
OFF = 4
BLOCKS = 8
SAMPLES = 256
NODES = 512
GROUPS = 11
MESSAGE = 128
F32 = jnp.float32
VMEM = pl.BlockSpec(memory_space=pltpu.VMEM)
HBM = pl.BlockSpec(memory_space=pltpu.HBM)
SIZES = {"x": 4, "zh": 2, "y": 4, "core": 2}


def permute(value, axes, target):
    dims = [SIZES[a] for a in axes]

    def flat(place):
        number = 0
        for coordinate, size in zip(place, dims):
            number = number * size + coordinate
        return number

    pairs = []
    for place in itertools.product(*[range(d) for d in dims]):
        other = target(*place)
        if other is not None:
            pairs.append((flat(place), flat(other)))
    return lax.ppermute(value, axes if len(axes) > 1 else axes[0], pairs)


def even_pair(a, b):
    return (a, b ^ 1)


def odd_pair(a, b):
    if b == 1:
        return (a + 1, 0) if a < 3 else None
    return (a - 1, 1) if a > 0 else None


def odd_along_x(x, zh, core):
    other = odd_pair(x, zh)
    return other + (core,) if other else (x, zh, core ^ 1)


def odd_along_y(x, y, core):
    other = odd_pair(y, core)
    return (x,) + other if other else (x ^ 1, y, core)


def half_lanes(shape):
    return lax.broadcasted_iota(jnp.int32, shape, len(shape) - 1) < Z


def swap_halves(value):
    return pltpu.roll(value, Z, axis=value.ndim - 1)


def pack(first, second):
    return jnp.where(half_lanes(first.shape), first, second)


def unpack(row):
    low = half_lanes(row.shape)
    other = swap_halves(row)
    return jnp.where(low, row, other), jnp.where(low, other, row)


def whereabouts():
    x, zh, y, core = [lax.axis_index(axis) for axis in ("x", "zh", "y", "core")]
    return zh, core, 4 * x + y, ((x * 2 + zh) * 4 + y) * 2 + core


def has_odd_pair(outer, inner):
    return lax.axis_index(outer) != 3 * lax.axis_index(inner)


def edge_y_kernel(
    noise_far, classes_far, owner_far,
    odd, even, names,
    noise_edges, class_edges, owner, sems,
):
    copies = [
        pltpu.make_async_copy(noise_far.at[:, 0:8, :], noise_edges.at[0], sems.at[0]),
        pltpu.make_async_copy(noise_far.at[:, Y - 8 : Y, :], noise_edges.at[1], sems.at[1]),
        pltpu.make_async_copy(classes_far.at[:, 0:8, :], class_edges.at[0], sems.at[2]),
        pltpu.make_async_copy(classes_far.at[:, Y - 8 : Y, :], class_edges.at[1], sems.at[3]),
        pltpu.make_async_copy(owner_far, owner, sems.at[4]),
    ]
    for copy in copies:
        copy.start()
    for copy in copies:
        copy.wait()
    core = whereabouts()[1]
    lane = lax.broadcasted_iota(jnp.int32, (8, W), 1)
    own = jnp.zeros((8, W), F32)
    for b in range(BLOCKS):
        own = jnp.where(lane == b, (owner[b] + 1).astype(F32), own)
    names[...] = own
    odd[X] = own[0:4]
    even[X] = own[0:4]

    def message(out, end, start, one, two):
        out[0:X, 0:3, :] = noise_edges[end, :, start : start + 3, :]
        kinds = (class_edges[end] + 1).astype(F32)
        out[0:X, 3:4, :] = jnp.concatenate([kinds[:, one : one + 1], kinds[:, two : two + 1]], axis=-1)

    @pl.when(core == 0)
    def _():
        message(even, 1, 5, 6, 7)
        message(odd, 0, 0, 0, 1)

    @pl.when(core == 1)
    def _():
        message(even, 0, 0, 0, 1)
        message(odd, 1, 5, 6, 7)


def prepare_kernel(
    noise_far, classes_far, table, field, kinds, tables, noise, classes, held_table, sems
):
    copies = [
        pltpu.make_async_copy(noise_far, noise, sems.at[0]),
        pltpu.make_async_copy(classes_far, classes, sems.at[1]),
        pltpu.make_async_copy(table, held_table, sems.at[2]),
    ]
    for copy in copies:
        copy.start()
    for copy in copies:
        copy.wait()
    half = whereabouts()[0]
    for out in (field, kinds):
        out[:, 0:8, :] = jnp.zeros((X, 8, W), F32)
        out[:, 32:40, :] = jnp.zeros((X, 8, W), F32)
    for x in range(X):
        true = mirrored(x, half)
        field[x, OFF : OFF + Y, :] = noise[true]
        kind = (classes[true] + 1).astype(F32)
        kinds[x, OFF : OFF + Y, :] = jnp.concatenate([kind, kind], axis=-1)
    spread_table(held_table, half, tables)


def edge_x_kernel(
    odd_in, even_in, field_in, kinds_in, names, tables,
    field, kinds, odd, even, lists,
    weights, moved,
):
    half, core = whereabouts()[0:2]
    field[...] = field_in[...]
    kinds[...] = kinds_in[...]
    lists[0:4] = names[0:4]
    lists[1:2] = even_in[X, 0:1, :]

    inside = has_odd_pair("y", "core")

    def sides(low, high):
        for x in range(X):
            true = mirrored(x, half)
            for message, start, one in ((low, 1, 2), (high, 36, 36)):
                held = message[true]
                if message is odd_in:
                    held = jnp.where(inside, held, 0.0)
                field[x, start : start + 3, :] = held[0:3]
                first, second = unpack(held[3:4])
                kinds[x, one : one + 1, :] = first
                kinds[x, one + 1 : one + 2, :] = second

    @pl.when(core == 0)
    def _():
        sides(odd_in, even_in)

    @pl.when(core == 1)
    def _():
        sides(even_in, odd_in)

    for out, row, step in ((odd, 0, 1), (even, X - 1, -1)):
        for n in range(2):
            def put(o, part, value, n=n):
                weights[n, o, part, :] = value

            weigh(kinds[row + n * step], tables, put)
        for n in range(3):
            for c, value in enumerate(lean(field[row + n * step])):
                moved[c, n] = value
        second = operate(
            lambda o: weights[1, o],
            lambda a, c: moved[c, a if step == 1 else 2 - a],
            jnp.minimum(kinds[row + step], 1.0),
        )
        for c, value in enumerate(lean(second)):
            moved[c, 3] = value
        kind = kinds[row]
        inside = jnp.minimum(kind, 1.0)
        known = operate(
            lambda o: weights[0, o],
            lambda a, c: moved[c, (a - 1) * step],
            inside,
            (1, 2) if step == 1 else (0, 1),
        )
        onward = operate(
            lambda o: weights[0, o], lambda a, c: moved[c, 3], inside, (2,) if step == 1 else (0,)
        )
        out[0:38, :] = field[row][1:39]
        out[38:74, :] = known[2:38]
        out[74:108, :] = (2.0 * onward - field[row])[3:37]
        out[108:126, :] = pack(kind[2:20], kind[20:38])
        out[126:128, :] = lists[0:2]


def mirrored(x, half):
    return x + half * (X - 1 - 2 * x)


def rows_by_column(block_rows):
    return [block_rows[pl.ds(c, 8, stride=8), :] for c in range(8)]


def split(value):
    high = value.astype(jnp.bfloat16)
    low = (value - high.astype(F32)).astype(jnp.bfloat16)
    return high, low


def weigh(kinds, table, put):
    for b in range(3):
        moved = kinds if b == 1 else pltpu.roll(kinds, (b - 1) % YP, axis=0)
        index = jnp.maximum(moved.astype(jnp.int32) - 1, 0)
        for g in range(YP // 8):
            part = index[8 * g : 8 * g + 8]
            for a in range(3):
                for c in range(3):
                    o = 9 * a + 3 * b + c
                    put(
                        o,
                        pl.ds(8 * g, 8),
                        jnp.take_along_axis(table[o], part, axis=0, mode="promise_in_bounds"),
                    )


def spread_table(table, half, out):
    held = table[...]
    columns = [jnp.broadcast_to(held[:, o : o + 1], (8, W)) for o in range(27)]
    for o in range(27):
        out[o] = jnp.where(half == 0, columns[o], columns[o + 9 * (2 - 2 * (o // 9))])


def lean(row):
    lanes = lax.broadcasted_iota(jnp.int32, (YP, W), 1) % Z
    below = jnp.where(lanes > 0, pltpu.roll(row, 1, axis=1), 0.0)
    above = jnp.where(lanes < Z - 1, pltpu.roll(row, W - 1, axis=1), 0.0)
    return below, row, above


def operate(weight, moved, inside, rows=(0, 1, 2)):
    sums = []
    for b in range(3):
        total = None
        for a in rows:
            for c in range(3):
                term = weight(9 * a + 3 * b + c) * moved(a, c)
                total = term if total is None else total + term
        sums.append(total)
    result = pltpu.roll(sums[0], 1, axis=0) + sums[1] + pltpu.roll(sums[2], YP - 1, axis=0)
    return result * inside


def interior_kernel(
    field, kinds, tables, matrix, drill, gain, node_block, count, owner,
    weights, first, second, third, smooth, held_matrix, turned, held_rows, other, live, blocks,
    scalars, sems,
):
    copies = [
        pltpu.make_async_copy(matrix, held_matrix, sems.at[0]),
        pltpu.make_async_copy(drill, held_rows.at[0], sems.at[1]),
        pltpu.make_async_copy(gain, held_rows.at[1], sems.at[2]),
        pltpu.make_async_copy(node_block, scalars.at[0], sems.at[3]),
        pltpu.make_async_copy(count, scalars.at[1], sems.at[4]),
        pltpu.make_async_copy(owner, scalars.at[2], sems.at[5]),
    ]
    for copy in copies:
        copy.start()
    plane = whereabouts()[2]
    for x in range(X):
        def put(o, rows, value, x=x):
            weights[o, x, rows, :] = value

        weigh(kinds[x], tables, put)
        for c, value in enumerate(lean(field[x])):
            first[c, x] = value

    def step(source, start, x):
        return operate(
            lambda o: weights[o, x],
            lambda a, c: source[c, x + a - 1 - start],
            jnp.minimum(kinds[x], 1.0),
        )

    for x in range(1, 7):
        for c, value in enumerate(lean(step(first, 0, x))):
            second[c, x - 1] = value
    for x in range(2, 6):
        value = 2.0 * step(second, 1, x) - first[1, x]
        for c, value in enumerate(lean(value)):
            third[c, x - 2] = value
    for x in range(3, 5):
        fourth = 2.0 * step(third, 2, x) - second[1, x - 1]
        result = (
            CHEB[0] * first[1, x] + CHEB[1] * second[1, x - 1] + CHEB[2] * third[1, x - 2] + CHEB[3] * fourth
        )
        for g in range(4):
            smooth[4 * (x - 3) + g] = result[OFF + 8 * g : OFF + 8 * g + 8]
    for copy in copies:
        copy.wait()
    for b in range(BLOCKS):
        turned[b] = held_matrix[b].T
    other[...] = jnp.zeros((8, SAMPLES), F32)
    for k in range(2):
        for h in range(2):
            for kind in range(2):
                row = 4 * kind + 2 * k + h
                other[row : row + 1, 0:W] = held_rows[kind, k : k + 1, h * W : h * W + W]
    lane = lax.broadcasted_iota(jnp.int32, (8, W), 1)
    names = jnp.zeros((8, W), F32)
    places = jnp.zeros((8, W), jnp.int32)
    limit = jnp.zeros((BLOCKS, SAMPLES), jnp.int32)
    block = lax.broadcasted_iota(jnp.int32, (BLOCKS, SAMPLES), 0)
    for b in range(BLOCKS):
        names = jnp.where(lane == 8 * plane + b, (scalars[2, b] + 1).astype(F32), names)
        places = jnp.where(lane == b, scalars[0, b], places)
        limit = jnp.where(block == b, scalars[1, b], limit)
    other[0:1, W : 2 * W] = names[0:1]
    blocks[...] = places
    sample = lax.broadcasted_iota(jnp.int32, (BLOCKS, SAMPLES), 1)
    live[...] = (sample < limit).astype(F32)


def fill_halo(message, inside, tables, halo_kinds, halo_weights, halo_first, partial):
    held = jnp.where(inside, message[...], 0.0)
    one, two, three = [jnp.zeros((n, W), F32) for n in (1, 2, 3)]
    low, high = unpack(held[108:126])
    halo_kinds[...] = jnp.concatenate([two, low, high, two], axis=0)

    def put(o, part, value):
        halo_weights[o, part, :] = value

    weigh(halo_kinds[...], tables, put)
    for c, value in enumerate(lean(jnp.concatenate([one, held[0:38], one], axis=0))):
        halo_first[c, 0] = value
    partial[0] = jnp.concatenate([two, held[38:74], two], axis=0)
    partial[1] = jnp.concatenate([three, held[74:108], three], axis=0)


def side(
    high, kinds, weights, first, second, third, halo_kinds, halo_weights, halo_first, edge_second, edge_third, partial, put
):
    def beyond(x):
        return x - X if high else -1 - x

    def weight(x):
        if 0 <= x < X:
            return (lambda o: weights[o, x]), jnp.minimum(kinds[x], 1.0)
        return (lambda o: halo_weights[o]), jnp.minimum(halo_kinds[...], 1.0)

    def at_first(x, c):
        return first[c, x] if 0 <= x < X else halo_first[c, beyond(x)]

    def at_second(x, c):
        return second[c, x - 1] if 1 <= x < 7 else edge_second[c, beyond(x) + 1]

    def at_third(x, c):
        return third[c, x - 2] if 2 <= x < 6 else edge_third[c, beyond(x) + 2]

    def step(at, x, rows=(0, 1, 2)):
        of, inside = weight(x)
        return operate(of, lambda a, c: at(x + a - 1, c), inside, rows)

    def row(n):
        return X - 1 - n if high else n

    inward, itself = ((0,), (0, 1)) if high else ((2,), (1, 2))
    for n in (-1, 0):
        if n < 0:
            value = partial[0] + step(at_first, row(n), inward)
        else:
            value = step(at_first, row(n))
        for c, value in enumerate(lean(value)):
            edge_second[c, -n] = value
    for n in (-1, 0, 1):
        if n < 0:
            value = partial[1] + 2.0 * step(at_second, row(n), itself)
        else:
            value = 2.0 * step(at_second, row(n)) - at_first(row(n), 1)
        for c, value in enumerate(lean(value)):
            edge_third[c, 1 - n] = value
    for n in (0, 1, 2):
        x = row(n)
        fourth = 2.0 * step(at_third, x) - at_second(x, 1)
        result = (
            CHEB[0] * at_first(x, 1) + CHEB[1] * at_second(x, 1) + CHEB[2] * at_third(x, 1) + CHEB[3] * fourth
        )
        for g in range(4):
            put(x, g, result[OFF + 8 * g : OFF + 8 * g + 8])


def lower_kernel(
    kinds, edges, weights, first, second, third, tables,
    lower,
    halo_kinds, halo_weights, halo_first, edge_second, edge_third, partial,
):
    fill_halo(edges, has_odd_pair("x", "zh"), tables, halo_kinds, halo_weights, halo_first, partial)

    def put(x, g, value):
        lower[4 * x + g] = value

    side(
        False, kinds, weights, first, second, third,
        halo_kinds, halo_weights, halo_first, edge_second, edge_third, partial, put,
    )


def finish_kernel(
    kinds, edges, near, weights, first, second, third, middle, lower, tables, turned, other, live, blocks,
    smooth, payload, lists,
    halo_kinds, halo_weights, halo_first, edge_second, edge_third, partial, chosen, node_block, sem,
):
    copy = pltpu.make_async_copy(blocks.at[0:1], node_block, sem)
    copy.start()
    half = whereabouts()[0]
    lists[0:4] = near[0:4]
    lists[4:8] = jnp.zeros((4, W), F32)
    lists[2:4] = edges[126:128]
    fill_halo(edges, True, tables, halo_kinds, halo_weights, halo_first, partial)

    def put(x, g, value):
        smooth[4 * mirrored(x, half) + g] = value

    side(
        True, kinds, weights, first, second, third,
        halo_kinds, halo_weights, halo_first, edge_second, edge_third, partial, put,
    )
    for g in range(4):
        for x in (0, 1, 2):
            put(x, g, lower[4 * x + g])
        for x in (3, 4):
            put(x, g, middle[4 * (x - 3) + g])

    copy.wait()
    for b in range(BLOCKS):
        chosen[pl.ds(8 * b, 8), :] = smooth[node_block[0, b]]
    columns = rows_by_column(chosen)
    low = half_lanes((8, W))
    parts = ([], [])
    for j in range(4):
        one, two = columns[2 * j], columns[2 * j + 1]
        parts[0].append(jnp.where(low, one, swap_halves(two)))
        parts[1].append(jnp.where(low, swap_halves(one), two))
    values = [jnp.concatenate(p, axis=1) for p in parts]
    pieces = [split(v) for v in values]
    left = jnp.concatenate([pieces[0][0], pieces[1][0], pieces[0][1], pieces[1][1]], axis=0)
    block = lax.broadcasted_iota(jnp.int32, (BLOCKS, SAMPLES), 0)
    sums = [jnp.zeros((BLOCKS, SAMPLES), F32) for _ in range(2)]
    for b in range(BLOCKS):
        product = jnp.dot(left, turned[b], preferred_element_type=F32)
        for r in range(2):
            both = product[8 * r : 8 * r + 8] + product[16 + 8 * r : 24 + 8 * r]
            sums[r] = jnp.where(block == b, both, sums[r])
    tiles = []
    for r in range(2):
        told = jnp.where(live[...] > 0.0, sums[r], 0.0)
        tiles += [told[:, 0:W], told[:, W : 2 * W]]
    tiles.append(other[:, 0:W])
    for peer in range(16):
        for n, tile in enumerate(tiles):
            payload[peer, 2 * n] = tile[0:4]
            payload[peer, 2 * n + 1] = tile[4:8]
        payload[peer, 10] = other[0:4, W : 2 * W]


def collect_kernel(lists, here, keep, send):
    names = here[0, 10]
    for n in range(1, 16):
        names = names + here[n, 10]
    names = jnp.broadcast_to(names[0:1], (8, W))
    lane = lax.broadcasted_iota(jnp.int32, (8, W), 1)
    row = lax.broadcasted_iota(jnp.int32, (8, W), 0)
    hits, spots = [], []
    half, core, _, me = whereabouts()
    for member in range(4):
        tile = me ^ (1 if member & 1 else 0) ^ (8 if member & 2 else 0)
        held = jnp.broadcast_to(lists[member : member + 1], (8, W))
        name = jnp.sum(jnp.where(lane == row, held, 0.0), axis=1, keepdims=True)
        name = jnp.broadcast_to(name, (8, W))
        hits.append(name == names)
        hits.append((2 * tile + 1 + (row & 1)).astype(F32) == names)
        block = name.astype(jnp.int32) - 1
        holder = block >> 1
        spot = ((holder >> 4) * 4 + ((holder >> 1) & 3)) * 8 + 2 * (block & 1)
        mine = ((holder & 1) == core) & (((holder >> 3) & 1) == half)
        spots.append(jnp.where(mine, spot, -1024))
    hit = jnp.concatenate([h.astype(F32) for h in hits], axis=0).astype(jnp.bfloat16)
    spots = jnp.concatenate(spots, axis=0)
    lane = lax.broadcasted_iota(jnp.int32, (32, W), 1)
    choose = jnp.concatenate(
        [(lane == spots + 4 * kind + h).astype(F32) for kind in range(2) for h in range(2)], axis=0
    ).astype(jnp.bfloat16)

    def column(tile):
        return jnp.concatenate([here[n, 2 * tile + k] for n in range(16) for k in range(2)], axis=0)

    def gather(left, data):
        high, low = split(data)
        return jnp.dot(left, high, preferred_element_type=F32) + jnp.dot(
            left, low, preferred_element_type=F32
        )

    totals = [
        gather(hit, jnp.concatenate([column(2 * r), column(2 * r + 1)], axis=1)) for r in range(2)
    ]
    found = gather(choose, column(4))
    row = lax.broadcasted_iota(jnp.int32, (8, W), 0)
    for member in range(4):
        out = (send if member & 1 else keep).at[member // 2]
        own = []
        for h in range(2):
            lanes = slice(h * W, h * W + W)
            drill, gain = [
                found[64 * kind + 32 * h + 8 * member : 64 * kind + 32 * h + 8 * member + 8]
                for kind in range(2)
            ]
            for r in range(2):
                out[16 * r + 8 * h : 16 * r + 8 * h + 8, :] = drill - totals[r][16 * member : 16 * member + 8, lanes]
                own.append(totals[r][16 * member + 8 : 16 * member + 16, lanes])
            out[32 + 8 * h : 40 + 8 * h, :] = gain
        out[48:56, :] = jnp.where(
            row < 4, jnp.where(row < 2, own[0], own[1]), jnp.where(row < 6, own[2], own[3])
        )


def update_kernel(
    keep, near, far, smooth, matrix, rows, live, blocks,
    out, misfit,
    update, node_block, sem,
):
    copy = pltpu.make_async_copy(blocks.at[0:1], node_block, sem)
    copy.start()
    sums = keep[0] + near[0] + far[...]
    for k in range(2):
        for r in range(2):
            for h in range(2):
                t = 48 + 4 * h + 2 * r + k
                lanes = slice(h * W, h * W + W)
                misfit[k, r : r + 1, lanes] = rows[0, k : k + 1, lanes] - sums[t : t + 1, :]
    gain = jnp.concatenate([sums[32:40], sums[40:48]], axis=1)
    picked = [
        jnp.where(
            live[...] > 0.0,
            gain * jnp.concatenate([sums[16 * r : 16 * r + 8], sums[16 * r + 8 : 16 * r + 16]], axis=1),
            0.0,
        )
        for r in range(2)
    ]
    pieces = [split(v) for v in picked]
    left = jnp.concatenate([pieces[0][0], pieces[1][0], pieces[0][1], pieces[1][1]], axis=0)
    block = lax.broadcasted_iota(jnp.int32, (BLOCKS, NODES), 0)
    sums = [jnp.zeros((BLOCKS, NODES), F32) for _ in range(2)]
    for b in range(BLOCKS):
        product = jnp.dot(left, matrix[b], preferred_element_type=F32)
        for r in range(2):
            both = product[8 * r : 8 * r + 8] + product[16 + 8 * r : 24 + 8 * r]
            sums[r] = jnp.where(block == b, both, sums[r])
    low = half_lanes((8, W))
    for j in range(4):
        one, two = sums[0][:, j * W : j * W + W], sums[1][:, j * W : j * W + W]
        update[pl.ds(2 * j, 8, stride=8), :] = jnp.where(low, one, swap_halves(two))
        update[pl.ds(2 * j + 1, 8, stride=8), :] = jnp.where(low, swap_halves(one), two)
    out[...] = smooth[...]
    copy.wait()
    for b in range(BLOCKS):
        n = node_block[0, b]
        out[n] = out[n] + update[8 * b : 8 * b + 8, :]


def shape(*dims, dtype=F32):
    return jax.ShapeDtypeStruct(dims, dtype)


def call(kernel, outs, ins, name, scratch=()):
    return pl.pallas_call(
        kernel,
        out_shape=outs,
        in_specs=ins,
        out_specs=(VMEM,) * len(outs),
        scratch_shapes=scratch,
        compiler_params=pltpu.CompilerParams(vmem_limit_bytes=24 * 1024 * 1024),
        name=name,
    )


def shards(
    noise, classes, table, obs_matrix, node_block, sample_block, sample_count, drill_data, obs_gain
):
    noise, classes, table, matrix, blocks, owner, count, drill, gain = [
        pltpu.with_memory_space_constraint(a, pltpu.HBM)
        for a in (
            noise, classes, table, obs_matrix, node_block, sample_block, sample_count, drill_data, obs_gain
        )
    ]
    odd, even, names = call(
        edge_y_kernel,
        (shape(X + 1, 4, W), shape(X + 1, 4, W), shape(8, W)),
        [HBM] * 3,
        "edge_y",
        [
            pltpu.VMEM((2, X, 8, W), F32),
            pltpu.VMEM((2, X, 8, Z), jnp.int32),
            pltpu.SMEM((BLOCKS,), jnp.int32),
            pltpu.SemaphoreType.DMA((5,)),
        ],
    )(noise, classes, owner)
    odd = permute(odd, ("x", "y", "core"), odd_along_y)
    even = permute(even, ("y", "core"), even_pair)
    field, kinds, tables = call(
        prepare_kernel,
        (shape(X, YP, W), shape(X, YP, W), shape(27, 8, W)),
        [HBM] * 3,
        "prepare",
        [
            pltpu.VMEM((X, Y, W), F32),
            pltpu.VMEM((X, Y, Z), jnp.int32),
            pltpu.VMEM((8, 27), F32),
            pltpu.SemaphoreType.DMA((3,)),
        ],
    )(noise, classes, table)
    field, kinds, odd, even, lists = call(
        edge_x_kernel,
        (shape(X, YP, W), shape(X, YP, W), shape(MESSAGE, W), shape(MESSAGE, W), shape(4, W)),
        [VMEM] * 6,
        "edge_x",
        [pltpu.VMEM((2, 27, YP, W), F32), pltpu.VMEM((3, 4, YP, W), F32)],
    )(odd, even, field, kinds, names, tables)
    odd = permute(odd, ("x", "zh", "core"), odd_along_x)
    even = permute(even, ("x", "zh"), even_pair)
    weights, first, second, third, middle, matrix, turned, rows, other, live, blocks = call(
        interior_kernel,
        (
            shape(27, X, YP, W),
            shape(3, X, YP, W),
            shape(3, 6, YP, W),
            shape(3, 4, YP, W),
            shape(8, 8, W),
            shape(BLOCKS, SAMPLES, NODES, dtype=jnp.bfloat16),
            shape(BLOCKS, NODES, SAMPLES, dtype=jnp.bfloat16),
            shape(2, 2, SAMPLES),
            shape(8, SAMPLES),
            shape(BLOCKS, SAMPLES),
            shape(8, W, dtype=jnp.int32),
        ),
        [VMEM] * 3 + [HBM] * 6,
        "interior",
        [pltpu.SMEM((3, BLOCKS), jnp.int32), pltpu.SemaphoreType.DMA((6,))],
    )(field, kinds, tables, matrix, drill, gain, blocks, count, owner)
    halo_scratch = [
        pltpu.VMEM((YP, W), F32),
        pltpu.VMEM((27, YP, W), F32),
        pltpu.VMEM((3, 1, YP, W), F32),
        pltpu.VMEM((3, 2, YP, W), F32),
        pltpu.VMEM((3, 3, YP, W), F32),
        pltpu.VMEM((2, YP, W), F32),
    ]
    (lower,) = call(lower_kernel, (shape(12, 8, W),), [VMEM] * 7, "lower", halo_scratch)(
        kinds, odd, weights, first, second, third, tables
    )
    index_scratch = [pltpu.SMEM((1, W), jnp.int32), pltpu.SemaphoreType.DMA]
    smooth, payload, lists = call(
        finish_kernel,
        (shape(32, 8, W), shape(16, GROUPS, 4, W), shape(8, W)),
        [VMEM] * 14,
        "finish",
        halo_scratch + [pltpu.VMEM((64, W), F32)] + index_scratch,
    )(
        kinds, even, lists, weights, first, second, third, middle, lower, tables, turned,
        other, live, blocks,
    )
    here = lax.all_to_all(payload, ("x", "y"), 0, 0, tiled=True)
    keep, send = call(
        collect_kernel, (shape(2, 56, W), shape(2, 56, W)), [VMEM] * 2, "collect"
    )(lists, here)
    near = permute(send, ("core",), lambda c: (c ^ 1,))
    far = permute(keep[1] + near[1], ("zh",), lambda z: (z ^ 1,))
    out, misfit = call(
        update_kernel,
        (shape(32, 8, W), shape(2, 2, SAMPLES)),
        [VMEM] * 8,
        "update",
        [pltpu.VMEM((64, W), F32)] + index_scratch,
    )(keep, near, far, smooth, matrix, rows, live, blocks)
    return out.reshape(X, Y, W), misfit


def solution(mesh):
    fine = Mesh(
        mesh.devices.reshape(4, 4, 2, 4, 2), ("real", "x", "zh", "y", "core")
    )
    sx, sy = ("x", "zh"), ("y", "core")
    both = sx + sy
    in_specs = (
        P(sx, sy, "real"),
        P(sx, sy, None),
        P(),
        P(both, None, None),
        P(both),
        P(both),
        P(both),
        P(both, None),
        P(both, None),
    )
    out_specs = (P(sx, sy, "real"), P(both, "real", None))
    return jax.shard_map(shards, mesh=fine, in_specs=in_specs, out_specs=out_specs, check_vma=False)
```
